32 devices in a mesh: section: 2 (over x), dp: 4 (over y, core), tensor: 4 (over z).
Axes of the slice: x: 2, y: 2, z: 4, core: 2. Of those that a mesh axis runs over, the one named last changes fastest.
Arguments:
- block_input: bfloat16 [8, 1024, 768], P('dp', 'tensor'), may hold values from -6 to 6
- cotangent: bfloat16 [8, 1024, 768], P('dp', 'tensor'), may hold values from -6 to 6
- query_key_value_weights: bfloat16 [2, 3, 768, 768], P('section', None, 'dp', 'tensor'), may hold values from -0.21875 to 0.21875
- attention_output_weights: bfloat16 [2, 768, 768], P('section', 'tensor', 'dp'), may hold values from -1.75 to 1.75
- bias_table: bfloat16 [2, 32, 12], P('section'), may hold values from -6 to 6
- norm_first: bfloat16 [2, 768], P('section'), may hold values from 0.5 to 1.5
- norm_second: bfloat16 [2, 768], P('section'), may hold values from 0.5 to 1.5
- router_projection_weights: bfloat16 [2, 768, 4], P('section'), may hold values from -0.15625 to 0.15625
- expert_up: bfloat16 [2, 4, 768, 3072], P('section', 'dp', None, 'tensor'), may hold values from -0.21875 to 0.21875
- expert_down: bfloat16 [2, 4, 3072, 768], P('section', 'dp', 'tensor'), may hold values from -0.4375 to 0.4375
- routes: int32 [2, 8, 1024, 1], P('section', 'dp'), may hold values from 0 to 3; in each aligned block of 1024 rows (0 to 1023, 1024 to 2047, ..., all dimensions but the last counted through in order) at most 320 rows name the same one
- prefix_lengths: int32 [8], P('dp'), may hold values from 1 to 1024
- relative_buckets: int32 [2047], replicated, may hold values from 0 to 31
Outputs:
- layer_outputs: bfloat16 [2, 8, 1024, 768], P('section', 'dp', 'tensor')
- input_grads: bfloat16 [2, 8, 1024, 768], P('section', 'dp', 'tensor')
- input_weights_grad: float32 [2, 3, 768, 768], P('section', None, 'dp', 'tensor')
- output_weights_grad: float32 [2, 768, 768], P('section', 'tensor', 'dp')
- bias_table_grad: float32 [2, 32, 12], P('section')
- norm_first_grad: float32 [2, 768], P('section')
- norm_second_grad: float32 [2, 768], P('section')
- router_weights_grad: float32 [2, 768, 4], P('section')
- expert_up_grad: float32 [2, 4, 768, 3072], P('section', 'dp', None, 'tensor')
- expert_down_grad: float32 [2, 4, 3072, 768], P('section', 'dp', 'tensor')
The draws below stay inside these ranges and needn't reach their ends.
Inputs may be any that keep to these rules, and one draw needn't show every extreme that they name: `routes`: in every aligned block of 1024 rows (one micro-batch of one index of dp) no expert is named by more than 320 rows, and in some block one expert is named by exactly 320 rows.
All inputs are finite; a program needn't handle non-finite values.
Results may differ from the reference program's by a relative error of at most 0.034.
Values may be sent and summed in bfloat16 or wider, within the bound.
No kernel may reach another device: no remote copies, remote signals or barrier semaphores. Data moves between devices by JAX's collectives and lax.ppermute only.
A program may use at most 256 MiB of HBM per device.

```python
import math
import jax
import jax.numpy as jnp
import numpy as np
from jax import lax

D = 768
HEADS = 12
HEAD_DIM = 64
FF = 3072
BUCKETS = 32
SEQ_LEN = 1024
SEQ_MB = 1
EXPERTS = 4
CAP = 320
SEQS = 8


def place_ends(drawn, key, low, largest):
    shape = drawn.shape
    index_at = [jax.random.randint(jax.random.fold_in(key, axis), (), 0, shape[axis]) for axis in range(len(shape))]
    drawn = drawn.at[tuple(index_at)].set(low)
    longest = shape.index(max(shape))
    index_at[longest] = (index_at[longest] + 1) % shape[longest]
    return drawn.at[tuple(index_at)].set(largest)


def steps_of(rng, dims, pieces, smallest, largest):
    def one(axis_at, blocks):
        heights = jax.random.uniform(jax.random.fold_in(jax.random.fold_in(rng, 6), axis_at), (blocks,), jnp.float32, smallest / len(pieces), largest / len(pieces))
        return jnp.repeat(jnp.exp(heights), dims[axis_at] // blocks).reshape((-1,) + (1,) * (len(dims) - axis_at - 1))

    factor_of = one(*pieces[0])
    for cut in pieces[1:]:
        factor_of = factor_of * one(*cut)
    return factor_of


def assign_block(own_key, own, number, rows, amount, top, most, skew):
    ranking = jax.random.permutation(own_key, amount)
    heavy_load, usual = portions_of(amount, rows * top, most, skew, True), portions_of(amount, rows * top, most, skew, False)
    places = jnp.arange(amount)

    def named(lengths, offset_by):
        used = int((lengths > 0).sum())
        fixed = max(1, used // 4)
        moved = fixed + (places - fixed + offset_by * (used - fixed)) % max(1, amount - fixed)
        return jnp.zeros((amount,), jnp.int32).at[ranking[jnp.where(places < fixed, places, moved)]].set(jnp.asarray(lengths, jnp.int32))

    lengths = jnp.where(number % 4 == 0, named(heavy_load, number // 4), named(usual, number - number // 4 - 1))
    mixed = jax.random.permutation(jax.random.fold_in(own, 3), amount)
    donor, receiver = mixed[0:amount // 2 * 2:2], mixed[1:amount // 2 * 2:2]
    room = jnp.minimum(lengths[donor] - 1, most - lengths[receiver]) // 2
    room = jnp.where((donor == ranking[0]) | (receiver == ranking[0]) | (lengths[receiver] == 0), 0, jnp.maximum(room, 0))
    moved = jax.random.randint(jax.random.fold_in(own, 4), (amount // 2,), 0, 1 << 20) % (room + 1)
    lengths = lengths.at[donor].add(-moved).at[receiver].add(moved)
    items = jnp.searchsorted(jnp.cumsum(lengths), jnp.arange(rows * top), side="right").astype(jnp.int32)
    grid = items.reshape(top, rows).T
    grid = grid[jax.random.permutation(jax.random.fold_in(own, 1), rows)]
    offset_by = jax.random.randint(jax.random.fold_in(own, 2), (rows, 1), 0, top)
    return jnp.take_along_axis(grid, (jnp.arange(top)[None, :] + offset_by) % top, axis=1)


def portions_of(count, total, most, slope, full):
    weights = [(1 << 20) // math.isqrt(rank ** slope) + 1 for rank in range(1, count + 1)]
    largest = most if full else min(most, max(-(-total // count), total * weights[0] // sum(weights)))
    least = 1 if total - largest >= count - 1 else 0
    counts, spare = [largest] + [least] * (count - 1), total - largest - least * (count - 1)
    while spare > 0:
        candidates = [i for i in range(1, count) if counts[i] < largest] or [i for i in range(1, count) if counts[i] < most]
        pool, remaining = sum([weights[i] for i in candidates]), spare
        for i in candidates:
            more = min(most - counts[i], max(1, remaining * weights[i] // pool), spare)
            counts[i] = counts[i] + more
            spare = spare - more
    return np.array(counts)


def scatter_about(key, extent, spread, bound, cuts=(), kind=jnp.bfloat16):
    level = steps_of(key, extent, cuts, -0.22, 0.18) if cuts else 1.0
    drawn = jax.random.normal(key, extent, jnp.float32) * spread * level
    return jnp.minimum(jnp.maximum(drawn, -bound), bound).astype(kind)


def setup_inputs(seed: int = 0) -> dict:
    streams_of = jax.random.split(jax.random.key(seed), 14)
    block_input = scatter_about(streams_of[0], (SEQS, SEQ_LEN, D), 1.0, 6.0, ((0, 4), (1, 4)))
    cotangent = scatter_about(streams_of[1], (SEQS, SEQ_LEN, D), 1.0, 6.0, ((0, 4), (1, 4)))
    query_key_value_weights = scatter_about(streams_of[2], (2, 3, D, HEADS * HEAD_DIM), D ** -0.5, 0.21875, ((0, 2), (2, 4), (3, 4)))
    attention_output_weights = scatter_about(streams_of[3], (2, HEADS * HEAD_DIM, D), (D * 16 // SEQ_LEN) ** -0.5, 1.75, ((0, 2), (1, 4), (2, 4)))
    bias_table = scatter_about(streams_of[4], (2, BUCKETS, HEADS), 1.0, 6.0, ((0, 2),))
    norm_first = jnp.clip(1.0 + 0.1 * jax.random.normal(streams_of[5], (2, D), jnp.float32), 0.5, 1.5).astype(jnp.bfloat16)
    norm_second = jnp.clip(1.0 + 0.1 * jax.random.normal(streams_of[6], (2, D), jnp.float32), 0.5, 1.5).astype(jnp.bfloat16)
    router_projection_weights = scatter_about(streams_of[7], (2, D, EXPERTS), (2 * D) ** -0.5, 0.15625, ((0, 2),))
    expert_up = scatter_about(streams_of[8], (2, EXPERTS, D, FF), D ** -0.5, 0.21875, ((0, 2), (1, 4), (3, 4)))
    expert_down = scatter_about(streams_of[9], (2, EXPERTS, FF, D), (max(FF // (EXPERTS * EXPERTS), 1)) ** -0.5, 0.4375, ((0, 2), (1, 4), (2, 4)))
    routes_keys = jax.random.split(jax.random.fold_in(streams_of[10], 1), 2 * SEQS * SEQ_LEN // (SEQ_MB * SEQ_LEN))
    routes_turns = jax.random.permutation(jax.random.fold_in(streams_of[10], 3), 2 * SEQS * SEQ_LEN // (SEQ_MB * SEQ_LEN))
    routes = jax.vmap(lambda own, number: assign_block(jax.random.fold_in(streams_of[10], 2), own, number, SEQ_MB * SEQ_LEN, EXPERTS, 1, CAP, 1))(routes_keys, routes_turns).reshape((2, SEQS, SEQ_LEN, 1))
    prefix_lengths = place_ends(jax.random.randint(streams_of[11], (SEQS,), 1, SEQ_LEN + 1), jax.random.fold_in(streams_of[11], 1), 1, SEQ_LEN).astype(jnp.int32)
    relative_buckets = place_ends(jax.random.randint(streams_of[12], (2 * SEQ_LEN - 1,), 0, BUCKETS), jax.random.fold_in(streams_of[12], 1), 0, BUCKETS - 1).astype(jnp.int32)
    return dict(block_input=block_input, cotangent=cotangent, query_key_value_weights=query_key_value_weights, attention_output_weights=attention_output_weights, bias_table=bias_table, norm_first=norm_first, norm_second=norm_second, router_projection_weights=router_projection_weights, expert_up=expert_up, expert_down=expert_down, routes=routes, prefix_lengths=prefix_lengths, relative_buckets=relative_buckets)


EPSILON = 1e-06
MASKED = -1000000000.0
MATMUL_PRECISION = lax.Precision.HIGHEST

@jax.custom_vjp
def low(v):
    return lax.optimization_barrier(v.astype(jnp.bfloat16)).astype(jnp.float32)

@jax.custom_vjp
def low_back(v):
    return v

def low_keep(v):
    return (low(v), None)

def low_pass(kept, grad):
    return (grad,)

def back_keep(v):
    return (v, None)

def back_low(kept, grad):
    return (low(grad),)
low.defvjp(low_keep, low_pass)
low_back.defvjp(back_keep, back_low)

def attend_sequence(queries, key_rows, value_rows, prefix_one, rel_bias):
    seq_len, head_count, head_dim = queries.shape
    block_rows = min(512, seq_len)
    key_pos = jnp.arange(seq_len).astype(jnp.int32)

    def one_block(row_start):
        query_rows = lax.dynamic_slice_in_dim(queries, row_start, block_rows, 0)
        row_pos = row_start + jnp.arange(block_rows).astype(jnp.int32)
        scores = jnp.einsum('bhd,lhd->hbl', query_rows, key_rows, precision=MATMUL_PRECISION) * head_dim ** (-0.5)
        offsets = (key_pos[None, :] - row_pos[:, None] + seq_len - 1).astype(jnp.int32)
        scores = scores + jnp.transpose(jnp.take(rel_bias, offsets, axis=0), (2, 0, 1))
        allowed = (key_pos[None, :] <= row_pos[:, None]) | (key_pos[None, :] < prefix_one)
        scores = low_back(jnp.where(allowed[None], scores, MASKED))
        top_score = lax.optimization_barrier(jnp.max(scores, -1, keepdims=True))
        weights = jnp.exp(scores - top_score)
        weights_low = low(weights / lax.optimization_barrier(jnp.sum(weights, -1, keepdims=True)))
        return low(jnp.einsum('hbl,lhd->bhd', weights_low, value_rows, precision=MATMUL_PRECISION))
    starts = (jnp.arange(seq_len // block_rows) * block_rows).astype(jnp.int32)
    outputs = lax.map(jax.checkpoint(one_block), starts)
    return outputs.reshape(seq_len, head_count, head_dim)

def layer(inputs, gain_one, query_key_value_weights, attention_output_weights, bias_table, gain_two, router_projection_weights, expert_up, expert_down, section_routes, prefix_lengths, relative_buckets):
    sequences, seq_len, model_width = inputs.shape
    buckets, head_count = bias_table.shape
    head_dim = query_key_value_weights.shape[2] // head_count
    experts_all = router_projection_weights.shape[1]
    first_norm_output = low(inputs * lax.rsqrt(lax.optimization_barrier(jnp.mean(inputs * inputs, -1, keepdims=True)) + EPSILON) * gain_one)
    projected_rows = low_back(low(jnp.einsum('trx,vxj->vtrj', first_norm_output, query_key_value_weights, precision=MATMUL_PRECISION)))
    shaped = projected_rows.reshape(3, sequences, seq_len, head_count, head_dim)
    bucket_onehot = (relative_buckets[:, None] == jnp.arange(buckets).astype(jnp.int32)[None, :]).astype(inputs.dtype)
    rel_bias = jnp.dot(bucket_onehot, bias_table, precision=MATMUL_PRECISION)
    attended = lax.map(lambda element: attend_sequence(element[0], element[1], element[2], element[3], rel_bias), (shaped[0], shaped[1], shaped[2], prefix_lengths))
    merged_heads = low_back(attended.reshape(sequences, seq_len, head_count * head_dim))
    residual_branch = low_back(jnp.einsum('ubz,zv->ubv', merged_heads, attention_output_weights, precision=MATMUL_PRECISION))
    middle = inputs + residual_branch
    second_norm_output = low(middle * lax.rsqrt(lax.optimization_barrier(jnp.mean(middle * middle, -1, keepdims=True)) + EPSILON) * gain_two)
    router_scores = low_back(jnp.einsum('kiu,uo->kio', second_norm_output, router_projection_weights, precision=MATMUL_PRECISION))
    router_probs = jax.nn.softmax(router_scores, -1)
    expert_ids = jnp.arange(experts_all).astype(jnp.int32)
    chosen = (section_routes[..., None] == expert_ids).astype(inputs.dtype)
    gates = lax.optimization_barrier(jnp.sum(router_probs * chosen, -1, keepdims=True))
    groups = sequences // SEQ_MB
    flat_routes = section_routes.reshape(groups, SEQ_MB * seq_len)
    onehot = (flat_routes[..., None] == expert_ids).astype(jnp.int32)
    slot_index = lax.optimization_barrier(jnp.sum((jnp.cumsum(onehot, 1).astype(jnp.int32) - 1) * onehot, -1)).astype(jnp.int32)
    group_ids = jnp.arange(groups).astype(jnp.int32)[:, None]
    target = ((flat_routes * groups + group_ids) * CAP + slot_index).astype(jnp.int32).reshape(-1)
    buffers = jnp.zeros((experts_all * groups * CAP, model_width), inputs.dtype).at[target].set(second_norm_output.reshape(-1, model_width))
    hidden = low_back(jnp.einsum('ecd,edf->ecf', buffers.reshape(experts_all, groups * CAP, model_width), expert_up, precision=MATMUL_PRECISION))
    activated = low(jax.nn.gelu(hidden))
    produced = jnp.einsum('ecf,efd->ecd', activated, expert_down, precision=MATMUL_PRECISION).reshape(-1, model_width)
    expert_out = low_back(jnp.take(produced, target, axis=0).reshape(sequences, seq_len, model_width))
    return middle + gates * expert_out

def reference(block_input, cotangent, query_key_value_weights, attention_output_weights, bias_table, norm_first, norm_second, router_projection_weights, expert_up, expert_down, routes, prefix_lengths, relative_buckets):

    def weights_of(section_id):
        return tuple((member[section_id].astype(jnp.float32) for member in (norm_first, query_key_value_weights, attention_output_weights, bias_table, norm_second, router_projection_weights, expert_up, expert_down)))

    def section_zero(hidden_in, *weights):
        result = layer(hidden_in, *weights, routes[0, :, :, 0], prefix_lengths, relative_buckets)
        return low(low_back(result))

    def section_one(hidden_in, *weights):
        return layer(hidden_in, *weights, routes[1, :, :, 0], prefix_lengths, relative_buckets)
    first_out, back_zero = jax.vjp(section_zero, block_input.astype(jnp.float32), *weights_of(0))
    second_out, back_one = jax.vjp(section_one, first_out, *weights_of(1))
    grads_one = back_one(cotangent.astype(jnp.float32))
    grads_zero = back_zero(grads_one[0])
    layer_outputs = jnp.stack([first_out, second_out]).astype(jnp.bfloat16)
    input_grads = jnp.stack([grads_zero[0], grads_one[0]]).astype(jnp.bfloat16)
    stacked = [jnp.stack([grads_zero[number + 1], grads_one[number + 1]]).astype(jnp.float32) for number in range(8)]
    return (layer_outputs, input_grads, stacked[1], stacked[2], stacked[3], stacked[0], stacked[4], stacked[5], stacked[6], stacked[7])
```

```python
import functools

import jax
import jax.numpy as jnp
from jax import lax
from jax.experimental import pallas as pl
from jax.experimental.pallas import tpu as pltpu
from jax.sharding import PartitionSpec as P

HEAD_DIM = 64
EPSILON = 1e-06
MASKED = -1000000000.0
AXES = ("section", "dp", "tensor")
BLOCK = 128
DIRECT = 8
BF16 = jnp.bfloat16
F32 = jnp.float32


def send(value, to):
    sections, width, depth = (lax.axis_size(name) for name in AXES)

    def number(x, h, c, t):
        return (x * width + 2 * h + c) * depth + t

    pairs = []
    for x in range(sections):
        for d in range(width):
            for t in range(depth):
                target = to(x, d // 2, d % 2, t)
                if target is not None:
                    pairs.append((number(x, d // 2, d % 2, t), number(*target)))
    return lax.ppermute(value, AXES, pairs)


def core_swap(value):
    return send(value, lambda x, h, c, t: (x, h, 1 - c, t))


def section_swap(value):
    return send(value, lambda x, h, c, t: (1 - x, h, c, t))


def tensor_swap(value, j):
    return send(value, lambda x, h, c, t: (x, h, c, t ^ j))


def host_swap(value, j):
    return send(value, lambda x, h, c, t: (x, h ^ j, c, t))


def expert_swap(value, j):
    def to(x, h, c, t):
        e = (2 * h + (t & 1)) ^ j
        return (x, e >> 1, c, (t & 2) | (e & 1))

    return send(value, to)


def expert_exchange(values):
    count, bit = values.shape[0], 1
    while bit < count:
        parts = values.reshape(count // (2 * bit), 2, bit, *values.shape[1:])
        other = expert_swap(parts[:, 1], bit)
        values = jnp.stack([parts[:, 0], other], 1).reshape(values.shape)
        bit *= 2
    return values


def place():
    d = lax.axis_index("dp")
    return lax.axis_index("section"), d // 2, d % 2, lax.axis_index("tensor")


def ordered(flag, own, other, axis):
    first = jnp.where(flag == 0, own, other)
    second = jnp.where(flag == 0, other, own)
    return jnp.concatenate([first, second], axis)


def at(values, index):
    return lax.dynamic_index_in_dim(values, index, 0, keepdims=False)


def rows_over_hosts(value, axis):
    _, h, _, _ = place()
    bit = 1
    while bit < lax.axis_size("dp") // 2:
        other = host_swap(value, bit)
        value = ordered((h // bit) % 2, value, other, axis)
        bit *= 2
    return value


def to_groups(rows):
    _, _, c, t = place()
    count, piece, width = rows.shape
    parts = rows.reshape(count, 2, piece // 2, width)
    keep = jnp.where(c == 0, parts[:, 0], parts[:, 1])
    give = jnp.where(c == 0, parts[:, 1], parts[:, 0])
    four = ordered(c, keep, core_swap(give), 0)
    got = jnp.stack([at(four, t)] + [tensor_swap(at(four, t ^ j), j) for j in (1, 2, 3)])
    halves = jnp.stack([at(got, t ^ p) for p in range(4)])
    whole = ordered(c, halves[:, None], core_swap(halves)[:, None], 1)
    return whole.reshape(4 * piece, width)


def from_groups(rows):
    _, _, c, t = place()
    length, width = rows.shape
    half = length // 8
    parts = rows.reshape(4, 2, half, width)
    mine = jnp.where(c == 0, parts[:, 0], parts[:, 1])
    got = jnp.stack([at(mine, t)] + [tensor_swap(at(mine, t ^ j), j) for j in (1, 2, 3)])
    four = jnp.stack([at(got, t ^ p) for p in range(4)])
    keep = jnp.where(c == 0, four[:2], four[2:])
    give = jnp.where(c == 0, four[2:], four[:2])
    whole = ordered(c, keep[:, None], core_swap(give)[:, None], 1)
    return whole.reshape(2, 2 * half, width)


def head_lanes(width, head):
    lane = lax.broadcasted_iota(jnp.int32, (1, width), 1)
    return (lane // HEAD_DIM) == head


def attend_kernel(heads, prefix_ref, q_ref, k_ref, v_ref, base_ref, o_ref, a_ref, strip):
    block = pl.program_id(0)
    rows, width = q_ref.shape
    length = k_ref.shape[0]
    span = base_ref.shape[1]

    @pl.when(block == 0)
    def _():
        sub = lax.broadcasted_iota(jnp.int32, (8, span), 0)
        for head in range(heads):
            part = jnp.broadcast_to(base_ref[head : head + 1, :], (8, span))
            for bit in (1, 2, 4):
                part = jnp.where((sub & bit) != 0, pltpu.roll(part, bit, 1), part)
            size = 8
            while size < rows:
                part = jnp.concatenate([part, pltpu.roll(part, size, 1)], 0)
                size *= 2
            strip[head] = part

    start = pl.multiple_of((length // rows - 1 - block) * rows, rows)
    row = block * rows + lax.broadcasted_iota(jnp.int32, (rows, length), 0)
    col = lax.broadcasted_iota(jnp.int32, (rows, length), 1)
    allowed = (col <= row) | (col < prefix_ref[0])
    queries, keys, values = q_ref[...], k_ref[...], v_ref[...]
    out = jnp.zeros((rows, width), F32)
    for head in range(heads):
        lanes = head_lanes(width, head)
        own = jnp.where(lanes, queries, jnp.zeros_like(queries))
        scores = lax.dot_general(own, keys, (((1,), (1,)), ((), ())), preferred_element_type=F32)
        scores = scores * HEAD_DIM ** (-0.5) + strip[head, :, pl.ds(start, length)]
        scores = jnp.where(allowed, scores, MASKED)
        weights = jnp.exp(scores - jnp.max(scores, -1, keepdims=True))
        weights = weights / jnp.sum(weights, -1, keepdims=True)
        low = weights.astype(BF16)
        a_ref[head] = low
        out = jnp.where(lanes, jnp.dot(low, values, preferred_element_type=F32), out)
    o_ref[...] = out.astype(BF16)


def attend(qkv, base, prefix):
    _, length, width = qkv.shape
    heads = width // HEAD_DIM
    span = base.shape[1]
    return pl.pallas_call(
        functools.partial(attend_kernel, heads),
        grid=(length // BLOCK,),
        in_specs=[
            pl.BlockSpec(memory_space=pltpu.SMEM),
            pl.BlockSpec((None, BLOCK, width), lambda i: (0, i, 0)),
            pl.BlockSpec((None, length, width), lambda i: (1, 0, 0)),
            pl.BlockSpec((None, length, width), lambda i: (2, 0, 0)),
            pl.BlockSpec((heads, span), lambda i: (0, 0)),
        ],
        out_specs=[
            pl.BlockSpec((BLOCK, width), lambda i: (i, 0)),
            pl.BlockSpec((heads, BLOCK, length), lambda i: (0, i, 0)),
        ],
        out_shape=[
            jax.ShapeDtypeStruct((length, width), BF16),
            jax.ShapeDtypeStruct((heads, length, length), BF16),
        ],
        scratch_shapes=[pltpu.VMEM((heads, BLOCK, span), F32)],
        compiler_params=pltpu.CompilerParams(vmem_limit_bytes=40 * 2**20),
    )(prefix, qkv, qkv, qkv, base)


def attend_back_kernel(
    heads, q_ref, k_ref, v_ref, a_ref, do_ref, dq_ref, dk_ref, dv_ref, diag_ref, dk, dv, strip
):
    block = pl.program_id(0)
    rows, width = q_ref.shape
    length = k_ref.shape[0]
    span = strip.shape[2]
    scaling = HEAD_DIM ** (-0.5)

    @pl.when(block == 0)
    def _():
        dk[...] = jnp.zeros_like(dk)
        dv[...] = jnp.zeros_like(dv)
        strip[...] = jnp.zeros_like(strip)

    start = pl.multiple_of((length // rows - 1 - block) * rows, rows)
    queries, keys, values, grads = q_ref[...], k_ref[...], v_ref[...], do_ref[...]
    dq = jnp.zeros((rows, width), F32)
    for head in range(heads):
        lanes = head_lanes(width, head)
        low = a_ref[head]
        own_grad = jnp.where(lanes, grads, jnp.zeros_like(grads))
        own_query = jnp.where(lanes, queries, jnp.zeros_like(queries))
        weights = low.astype(F32)
        da = lax.dot_general(own_grad, values, (((1,), (1,)), ((), ())), preferred_element_type=F32)
        ds = weights * (da - jnp.sum(weights * da, -1, keepdims=True))
        ds = ds.astype(BF16)
        dq = jnp.where(lanes, jnp.dot(ds, keys, preferred_element_type=F32), dq)
        dk[...] += lax.dot_general(
            ds, own_query, (((0,), (0,)), ((), ())), preferred_element_type=F32
        )
        dv[...] += lax.dot_general(
            low, own_grad, (((0,), (0,)), ((), ())), preferred_element_type=F32
        )
        strip[head, :, pl.ds(start, length)] += ds.astype(F32)
    dq_ref[...] = (dq * scaling).astype(BF16)

    @pl.when(block == length // rows - 1)
    def _():
        dk_ref[...] = (dk[...] * scaling).astype(BF16)
        dv_ref[...] = dv[...].astype(BF16)
        sub = lax.broadcasted_iota(jnp.int32, (8, span), 0)
        for head in range(heads):
            part = strip[head]
            size = rows // 2
            while size >= 8:
                part = part[:size] + pltpu.roll(part[size:], span - size, 1)
                size //= 2
            for bit in (4, 2, 1):
                part = jnp.where((sub & bit) != 0, pltpu.roll(part, span - bit, 1), part)
            diag_ref[head : head + 1, :] = jnp.sum(part, 0, keepdims=True)


def attend_back(qkv, weights, grads):
    _, length, width = qkv.shape
    heads = width // HEAD_DIM
    span = 2 * length
    whole = jax.ShapeDtypeStruct((length, width), BF16)
    return pl.pallas_call(
        functools.partial(attend_back_kernel, heads),
        grid=(length // BLOCK,),
        in_specs=[
            pl.BlockSpec((None, BLOCK, width), lambda i: (0, i, 0)),
            pl.BlockSpec((None, length, width), lambda i: (1, 0, 0)),
            pl.BlockSpec((None, length, width), lambda i: (2, 0, 0)),
            pl.BlockSpec((heads, BLOCK, length), lambda i: (0, i, 0)),
            pl.BlockSpec((BLOCK, width), lambda i: (i, 0)),
        ],
        out_specs=[
            pl.BlockSpec((BLOCK, width), lambda i: (i, 0)),
            pl.BlockSpec((length, width), lambda i: (0, 0)),
            pl.BlockSpec((length, width), lambda i: (0, 0)),
            pl.BlockSpec((heads, span), lambda i: (0, 0)),
        ],
        out_shape=[whole, whole, whole, jax.ShapeDtypeStruct((heads, span), F32)],
        scratch_shapes=[
            pltpu.VMEM((length, width), F32),
            pltpu.VMEM((length, width), F32),
            pltpu.VMEM((heads, BLOCK, span), F32),
        ],
        compiler_params=pltpu.CompilerParams(vmem_limit_bytes=40 * 2**20),
    )(qkv, qkv, qkv, weights, grads)


def norm(values, gain):
    scale = lax.rsqrt(jnp.mean(values * values, -1, keepdims=True) + EPSILON)
    return scale, (values * scale * gain).astype(BF16)


def norm_back(values, scale, gain, grad):
    scaled = grad * gain
    mean = jnp.mean(scaled * values, -1, keepdims=True)
    return (
        scale * scaled - values * (scale * scale * scale) * mean,
        jnp.sum(grad * values * scale, axis=0),
    )


def attention_weights(pieces):
    x, h, c, t = place()
    quarter = x + 2 * c
    both = ordered(c, pieces[:3], core_swap(pieces[:3]), 1)
    arrived = None
    for j in (1, 2, 3):

        def to(x, h, c, t, j=j):
            return (x, h, c, t ^ j) if t == x + 2 * c else None

        part = send(both, to)
        arrived = part if arrived is None else arrived + part
    qkv = rows_over_hosts(jnp.where(t == quarter, both, arrived)[:, None], 1)
    qkv = qkv.reshape(3, -1, pieces.shape[2])
    out = pieces[3]
    got = jnp.stack([out] + [tensor_swap(out, j) for j in (1, 2, 3)])
    four = jnp.stack([at(got, t ^ p) for p in range(4)])
    four = rows_over_hosts(four[:, None], 1)
    four = ordered(c, four[:, :, None], core_swap(four)[:, :, None], 2)
    out = jnp.transpose(four, (1, 2, 3, 0, 4)).reshape(qkv.shape[1], -1)
    return qkv, out


def weights_out(i):
    def to(x, h, c, t):
        return (x, h, t >> 1, c + 2 * (i ^ (t & 1)))

    return to


def weights_home(i):
    def to(x, h, c, t):
        return (x, h, t & 1, 2 * c + (i ^ (t >> 1)))

    return to


def expert_weights(up, down):
    up = jnp.concatenate([send(up, weights_out(i)) for i in range(2)], 1)
    down = jnp.concatenate([send(down, weights_out(i)) for i in range(2)], 0)
    return up, down


def expert_grads_home(layer, grad_up, grad_down):
    half = grad_up.shape[1] // 2

    def home(first, second):
        first = send(first.astype(BF16), weights_home(0)).astype(F32)
        return first + send(second.astype(BF16), weights_home(1)).astype(F32)

    grad_up = home(grad_up[:, :half], grad_up[:, half:])
    grad_down = home(grad_down[:half], grad_down[half:])

    def across(value):
        return send(
            value.astype(BF16), lambda x, h, c, t: (layer, h, c, t) if x != layer else None
        ).astype(F32)

    return (grad_up, across(grad_up)), (grad_down, across(grad_down))


def to_expert(selection, rows, experts):
    _, _, c, _ = place()
    half = rows.shape[1] // 2
    own = jnp.where(c == 0, rows[:, :half], rows[:, half:])
    buffers = jnp.dot(selection, own, preferred_element_type=F32).astype(BF16)
    buffers = buffers.reshape(experts, -1, half)
    if experts > DIRECT:
        arrived = expert_exchange(buffers).reshape(-1, half)
    else:
        arrived = jnp.concatenate(
            [buffers[0]] + [expert_swap(buffers[j], j) for j in range(1, experts)], 0
        )
    return ordered(c, arrived, core_swap(arrived), 1)


def from_expert(selection, partial, experts):
    _, _, c, _ = place()
    half = partial.shape[1] // 2
    keep = jnp.where(c == 0, partial[:, :half], partial[:, half:])
    give = jnp.where(c == 0, partial[:, half:], partial[:, :half])
    chip = (keep + core_swap(give.astype(BF16)).astype(F32)).astype(BF16)
    chip = chip.reshape(experts, -1, half)
    if experts > DIRECT:
        total = (chip.astype(F32) + section_swap(chip).astype(F32)).astype(BF16)
        produced = expert_exchange(total).reshape(-1, half)
    else:
        back = [None] * experts
        for j in range(experts - 1, -1, -1):
            total = (chip[j].astype(F32) + section_swap(chip[j]).astype(F32)).astype(BF16)
            back[j] = total if j == 0 else expert_swap(total, j)
        produced = jnp.concatenate(back, 0)
    rows = lax.dot_general(
        selection, produced, (((0,), (0,)), ((), ())), preferred_element_type=F32
    ).astype(BF16)
    return ordered(c, rows, core_swap(rows), 1)


def layer_forward(rows, params, attention, expert, table, experts):
    gain_one, base, prefix, gain_two, router, chosen, selection = params
    qkv_weights, out_weights = attention
    up, down = expert
    x, _, c, _ = place()
    values = rows.astype(F32)
    scale_one, normed = norm(values, gain_one)
    qkv = jnp.einsum("rx,vxj->vrj", normed, qkv_weights, preferred_element_type=F32).astype(BF16)
    own, weights = attend(qkv, base, prefix)
    pair = ordered(x, own, section_swap(own), 1)
    merged = ordered(c, pair, core_swap(pair), 1)
    middle = values + lax.dot_general(
        merged, out_weights, (((1,), (1,)), ((), ())), preferred_element_type=F32
    )
    scale_two, normed_two = norm(middle, gain_two)
    logits = jnp.dot(normed_two, router, preferred_element_type=F32)
    probs = jax.nn.softmax(logits, -1)
    gates = jnp.sum(probs * chosen, 1, keepdims=True)
    arrived = to_expert(selection, normed_two, experts)
    hidden = jnp.dot(arrived, up, preferred_element_type=F32)
    active = jax.nn.gelu(hidden).astype(BF16)
    partial = jnp.dot(active, down, preferred_element_type=F32)
    produced = from_expert(selection, partial, experts).astype(F32)
    result = middle + gates * produced
    saved = (
        values,
        scale_one,
        normed,
        qkv,
        own,
        weights,
        middle,
        scale_two,
        normed_two,
        probs,
        gates,
        arrived,
        hidden,
        active,
        produced,
    )
    return result.astype(BF16), saved


def layer_backward(layer, grad, saved, params, attention, expert, experts):
    gain_one, base, prefix, gain_two, router, chosen, selection = params
    qkv_weights, out_weights = attention
    up, down = expert
    (
        values,
        scale_one,
        normed,
        qkv,
        own,
        weights,
        middle,
        scale_two,
        normed_two,
        probs,
        gates,
        arrived,
        hidden,
        active,
        produced,
    ) = saved
    x, h, c, t = place()
    grad = grad.astype(F32)
    grad_expert = (gates * grad).astype(BF16)
    grad_gates = jnp.sum(grad * produced, -1, keepdims=True)
    grad_arrived = to_expert(selection, grad_expert, experts)
    grad_active = lax.dot_general(
        grad_arrived, down, (((1,), (1,)), ((), ())), preferred_element_type=F32
    )
    grad_hidden = jax.vjp(jax.nn.gelu, hidden)[1](grad_active)[0].astype(BF16)
    partial = lax.dot_general(
        grad_hidden, up, (((1,), (1,)), ((), ())), preferred_element_type=F32
    )
    over_rows = (((0,), (0,)), ((), ()))
    grad_up = lax.dot_general(arrived, grad_hidden, over_rows, preferred_element_type=F32)
    grad_down = lax.dot_general(active, grad_arrived, over_rows, preferred_element_type=F32)
    expert_grads = expert_grads_home(layer, grad_up, grad_down)
    grad_normed_two = from_expert(selection, partial, experts).astype(F32)
    grad_probs = chosen * grad_gates
    grad_logits = (
        probs * (grad_probs - jnp.sum(probs * grad_probs, 1, keepdims=True))
    ).astype(BF16)
    grad_router = lax.dot_general(
        normed_two, grad_logits, over_rows, preferred_element_type=F32
    )
    grad_normed_two = grad_normed_two + lax.dot_general(
        grad_logits, router, (((1,), (1,)), ((), ())), preferred_element_type=F32
    )
    grad_middle, grad_gain_two = norm_back(middle, scale_two, gain_two, grad_normed_two)
    grad_middle = grad_middle + grad
    grad_low = grad_middle.astype(BF16)
    width = own.shape[1]
    own_weights = lax.dynamic_slice_in_dim(out_weights, (x + 2 * c) * width, width, 1)
    grad_own = jnp.dot(grad_low, own_weights, preferred_element_type=F32).astype(BF16)
    dq, dk, dv, diagonal = attend_back(qkv, weights, grad_own)
    dp = jnp.stack([dq, dk, dv])
    partial = jnp.einsum("vrj,vxj->rx", dp, qkv_weights, preferred_element_type=F32)
    half = partial.shape[1] // 2
    keep = jnp.where(c == 0, partial[:, :half], partial[:, half:])
    give = jnp.where(c == 0, partial[:, half:], partial[:, :half])
    chip = (keep + core_swap(give.astype(BF16)).astype(F32)).astype(BF16)
    total = (chip.astype(F32) + section_swap(chip).astype(F32)).astype(BF16)
    grad_normed = ordered(c, total, core_swap(total), 1).astype(F32)
    grad_rows, grad_gain_one = norm_back(values, scale_one, gain_one, grad_normed)
    grad_rows = (grad_rows + grad_middle).astype(BF16)
    grad_in = jnp.einsum("rx,vrj->xvj", normed, dp, preferred_element_type=F32)
    grad_out = lax.dot_general(grad_low, own, over_rows, preferred_element_type=F32)
    head_grads = jnp.concatenate([grad_in, grad_out[:, None]], 1)
    head_grads = head_grads.reshape(head_grads.shape[0], -1)
    small = (grad_gain_one, grad_gain_two, grad_router, diagonal)
    return grad_rows, expert_grads, head_grads_home(layer, head_grads), small


def head_grads_home(layer, grads):
    _, h, _, t = place()
    groups = 2 * lax.axis_size("dp")
    pieces = grads.astype(BF16).reshape(groups, -1, grads.shape[1])
    mine = 4 * h + t

    def swap(value, j):
        def to(x, h, c, t):
            n = (4 * h + t) ^ j
            return (x, n >> 2, c, n & 3)

        return send(value, to)

    if groups > DIRECT:
        bit = groups // 2
        while bit:
            pair = pieces.reshape(2, bit, *pieces.shape[1:])
            upper = (mine & bit) != 0
            keep = jnp.where(upper, pair[1], pair[0]).astype(F32)
            give = jnp.where(upper, pair[0], pair[1]).astype(BF16)
            pieces = keep + swap(give, bit).astype(F32)
            bit //= 2
        total = pieces[0].astype(BF16)
    else:
        total = at(pieces, mine).astype(F32)
        for j in range(1, groups):
            total = total + swap(at(pieces, mine ^ j), j).astype(F32)
        total = total.astype(BF16)
    parts = []
    for i in range(2):

        def home(x, h, c, t, i=i):
            return (layer, h, t >> 1, x + 2 * c) if t & 1 == i else None

        parts.append(send(total, home))
    whole = jnp.concatenate(parts, 0).astype(F32)
    return whole.reshape(whole.shape[0], 4, -1)


def pick(flag, first, second):
    return jax.tree.map(lambda a, b: jnp.where(flag == 0, a, b), first, second)


def per_device(
    block_input,
    cotangent,
    query_key_value_weights,
    attention_output_weights,
    bias_table,
    norm_first,
    norm_second,
    router_projection_weights,
    expert_up,
    expert_down,
    routes,
    prefix_lengths,
    relative_buckets,
):
    x, h, c, t = place()
    _, piece, width = block_input.shape
    length = routes.shape[2]
    buckets, head_count = bias_table.shape[1:]
    experts = router_projection_weights.shape[2]
    heads = head_count // 4
    capacity = (5 * length + 4 * experts - 1) // (4 * experts)

    pieces = jnp.concatenate(
        [query_key_value_weights[0], attention_output_weights[0].T[None]], 0
    )
    other = section_swap(pieces)
    pieces = pick(x, (pieces, other), (other, pieces))
    scale = 32
    packed = jnp.concatenate(
        [
            routes[0, :, :, 0].reshape(-1),
            prefix_lengths // scale,
            prefix_lengths % scale,
        ]
    ).astype(BF16)
    both = ordered(c, packed[None], core_swap(packed)[None], 0)
    lower = at(both, t >> 1)
    route = lax.dynamic_slice_in_dim(lower, (t & 1) * length, length, 0)
    numbers = lower[2 * length :].astype(F32).astype(jnp.int32)
    prefix = lax.dynamic_slice_in_dim(numbers[:2] * scale + numbers[2:], t & 1, 1, 0)
    packed = jnp.concatenate(
        [
            route,
            norm_first[0],
            norm_second[0],
            router_projection_weights[0].reshape(-1),
            bias_table[0].reshape(-1),
        ]
    )
    other = section_swap(packed)
    packed = pick(x, (packed, other), (other, packed))

    half = expert_up.shape[3] // 2
    up, down = expert_up[0, 0], expert_down[0, 0]
    give = jnp.where(x == 0, up[:, half:], up[:, :half])
    keep = jnp.where(x == 0, up[:, :half], up[:, half:])
    other = section_swap(give)
    ups = pick(x, (keep, other), (other, keep))
    give = jnp.where(x == 0, down[half:], down[:half])
    keep = jnp.where(x == 0, down[:half], down[half:])
    other = section_swap(give)
    downs = pick(x, (keep, other), (other, keep))

    rows = to_groups(block_input)
    top = to_groups(cotangent)

    bucket_onehot = (
        relative_buckets[:, None] == jnp.arange(buckets, dtype=jnp.int32)[None, :]
    ).astype(BF16)
    earlier = (
        jnp.arange(length, dtype=jnp.int32)[None, :] < jnp.arange(length, dtype=jnp.int32)[:, None]
    ).astype(BF16)
    expert_ids = jnp.arange(experts, dtype=jnp.int32)

    def unpack(vector):
        route = vector[:length].astype(F32).astype(jnp.int32)
        at_one = length
        gain_one = vector[at_one : at_one + width].astype(F32)
        at_two = at_one + width
        gain_two = vector[at_two : at_two + width].astype(F32)
        at_router = at_two + width
        router = vector[at_router : at_router + width * experts].reshape(width, experts)
        table = vector[at_router + width * experts :].reshape(buckets, head_count)
        own = lax.dynamic_slice_in_dim(table, (x + 2 * c) * heads, heads, 1)
        rel = lax.dot_general(
            own, bucket_onehot, (((0,), (1,)), ((), ())), preferred_element_type=F32
        )
        base = jnp.roll(jnp.pad(rel, ((0, 0), (0, 1))), -(BLOCK - 1), axis=1)
        chosen = route[:, None] == expert_ids[None, :]
        rank = jnp.dot(earlier, chosen.astype(BF16), preferred_element_type=F32)
        rank = jnp.sum(jnp.where(chosen, rank, 0.0), 1).astype(jnp.int32)
        slot = (route ^ (2 * h + (t & 1))) * capacity + rank
        selection = (
            slot[None, :] == jnp.arange(experts * capacity, dtype=jnp.int32)[:, None]
        ).astype(BF16)
        return (gain_one, base, prefix, gain_two, router, chosen.astype(F32), selection)

    params = [unpack(vector) for vector in packed]
    attention = [attention_weights(part) for part in pieces]
    expert = [expert_weights(*pair) for pair in zip(ups, downs)]

    first, saved_first = layer_forward(rows, params[0], attention[0], expert[0], None, experts)
    second, saved_second = layer_forward(first, params[1], attention[1], expert[1], None, experts)
    outputs = from_groups(jnp.where(x == 0, first, second))

    grads_one = layer_backward(
        1, top, saved_second, params[1], attention[1], expert[1], experts
    )
    grads_zero = layer_backward(
        0, grads_one[0], saved_first, params[0], attention[0], expert[0], experts
    )
    grad_rows = from_groups(jnp.where(x == 0, grads_zero[0], grads_one[0]))

    def halves(zero, one, axis):
        own = jnp.where(x == 0, zero[0], one[0])
        other = jnp.where(x == 0, zero[1], one[1])
        return ordered(x, own, other, axis)

    grad_up = halves(grads_zero[1][0], grads_one[1][0], 1)
    grad_down = halves(grads_zero[1][1], grads_one[1][1], 0)
    heads_grad = jnp.where(x == 0, grads_zero[2], grads_one[2])
    grad_in = jnp.transpose(heads_grad[:, :3], (1, 0, 2))
    grad_out = heads_grad[:, 3].T

    def flat(small):
        gain_one, gain_two, router, diagonal = small
        total = jnp.roll(diagonal, BLOCK - 1, axis=1)[:, : 2 * length - 1]
        table = lax.dot_general(
            bucket_onehot.astype(F32),
            total,
            (((0,), (1,)), ((), ())),
            precision=lax.Precision.HIGHEST,
        )
        whole = lax.dynamic_update_slice_in_dim(
            jnp.zeros((buckets, head_count), F32), table, (x + 2 * c) * heads, 1
        )
        return jnp.concatenate([gain_one, gain_two, router.reshape(-1)]), whole.reshape(-1)

    shared = [flat(small) for small in (grads_zero[3], grads_one[3])]
    size = shared[0][0].shape[0]
    everything = jnp.concatenate([shared[0][0], shared[1][0], shared[0][1], shared[1][1]])
    for j in (1, 2):
        everything = everything + tensor_swap(everything, j)
    bit = 1
    while bit < lax.axis_size("dp") // 2:
        everything = everything + host_swap(everything, bit)
        bit *= 2
    tables = everything[2 * size :]
    tables = tables + core_swap(tables)
    tables = tables + section_swap(tables)
    table_grad = at(tables.reshape(2, buckets, head_count), x)
    own = lax.dynamic_slice_in_dim(everything, x * size, size, 0)
    return (
        outputs[None],
        grad_rows[None],
        grad_in[None],
        grad_out[None],
        table_grad[None],
        own[:width][None],
        own[width : 2 * width][None],
        own[2 * width :].reshape(width, experts)[None],
        grad_up[None, None],
        grad_down[None, None],
    )


def solution(mesh):
    in_specs = (
        P("dp", "tensor", None),
        P("dp", "tensor", None),
        P("section", None, "dp", "tensor"),
        P("section", "tensor", "dp"),
        P("section", None, None),
        P("section", None),
        P("section", None),
        P("section", None, None),
        P("section", "dp", None, "tensor"),
        P("section", "dp", "tensor", None),
        P("section", "dp", None, None),
        P("dp"),
        P(),
    )
    out_specs = (
        P("section", "dp", "tensor", None),
        P("section", "dp", "tensor", None),
        P("section", None, "dp", "tensor"),
        P("section", "tensor", "dp"),
        P("section", None, None),
        P("section", None),
        P("section", None),
        P("section", None, None),
        P("section", "dp", None, "tensor"),
        P("section", "dp", "tensor", None),
    )
    return jax.shard_map(
        per_device, mesh=mesh, in_specs=in_specs, out_specs=out_specs, check_vma=False
    )
```

```python
import functools

import jax
import jax.numpy as jnp
from jax import lax
from jax.experimental import pallas as pl
from jax.experimental.pallas import tpu as pltpu
from jax.sharding import PartitionSpec as P

HEAD_DIM = 64
EPSILON = 1e-06
MASKED = -1000000000.0
AXES = ("section", "dp", "tensor")
BLOCK = 128
DIRECT = 8
LONG = 10**11
BF16 = jnp.bfloat16
F32 = jnp.float32


def send(value, to):
    sections, width, depth = (lax.axis_size(name) for name in AXES)

    def number(x, h, c, t):
        return (x * width + 2 * h + c) * depth + t

    pairs = []
    for x in range(sections):
        for d in range(width):
            for t in range(depth):
                target = to(x, d // 2, d % 2, t)
                if target is not None:
                    pairs.append((number(x, d // 2, d % 2, t), number(*target)))
    return lax.ppermute(value, AXES, pairs)


def core_swap(value):
    return send(value, lambda x, h, c, t: (x, h, 1 - c, t))


def section_swap(value):
    return send(value, lambda x, h, c, t: (1 - x, h, c, t))


def tensor_swap(value, j):
    return send(value, lambda x, h, c, t: (x, h, c, t ^ j))


def host_swap(value, j):
    return send(value, lambda x, h, c, t: (x, h ^ j, c, t))


def expert_swap(value, j):
    def to(x, h, c, t):
        e = (2 * h + (t & 1)) ^ j
        return (x, e >> 1, c, (t & 2) | (e & 1))

    return send(value, to)


def expert_exchange(values):
    count, bit = values.shape[0], 1
    while bit < count:
        parts = values.reshape(count // (2 * bit), 2, bit, *values.shape[1:])
        other = expert_swap(parts[:, 1], bit)
        values = jnp.stack([parts[:, 0], other], 1).reshape(values.shape)
        bit *= 2
    return values


def place():
    d = lax.axis_index("dp")
    return lax.axis_index("section"), d // 2, d % 2, lax.axis_index("tensor")


def ordered(flag, own, other, axis):
    first = jnp.where(flag == 0, own, other)
    second = jnp.where(flag == 0, other, own)
    return jnp.concatenate([first, second], axis)


def at(values, index):
    return lax.dynamic_index_in_dim(values, index, 0, keepdims=False)


def rows_over_hosts(value, axis):
    _, h, _, _ = place()
    bit = 1
    while bit < lax.axis_size("dp") // 2:
        other = host_swap(value, bit)
        value = ordered((h // bit) % 2, value, other, axis)
        bit *= 2
    return value


def to_groups(rows):
    _, _, _, t = place()
    got = []
    for i in range(2):

        def to(x, h, c, t, i=i):
            return (x, h, 1 - (t >> 1), 2 * c + (i ^ (t & 1)))

        got.append(send(at(rows, i ^ (t & 1)), to))
    return got + [core_swap(part) for part in got]


def piece_order():
    c, low = which_core(), lax.axis_index("tensor") & 1
    return [2 * (1 - c) + low, 2 * (1 - c) + (1 - low), 2 * c + low, 2 * c + (1 - low)]


def whole_rows(pieces):
    order = piece_order()
    return jnp.concatenate([at_place(pieces, order, place) for place in range(4)], 0)


def at_place(pieces, order, place):
    value = pieces[3]
    for piece, number in zip(pieces[:3], order[:3]):
        value = jnp.where(number == place, piece, value)
    return value


def from_groups(rows):
    _, _, c, t = place()
    length, width = rows.shape
    pieces = rows.reshape(4, length // 4, width)
    got = []
    for i in range(2):

        def to(x, h, c, t, i=i):
            return (x, h, t >> 1, 2 * (1 - c) + (i ^ (t & 1)))

        got.append(send(at(pieces, 2 * (1 - c) + (i ^ (t & 1))), to))
    low = t & 1
    return jnp.stack([jnp.where(low == 0, got[0], got[1]), jnp.where(low == 0, got[1], got[0])])


def head_lanes(width, head):
    lane = lax.broadcasted_iota(jnp.int32, (1, width), 1)
    return (lane // HEAD_DIM) == head


def dot(a, b, contract=(1, 0)):
    dims = (((contract[0],), (contract[1],)), ((), ()))
    return lax.dot_general(a, b, dims, preferred_element_type=F32)


def which_core():
    return lax.rem(lax.axis_index("dp"), 2)


def which_member():
    return lax.axis_index("section") + 2 * which_core()


def half_at(index, half):
    return pl.ds(pl.multiple_of(index * half, half), half)


def row_scale(values):
    return lax.rsqrt(jnp.mean(values * values, -1, keepdims=True) + EPSILON)


def call(kernel, inputs, outputs, grid=(1,), scratch=(), vmem=24, flops=10**9):
    def spec(item):
        value, given = item
        if given is not None:
            return given
        return pl.BlockSpec(value.shape, lambda i, n=len(value.shape): (0,) * n)

    return pl.pallas_call(
        kernel,
        grid=grid,
        in_specs=[spec(item) for item in inputs],
        out_specs=[spec(item) for item in outputs],
        out_shape=[item[0] for item in outputs],
        scratch_shapes=list(scratch),
        cost_estimate=pl.CostEstimate(flops=flops, bytes_accessed=1000, transcendentals=0),
        compiler_params=pltpu.CompilerParams(vmem_limit_bytes=vmem * 2**20),
    )(*[item[0] for item in inputs])


def shape_of(*dims, dtype=BF16):
    return jax.ShapeDtypeStruct(dims, dtype)


SMEM = pl.BlockSpec(memory_space=pltpu.SMEM)


def attend_kernel(heads, mix, parts, *refs):
    if mix:
        middle_ref, gate_ref, own_ref, other_ref, *refs = refs
    else:
        row_refs, refs = refs[:4], refs[4:]
    part_refs, refs = refs[:parts], refs[parts:]
    prefix_ref, gain_ref, base_ref, x_ref, normed_ref, qkv_ref, w_ref, *refs = refs
    o_ref, a_ref, strip, causal, scores_ref = refs
    block = pl.program_id(0)
    length, width = x_ref.shape
    rows = o_ref.shape[0]
    span = base_ref.shape[1]
    lanes_all = o_ref.shape[1]

    @pl.when(block == 0)
    def _():
        step = 256
        for j, ref in enumerate(part_refs):
            count = ref.shape[1]
            first = (lax.axis_index("dp") ^ j) * count if parts > 1 else 0
            first = pl.multiple_of(first, 8) if parts > 1 else 0
            for v in range(3):
                w_ref[v, pl.ds(first, count), :] = ref[v]
        if not mix:
            for ref, piece in zip(row_refs, piece_order()):
                count = ref.shape[0]
                x_ref[pl.ds(pl.multiple_of(piece * count, count), count), :] = ref[...]
        for at_row in range(0, length, step):
            part = pl.ds(at_row, step)
            if mix:
                half = width // 2
                core = which_core()
                for ref, side in ((own_ref, core), (other_ref, 1 - core)):
                    lanes = half_at(side, half)
                    value = middle_ref[part, lanes] + gate_ref[part, :] * ref[part, :].astype(F32)
                    x_ref[part, lanes] = value.astype(BF16)
            values = x_ref[part, :].astype(F32)
            normed = (values * row_scale(values) * gain_ref[...]).astype(BF16)
            normed_ref[part, :] = normed
            for v in range(3):
                qkv_ref[v, part, :] = dot(normed, w_ref[v]).astype(BF16)
        sub = lax.broadcasted_iota(jnp.int32, (8, span), 0)
        for head in range(heads):
            part = jnp.broadcast_to(base_ref[head : head + 1, :], (8, span))
            for bit in (1, 2, 4):
                part = jnp.where((sub & bit) != 0, pltpu.roll(part, bit, 1), part)
            size = 8
            while size < rows:
                part = jnp.concatenate([part, pltpu.roll(part, size, 1)], 0)
                size *= 2
            strip[head] = part
            ahead = lax.broadcasted_iota(jnp.int32, (rows, span), 1) - lax.broadcasted_iota(
                jnp.int32, (rows, span), 0
            )
            causal[head] = jnp.where(ahead > length - rows, MASKED, part)

    start = pl.multiple_of((length // rows - 1 - block) * rows, rows)
    here = pl.ds(pl.multiple_of(block * rows, rows), rows)
    col = lax.broadcasted_iota(jnp.int32, (1, length), 1)
    inside = col < prefix_ref[0]
    queries, keys, values = qkv_ref[0, here, :], qkv_ref[1], qkv_ref[2]
    queries = queries * jnp.asarray(HEAD_DIM ** (-0.5), BF16)
    step = 32
    for head in range(heads):
        own = jnp.where(head_lanes(lanes_all, head), queries, jnp.zeros_like(queries))
        scores_ref[head] = dot(own, keys, (1, 1))
    out = jnp.zeros((rows, lanes_all), F32)
    for head in range(heads):
        for at_row in range(0, rows, step):
            part = pl.ds(at_row, step)
            across = pl.ds(start, length)
            bias = jnp.where(inside, strip[head, part, across], causal[head, part, across])
            scores = scores_ref[head, part, :] + bias
            weights = jnp.exp(scores - jnp.max(scores, -1, keepdims=True))
            weights = weights * (1.0 / jnp.sum(weights, -1, keepdims=True))
            a_ref[head, part, :] = weights.astype(BF16)
        out = jnp.where(head_lanes(lanes_all, head), dot(a_ref[head], values), out)
    o_ref[...] = out.astype(BF16)


def attend(source, mix, prefix, gain, weights, base):
    width = gain.shape[1]
    length = source[0].shape[0] * (1 if mix else 4)
    lanes = weights[0].shape[2]
    heads = lanes // HEAD_DIM
    span = base.shape[1]
    inputs = [(part, None) for part in (*source, *weights)]
    inputs += [(prefix, SMEM), (gain, None), (base, None)]
    return call(
        functools.partial(attend_kernel, heads, mix, len(weights)),
        inputs,
        [
            (shape_of(length, width), None),
            (shape_of(length, width), None),
            (shape_of(3, length, lanes), None),
            (shape_of(3, width, lanes), None),
            (shape_of(length, lanes), pl.BlockSpec((BLOCK, lanes), lambda i: (i, 0))),
            (
                shape_of(heads, length, length),
                pl.BlockSpec((heads, BLOCK, length), lambda i: (0, i, 0)),
            ),
        ],
        grid=(length // BLOCK,),
        scratch=[
            pltpu.VMEM((heads, BLOCK, span), F32),
            pltpu.VMEM((heads, BLOCK, span), F32),
            pltpu.VMEM((heads, BLOCK, length), F32),
        ],
        vmem=58,
        flops=LONG,
    )


def pieces_of(experts):
    return experts if experts <= DIRECT else 1


def selection_block(slot_ref, first, count):
    ids = first + lax.broadcasted_iota(jnp.int32, (count, slot_ref.shape[1]), 0)
    return jnp.where(ids == slot_ref[...], 1.0, 0.0).astype(BF16)


def dispatch_blocks(step, steps, slot_ref, rows_ref, buffer_refs):
    half = rows_ref.shape[1] // 2
    total = sum(ref.shape[0] for ref in buffer_refs) if len(buffer_refs) > 1 else None
    lanes = half_at(which_core(), half)
    if total is None:

        @pl.when(step >= steps)
        def _():
            count = buffer_refs[0].shape[0]
            chosen = selection_block(slot_ref, (step - steps) * count, count)
            buffer_refs[0][...] = dot(chosen, rows_ref[:, lanes]).astype(BF16)

        return
    first = 0
    for index, ref in enumerate(buffer_refs):

        @pl.when(step == steps + index)
        def _(ref=ref, first=first):
            chosen = selection_block(slot_ref, first, ref.shape[0])
            ref[...] = dot(chosen, rows_ref[:, lanes]).astype(BF16)

        first += ref.shape[0]


def buffer_outputs(experts, rows, half, steps):
    count = pieces_of(experts)
    if count > 1:
        return [(shape_of(rows // count, half), None)] * count, steps + count
    blocks = 4
    spec = pl.BlockSpec((rows // blocks, half), lambda i: (jnp.maximum(i - steps, 0), 0))
    return [(shape_of(rows, half), spec)], steps + blocks


def router_probs(normed, router_ref, experts):
    logits = dot(normed, router_ref[...])
    real = lax.broadcasted_iota(jnp.int32, logits.shape, 1) < experts
    logits = jnp.where(real, logits, MASKED)
    weights = jnp.exp(logits - jnp.max(logits, -1, keepdims=True))
    weights = jnp.where(real, weights, 0.0)
    return weights / jnp.sum(weights, -1, keepdims=True)


def middle_kernel(experts, steps, *refs):
    x_ref, *refs = refs
    piece_refs, refs = refs[:4], refs[4:]
    w_ref, gain_ref, router_ref, chosen_ref, slot_ref, middle_ref, normed_ref, gate_ref = refs[:8]
    buffer_refs, kept = refs[8:-1], refs[-1]
    step = pl.program_id(0)
    rows = x_ref.shape[0]

    @pl.when(step < steps)
    def _():
        member = which_member()
        parts = [dot(ref[...], w_ref[member ^ j], (1, 1)) for j, ref in enumerate(piece_refs)]
        values = x_ref[...].astype(F32) + ((parts[0] + parts[1]) + (parts[2] + parts[3]))
        middle_ref[...] = values
        normed = (values * row_scale(values) * gain_ref[...]).astype(BF16)
        normed_ref[...] = normed
        kept[pl.ds(pl.multiple_of(step * rows, rows), rows), :] = normed
        probs = router_probs(normed, router_ref, experts)
        gate_ref[...] = jnp.sum(probs * chosen_ref[...], -1, keepdims=True)

    dispatch_blocks(step, steps, slot_ref, kept, buffer_refs)


def middle_and_buffers(rows, pieces, weights, gain, router, chosen, slot, experts, slots):
    length, width = rows.shape
    steps = 4
    block = length // steps

    def by_rows(lanes):
        return pl.BlockSpec((block, lanes), lambda i: (jnp.minimum(i, steps - 1), 0))

    buffers, grid = buffer_outputs(experts, slots, width // 2, steps)
    lanes = pieces[0].shape[1]
    got = call(
        functools.partial(middle_kernel, experts, steps),
        [(rows, by_rows(width))]
        + [(piece, by_rows(lanes)) for piece in pieces]
        + [
            (weights, None),
            (gain, None),
            (router, None),
            (chosen, by_rows(chosen.shape[1])),
            (slot, None),
        ],
        [
            (shape_of(length, width, dtype=F32), by_rows(width)),
            (shape_of(length, width), by_rows(width)),
            (shape_of(length, 1, dtype=F32), by_rows(1)),
        ]
        + buffers,
        grid=(grid,),
        scratch=[pltpu.VMEM((length, width), BF16)],
    )
    return got[0], got[1], got[2], got[3:]


def order_of(index, count):
    return (index + count // 2) % count


def parts_of(refs, index, count):
    return refs[:2] if index >= count // 2 or count == 1 else refs[2:]


def part_outputs(rows, half, count):
    if count == 1:
        return [(shape_of(rows, half), None)] * 2
    split = count // 2
    shape = shape_of(rows * split, half)
    upper = pl.BlockSpec((rows, half), lambda i: (jnp.minimum(i, split - 1), 0))
    lower = pl.BlockSpec((rows, half), lambda i: (jnp.maximum(i - split, 0), 0))
    return [(shape, upper)] * 2 + [(shape, lower)] * 2


def ordered_blocks(rows, lanes, count):
    return pl.BlockSpec((rows, lanes), lambda i: ((i + count // 2) % count, 0))


GELU = 0.7978845608028654


def expert_kernel(count, *refs):
    own_refs, other_refs, refs = refs[:count], refs[count : 2 * count], refs[2 * count :]
    *pack_refs, active_ref, slope_ref = refs[:4]
    part_refs = refs[4:]
    half = own_refs[0].shape[1]
    upper, lower = pl.ds(0, half), pl.ds(half, half)
    core = which_core()
    step = pl.program_id(0)
    for index in range(count):
        keep_ref, give_ref = parts_of(part_refs, index, count)

        @pl.when(step == order_of(index, count))
        def _(index=index, keep_ref=keep_ref, give_ref=give_ref):
            mine, others = half_at(core, half), half_at(1 - core, half)
            own, other = own_refs[index][...], other_refs[index][...]
            keep = give = None
            for i, ref in enumerate(pack_refs):
                hidden = dot(own, ref[upper, mine]) + dot(other, ref[upper, others])
                square = hidden * hidden
                inner = jnp.tanh(GELU * hidden * (1.0 + 0.044715 * square))
                active = (0.5 * hidden * (1.0 + inner)).astype(BF16)
                slope = 0.5 * (1.0 + inner) + 0.5 * hidden * (1.0 - inner * inner) * (
                    GELU * (1.0 + 3 * 0.044715 * square)
                )
                active_ref[:, pl.ds(i * half, half)] = active
                slope_ref[:, pl.ds(i * half, half)] = slope.astype(BF16)
                first, second = dot(active, ref[lower, mine]), dot(active, ref[lower, others])
                keep = first if keep is None else keep + first
                give = second if give is None else give + second
            keep_ref[...] = keep.astype(BF16)
            give_ref[...] = give.astype(BF16)


def row_blocks(rows, lanes):
    return pl.BlockSpec((rows, lanes), lambda i: (i, 0))


def expert_rows(own, other, packs):
    count = len(own)
    rows, half = own[0].shape
    hidden = packs[0].shape[1]
    wide = (shape_of(rows * count, hidden), ordered_blocks(rows, hidden, count))
    got = call(
        functools.partial(expert_kernel, count),
        [(part, None) for part in own + other + packs],
        [wide, wide] + part_outputs(rows, half, count),
        grid=(count,),
    )
    return got[0], got[1], got[2:]


def expert_back_kernel(count, *refs):
    own_refs, other_refs, refs = refs[:count], refs[count : 2 * count], refs[2 * count :]
    slope_ref, *pack_refs, hidden_ref = refs[:4]
    part_refs = refs[4:]
    half = own_refs[0].shape[1]
    upper, lower = pl.ds(0, half), pl.ds(half, half)
    core = which_core()
    step = pl.program_id(0)
    for index in range(count):
        keep_ref, give_ref = parts_of(part_refs, index, count)

        @pl.when(step == order_of(index, count))
        def _(index=index, keep_ref=keep_ref, give_ref=give_ref):
            mine, others = half_at(core, half), half_at(1 - core, half)
            own, other = own_refs[index][...], other_refs[index][...]
            keep = give = None
            for i, ref in enumerate(pack_refs):
                lanes = pl.ds(i * half, half)
                grad = dot(own, ref[lower, mine], (1, 1)) + dot(other, ref[lower, others], (1, 1))
                grad = (grad * slope_ref[:, lanes].astype(F32)).astype(BF16)
                hidden_ref[:, lanes] = grad
                first = dot(grad, ref[upper, mine], (1, 1))
                second = dot(grad, ref[upper, others], (1, 1))
                keep = first if keep is None else keep + first
                give = second if give is None else give + second
            keep_ref[...] = keep.astype(BF16)
            give_ref[...] = give.astype(BF16)


def expert_rows_back(own, other, slope, packs):
    count = len(own)
    rows, half = own[0].shape
    hidden = packs[0].shape[1]
    blocks = ordered_blocks(rows, hidden, count)
    got = call(
        functools.partial(expert_back_kernel, count),
        [(part, None) for part in own + other]
        + [(slope, blocks)]
        + [(part, None) for part in packs],
        [(shape_of(rows * count, hidden), blocks)] + part_outputs(rows, half, count),
        grid=(count,),
    )
    return got[0], got[1:]


def expert_grads_kernel(count, *refs):
    own_refs, other_refs, refs = refs[:count], refs[count : 2 * count], refs[2 * count :]
    own_grads, other_grads, refs = refs[:count], refs[count : 2 * count], refs[2 * count :]
    active_ref, hidden_ref, first_ref, second_ref = refs
    rows, half = own_refs[0].shape
    core = which_core()
    for out, ref in enumerate((first_ref, second_ref)):
        own_half = pl.ds(out * half, half)
        for inputs, grads, side in (
            (own_refs, own_grads, core),
            (other_refs, other_grads, 1 - core),
        ):
            lanes = half_at(side, half)
            up = jnp.zeros((half, half), F32)
            down = jnp.zeros((half, half), F32)
            for index in range(count):
                part = pl.ds(index * rows, rows)
                up += dot(inputs[index][...], hidden_ref[part, own_half], (0, 0))
                down += dot(active_ref[part, own_half], grads[index][...], (0, 0))
            ref[pl.ds(0, half), lanes] = up.astype(BF16)
            ref[pl.ds(half, half), lanes] = down.astype(BF16)


def expert_weight_grads(own, other, own_grads, other_grads, active, hidden):
    count = len(own)
    rows, half = own[0].shape
    return call(
        functools.partial(expert_grads_kernel, count),
        [(part, None) for part in own + other + own_grads + other_grads]
        + [(active, None), (hidden, None)],
        [(shape_of(2 * half, 2 * half), None)] * 2,
        vmem=58,
    )


def combine_kernel(count, *refs):
    refs, slot_ref, out_ref = refs[:-2], refs[-2], refs[-1]
    block = out_ref.shape[0]
    total = jnp.zeros(out_ref.shape, F32)
    first = 0
    for index in range(count):
        if index == 0:
            value = (refs[0][...].astype(F32) + refs[1][...].astype(F32)).astype(BF16)
        else:
            value = refs[index + 1][...]
        ids = first + lax.broadcasted_iota(jnp.int32, (block, value.shape[0]), 1)
        chosen = jnp.where(ids == slot_ref[...], 1.0, 0.0).astype(BF16)
        total += dot(chosen, value)
        first += value.shape[0]
    out_ref[...] = total.astype(BF16)


def combine(first, rest, slot_column):
    length = slot_column.shape[0]
    half = first[0].shape[1]
    block = length // 4
    return call(
        functools.partial(combine_kernel, 1 + len(rest)),
        [(part, None) for part in first]
        + [(part, None) for part in rest]
        + [(slot_column, row_blocks(block, 1))],
        [(shape_of(length, half), row_blocks(block, half))],
        grid=(4,),
    )[0]


def grad_kernel(experts, steps, last, *refs):
    middle_ref, gate_ref, own_ref, other_ref, grad_ref, normed_ref, router_ref = refs[:7]
    chosen_ref, slot_ref, refs = refs[7], refs[8], refs[9:]
    if last:
        result_ref, *refs = refs
    logits_ref, refs = refs[0], refs[1:]
    buffer_refs, kept, joined = refs[:-2], refs[-2], refs[-1]
    step = pl.program_id(0)
    rows, width = middle_ref.shape

    @pl.when(step < steps)
    def _():
        half = width // 2
        core = which_core()
        joined[:, half_at(core, half)] = own_ref[...].astype(F32)
        joined[:, half_at(1 - core, half)] = other_ref[...].astype(F32)
        produced = joined[...]
        gate = gate_ref[...]
        if last:
            result_ref[...] = (middle_ref[...] + gate * produced).astype(BF16)
        grad = grad_ref[...].astype(F32)
        kept[pl.ds(pl.multiple_of(step * rows, rows), rows), :] = (gate * grad).astype(BF16)
        grad_gate = jnp.sum(grad * produced, -1, keepdims=True)
        probs = router_probs(normed_ref[...], router_ref, experts)
        grad_probs = chosen_ref[...] * grad_gate
        inner = jnp.sum(probs * grad_probs, -1, keepdims=True)
        logits_ref[...] = (probs * (grad_probs - inner)).astype(BF16)

    dispatch_blocks(step, steps, slot_ref, kept, buffer_refs)


def grads_and_buffers(
    middle, gate, own, other, grad, normed, router, chosen, slot, experts, slots, last
):
    length, width = middle.shape
    steps = 4
    block = length // steps

    def by_rows(value):
        lanes = value.shape[1]
        return (value, pl.BlockSpec((block, lanes), lambda i: (jnp.minimum(i, steps - 1), 0)))

    buffers, grid = buffer_outputs(experts, slots, width // 2, steps)
    outputs = [by_rows(shape_of(length, width))] if last else []
    outputs += [by_rows(shape_of(length, chosen.shape[1]))]
    got = call(
        functools.partial(grad_kernel, experts, steps, last),
        [by_rows(value) for value in (middle, gate, own, other, grad, normed)]
        + [(router, None), by_rows(chosen), (slot, None)],
        outputs + buffers,
        grid=(grid,),
        scratch=[pltpu.VMEM((length, width), BF16), pltpu.VMEM((block, width), F32)],
    )
    return got[: len(outputs)], got[len(outputs) :]


def attend_back_kernel(heads, *refs):
    own_ref, other_ref, logits_ref, router_ref, middle_ref, grad_ref, gain_ref = refs[:7]
    out_ref, qkv_ref, a_ref, w_ref, refs = refs[7], refs[8], refs[9], refs[10], refs[11:]
    mid_ref, low_ref, gain_grad_ref, dp_ref, diag_ref, keep_ref, give_ref = refs[:7]
    joined, grads_ref, dk, dv, strip, da_ref, ds_ref, query_ref, wide_ref = refs[7:]
    block = pl.program_id(0)
    length, width = middle_ref.shape
    rows = a_ref.shape[1]
    lanes_all = qkv_ref.shape[2]
    span = strip.shape[2]
    half = width // 2
    scaling = HEAD_DIM ** (-0.5)

    @pl.when(block == 0)
    def _():
        core = which_core()
        member = which_member()
        gain = gain_ref[...]
        gain_grad = jnp.zeros((1, width), F32)
        step = joined.shape[0]
        for at_row in range(0, length, step):
            part = pl.ds(at_row, step)
            joined[:, half_at(core, half)] = own_ref[part, :].astype(F32)
            joined[:, half_at(1 - core, half)] = other_ref[part, :].astype(F32)
            grad_normed = joined[...] + dot(logits_ref[part, :], router_ref[...], (1, 1))
            middle = middle_ref[part, :]
            scale = row_scale(middle)
            scaled = grad_normed * gain
            mean = jnp.mean(scaled * middle, -1, keepdims=True)
            grad = grad_ref[part, :].astype(F32) + (
                scale * scaled - middle * (scale * scale * scale) * mean
            )
            gain_grad += jnp.sum(grad_normed * middle * scale, 0, keepdims=True)
            mid_ref[part, :] = grad
            low = grad.astype(BF16)
            low_ref[part, :] = low
            grads_ref[part, :] = dot(low, out_ref[member]).astype(BF16)
        gain_grad_ref[...] = gain_grad
        dk[...] = jnp.zeros_like(dk)
        dv[...] = jnp.zeros_like(dv)
        strip[...] = jnp.zeros_like(strip)

    start = pl.multiple_of((length // rows - 1 - block) * rows, rows)
    here = pl.ds(pl.multiple_of(block * rows, rows), rows)
    queries, keys, values = qkv_ref[0, here, :], qkv_ref[1], qkv_ref[2]
    grads = grads_ref[here, :]
    for head in range(heads):
        lanes = head_lanes(lanes_all, head)
        part = pl.ds(head * rows, rows)
        own_grad = jnp.where(lanes, grads, jnp.zeros_like(grads))
        wide_ref[part, :] = own_grad
        query_ref[part, :] = jnp.where(lanes, queries, jnp.zeros_like(queries))
        da_ref[head] = dot(own_grad, values, (1, 1))
    step = 32
    dq = jnp.zeros((rows, lanes_all), F32)
    for head in range(heads):
        for at_row in range(0, rows, step):
            part = pl.ds(at_row, step)
            weights = a_ref[head, part, :].astype(F32)
            da = da_ref[head, part, :]
            ds = weights * (da - jnp.sum(weights * da, -1, keepdims=True))
            ds = ds.astype(BF16)
            ds_ref[pl.ds(head * rows + at_row, step), :] = ds
            strip[head, part, pl.ds(start, length)] += ds.astype(F32)
        own = dot(ds_ref[pl.ds(head * rows, rows), :], keys)
        dq = jnp.where(head_lanes(lanes_all, head), own, dq)
    dk[...] += dot(ds_ref[...], query_ref[...], (0, 0))
    dv[...] += dot(a_ref[...].reshape(heads * rows, length), wide_ref[...], (0, 0))
    dp_ref[0, here, :] = (dq * scaling).astype(BF16)

    @pl.when(block == length // rows - 1)
    def _():
        dp_ref[1] = (dk[...] * scaling).astype(BF16)
        dp_ref[2] = dv[...].astype(BF16)
        sub = lax.broadcasted_iota(jnp.int32, (8, span), 0)
        for head in range(heads):
            part = strip[head]
            size = rows // 2
            while size >= 8:
                part = part[:size] + pltpu.roll(part[size:], span - size, 1)
                size //= 2
            for bit in (4, 2, 1):
                part = jnp.where((sub & bit) != 0, pltpu.roll(part, span - bit, 1), part)
            diag_ref[head : head + 1, :] = jnp.sum(part, 0, keepdims=True)
        core = which_core()
        for side, ref in ((core, keep_ref), (1 - core, give_ref)):
            for at_row in range(0, length, 256):
                part = pl.ds(at_row, 256)
                total = jnp.zeros((256, half), F32)
                for v in range(3):
                    total += dot(dp_ref[v, part, :], w_ref[v, half_at(side, half), :], (1, 1))
                ref[part, :] = total.astype(BF16)


def attend_back(own, other, logits, router, middle, grad, gain, out, qkv, a, weights):
    length, width = middle.shape
    heads = a.shape[0]
    lanes = qkv.shape[2]
    half = width // 2
    span = 2 * length
    block = pl.BlockSpec((heads, BLOCK, length), lambda i: (0, i, 0))
    return call(
        functools.partial(attend_back_kernel, heads),
        [
            (value, None)
            for value in (own, other, logits, router, middle, grad, gain, out, qkv)
        ]
        + [(a, block), (weights, None)],
        [
            (shape_of(length, width, dtype=F32), None),
            (shape_of(length, width), None),
            (shape_of(1, width, dtype=F32), None),
            (shape_of(3, length, lanes), None),
            (shape_of(heads, span, dtype=F32), None),
            (shape_of(length, half), None),
            (shape_of(length, half), None),
        ],
        grid=(length // BLOCK,),
        scratch=[
            pltpu.VMEM((256, width), F32),
            pltpu.VMEM((length, lanes), BF16),
            pltpu.VMEM((length, lanes), F32),
            pltpu.VMEM((length, lanes), F32),
            pltpu.VMEM((heads, BLOCK, span), F32),
            pltpu.VMEM((heads, BLOCK, length), F32),
            pltpu.VMEM((heads * BLOCK, length), BF16),
            pltpu.VMEM((heads * BLOCK, lanes), BF16),
            pltpu.VMEM((heads * BLOCK, lanes), BF16),
        ],
        vmem=58,
        flops=LONG,
    )


def head_grads_kernel(normed_ref, dp_ref, low_ref, own_ref, out_ref):
    for v in range(3):
        out_ref[v] = dot(normed_ref[...], dp_ref[v], (0, 0)).astype(BF16)
    out_ref[3] = dot(low_ref[...], own_ref[...], (0, 0)).astype(BF16)


def head_weight_grads(normed, dp, low, own):
    length, width = normed.shape
    lanes = own.shape[1]
    return call(
        head_grads_kernel,
        [(value, None) for value in (normed, dp, low, own)],
        [(shape_of(4, width, lanes), None)],
        vmem=58,
    )[0]


def rows_back_kernel(own_ref, other_ref, x_ref, gain_ref, mid_ref, out_ref, gain_grad_ref, joined):
    rows, width = x_ref.shape
    half = width // 2
    core = which_core()

    @pl.when(pl.program_id(0) == 0)
    def _():
        gain_grad_ref[...] = jnp.zeros_like(gain_grad_ref)

    joined[:, half_at(core, half)] = own_ref[...].astype(F32)
    joined[:, half_at(1 - core, half)] = other_ref[...].astype(F32)
    grad = joined[...]
    values = x_ref[...].astype(F32)
    scale = row_scale(values)
    scaled = grad * gain_ref[...]
    mean = jnp.mean(scaled * values, -1, keepdims=True)
    change = scale * scaled - values * (scale * scale * scale) * mean
    out_ref[...] = (mid_ref[...] + change).astype(BF16)
    gain_grad_ref[...] += jnp.sum(grad * values * scale, 0, keepdims=True)


def rows_back(own, other, rows, gain, mid):
    length, width = rows.shape
    block = length // 4
    return call(
        rows_back_kernel,
        [
            (own, row_blocks(block, own.shape[1])),
            (other, row_blocks(block, own.shape[1])),
            (rows, row_blocks(block, width)),
            (gain, None),
            (mid, row_blocks(block, width)),
        ],
        [
            (shape_of(length, width), row_blocks(block, width)),
            (shape_of(1, width, dtype=F32), None),
        ],
        grid=(4,),
        scratch=[pltpu.VMEM((block, width), F32)],
    )


def query_weights(pieces, before_hosts=()):
    x, _, c, _ = place()

    def to(x, h, c, t):
        return (x, h, c, t ^ (x + 2 * c)) if x + 2 * c else None

    def across(x, h, c, t):
        return (x, h, 1 - c, t ^ (x + 2 * (1 - c)))

    own = jnp.where(x + 2 * c == 0, pieces, send(pieces, to))
    other = send(pieces, across)
    own, other = after((own, other), before_hosts)
    if lax.axis_size("dp") == 4:
        return [own, other, host_swap(own, 1), host_swap(other, 1)]
    both = ordered(c, own, other, 1)
    return [rows_over_hosts(both[:, None], 1).reshape(3, -1, pieces.shape[2])]


def out_weights(piece):
    _, _, c, _ = place()
    four = jnp.stack([piece] + [tensor_swap(piece, j) for j in (1, 2, 3)])
    four = rows_over_hosts(four[:, None], 1)
    four = ordered(c, four[:, :, None], core_swap(four)[:, :, None], 2)
    return four.reshape(4, -1, piece.shape[1])


def weights_out(i):
    def to(x, h, c, t):
        return (x, h, 1 - (t & 1), c + 2 * (i ^ (t >> 1) ^ c))

    return to


def weights_home(i):
    def to(x, h, c, t):
        return (x, h, t & 1, 2 * (i ^ (t >> 1) ^ (t & 1)) + 1 - c)

    return to


def pack(up, down):
    half = up.shape[0] // 2
    return jnp.concatenate([jnp.concatenate([up[:half], up[half:]], 1), down], 0)


def unpack_pair(packed):
    rows, half = packed.shape[0] // 2, packed.shape[1] // 2
    up = jnp.concatenate([packed[:rows, :half], packed[:rows, half:]], 0)
    return up, packed[rows:]


def expert_weights(packed):
    return [send(packed, weights_out(i)) for i in range(2)]


def for_own_layer(zero, one):
    x, _, _, _ = place()
    other = section_swap(jnp.where(x == 0, one, zero).astype(BF16))
    return jnp.where(x == 0, zero, one), other


def to_expert(buffers, experts):
    if len(buffers) == 1:
        pieces = buffers[0].reshape(experts, -1, buffers[0].shape[1])
        own = [expert_exchange(pieces).reshape(buffers[0].shape)]
    else:
        order = [len(buffers) - 1] + list(range(1, len(buffers) - 1))
        got = {j: expert_swap(buffers[j], j) for j in order}
        own = [buffers[0]] + [got[j] for j in range(1, len(buffers))]
    return own, [core_swap(part) for part in own]


def add(first, second):
    return first + second


def after(values, earlier):
    return lax.optimization_barrier((values, earlier))[0]


def from_expert(parts, slot_column, experts, at_sums=(), at_combine=()):
    if len(parts) == 2:
        keep, give = parts
        chip = add(keep, core_swap(give))
        pieces = add(chip, section_swap(chip)).reshape(experts, -1, chip.shape[1])
        whole = expert_exchange(pieces).reshape(chip.shape)
        rows = combine((whole, jnp.zeros_like(whole)), (), slot_column)
        return rows, core_swap(rows)
    split = experts // 2
    chips = [add(keep, core_swap(give)) for keep, give in (parts[:2], parts[2:])]
    back = {}
    for first, chip in ((split, chips[0]), (0, chips[1])):
        other = section_swap(chip)
        if not first:
            other = after(other, at_sums)
        count = chip.shape[0] // split
        for j in range(first + split - 1, first - 1, -1):
            piece = slice((j - first) * count, (j - first + 1) * count)
            if j == 0:
                local = (chip[piece], other[piece])
            else:
                back[j] = expert_swap(add(chip[piece], other[piece]), j)
    local = after(local, at_combine)
    rows = combine(local, [back[j] for j in range(1, experts)], slot_column)
    return rows, core_swap(rows)


def layer_forward(
    source, params, attention, packs, experts, slots, mix, at_own, at_middle, during
):
    gain_one, base, prefix, gain_two, router, chosen, slot, slot_column = params
    qkv_pieces, out_pieces = attention
    rows, normed, qkv, qkv_weights, own, weights = attend(
        source, mix, prefix, gain_one, qkv_pieces, base
    )
    own = after(own, at_own)
    other = section_swap(own)
    pieces = after((own, other, core_swap(own), core_swap(other)), at_middle)
    middle, normed_two, gate, buffers = middle_and_buffers(
        rows, pieces, out_pieces, gain_two, router, chosen, slot, experts, slots
    )
    arrived = to_expert(buffers, experts)
    at_sums, at_combine = during(arrived[0])
    active, slope, parts = expert_rows(*arrived, packs)
    produced = from_expert(parts, slot_column, experts, at_sums, at_combine)
    saved = (rows, normed, qkv, qkv_weights, own, weights, middle, normed_two, gate)
    return saved, (arrived, active, slope), produced


def layer_backward(
    layer, grad, forward, params, attention, packs, experts, slots, during, at_chip
):
    gain_one, base, prefix, gain_two, router, chosen, slot, slot_column = params
    out_pieces = attention[1]
    saved, (arrived, active, slope), produced = forward
    rows, normed, qkv, qkv_weights, own, weights, middle, normed_two, gate = saved
    last = layer == 1
    got, buffers = grads_and_buffers(
        middle, gate, *produced, grad, normed_two, router, chosen, slot, experts, slots, last
    )
    grad_logits = got[-1]
    grad_arrived = to_expert(buffers, experts)
    at_sums, at_combine = during(grad_arrived[0], got[0])
    hidden, parts = expert_rows_back(*grad_arrived, slope, packs)
    expert_grads = expert_weight_grads(*arrived, *grad_arrived, active, hidden)
    grad_normed_two = from_expert(
        parts, slot_column, experts, at_sums, (expert_grads, at_combine)
    )
    expert_grads = after(tuple(expert_grads), grad_normed_two[0])
    expert_grads = tuple(send(part, weights_home(i)) for i, part in enumerate(expert_grads))
    grad_router = dot(normed_two, grad_logits, (0, 0))[:, :experts]
    mid, low, grad_gain_two, dp, diagonal, keep, give = attend_back(
        *grad_normed_two,
        grad_logits,
        router,
        middle,
        grad,
        gain_two,
        out_pieces,
        qkv,
        weights,
        qkv_weights,
    )
    keep, give = after((keep, give), expert_grads[0])
    chip = add(keep, core_swap(give))
    head_grads = head_weight_grads(normed, dp, low, own)
    at_total = at_chip(grad_normed_two[0])
    total = add(chip, after(section_swap(chip), (head_grads, expert_grads[1], at_total)))
    grad_rows, grad_gain_one = rows_back(total, core_swap(total), rows, gain_one, mid)
    small = (grad_gain_one[0], grad_gain_two[0], grad_router, diagonal)
    return grad_rows, expert_grads, head_grads, small, total


def over_rows(grads, earlier=()):
    _, h, _, _ = place()
    hosts = lax.axis_size("dp") // 2
    parts = grads.reshape(4, hosts, 2, -1, grads.shape[2])
    parts = jnp.transpose(parts, (1, 2, 0, 3, 4))
    bit = hosts // 2
    while bit:
        pair = parts.reshape(2, bit, *parts.shape[1:])
        upper = (h & bit) != 0
        keep = jnp.where(upper, pair[1], pair[0])
        give = jnp.where(upper, pair[0], pair[1])
        parts = add(keep, after(host_swap(give, bit), earlier))
        bit //= 2
    return parts[0]


def to_quarter(part):
    x, _, c, _ = place()

    def to(x, h, c, t):
        return (x, h, c, t ^ (x + 2 * c)) if x + 2 * c else None

    return jnp.where(x + 2 * c == 0, part, send(part, to))


def over_cores(part):
    _, _, c, _ = place()
    keep = jnp.where(c == 0, part[0], part[1]).astype(F32)
    give = jnp.where(c == 0, part[1], part[0])
    return keep + core_swap(give).astype(F32)


def over_groups(values):
    one, two, three = (tensor_swap(values, j) for j in (1, 2, 3))
    values = (values + one) + (two + three)
    bit = 1
    while bit < lax.axis_size("dp") // 2:
        values = values + host_swap(values, bit)
        bit *= 2
    return values


def pick(flag, first, second):
    return jax.tree.map(lambda a, b: jnp.where(flag == 0, a, b), first, second)


def per_device(
    block_input,
    cotangent,
    query_key_value_weights,
    attention_output_weights,
    bias_table,
    norm_first,
    norm_second,
    router_projection_weights,
    expert_up,
    expert_down,
    routes,
    prefix_lengths,
    relative_buckets,
):
    x, h, c, t = place()
    _, piece, width = block_input.shape
    length = routes.shape[2]
    buckets, head_count = bias_table.shape[1:]
    experts = router_projection_weights.shape[2]
    heads = head_count // 4
    capacity = (5 * length + 4 * experts - 1) // (4 * experts)

    pieces = jnp.concatenate(
        [query_key_value_weights[0], attention_output_weights[0].T[None]], 0
    )
    other = section_swap(pieces)
    pieces = pick(x, (pieces, other), (other, pieces))
    scale = 32
    packed = jnp.concatenate(
        [
            routes[0, :, :, 0].reshape(-1),
            prefix_lengths // scale,
            prefix_lengths % scale,
        ]
    ).astype(BF16)
    both = ordered(c, packed[None], core_swap(packed)[None], 0)
    lower = at(both, t >> 1)
    route = lax.dynamic_slice_in_dim(lower, (t & 1) * length, length, 0)
    numbers = lower[2 * length :].astype(F32).astype(jnp.int32)
    prefix = lax.dynamic_slice_in_dim(numbers[:2] * scale + numbers[2:], t & 1, 1, 0)
    packed = jnp.concatenate(
        [
            route,
            norm_first[0],
            norm_second[0],
            router_projection_weights[0].reshape(-1),
            bias_table[0].reshape(-1),
        ]
    )
    other = section_swap(packed)
    packed = pick(x, (packed, other), (other, packed))

    half = expert_up.shape[3] // 2
    up, down = expert_up[0, 0], expert_down[0, 0]
    lower = pack(up[:, :half], down[:half])
    upper = pack(up[:, half:], down[half:])
    keep = jnp.where(x == 0, lower, upper)
    other = section_swap(after(jnp.where(x == 0, upper, lower), pieces))
    packs = pick(x, (keep, other), (other, keep))

    rows = to_groups(block_input)

    bucket_onehot = (
        relative_buckets[:, None] == jnp.arange(buckets, dtype=jnp.int32)[None, :]
    ).astype(BF16)
    earlier = (
        jnp.arange(length, dtype=jnp.int32)[None, :] < jnp.arange(length, dtype=jnp.int32)[:, None]
    ).astype(BF16)
    expert_ids = jnp.arange(experts, dtype=jnp.int32)

    def unpack(vector):
        route = vector[:length].astype(F32).astype(jnp.int32)
        at_one = length
        gain_one = vector[at_one : at_one + width].astype(F32)
        at_two = at_one + width
        gain_two = vector[at_two : at_two + width].astype(F32)
        at_router = at_two + width
        router = vector[at_router : at_router + width * experts].reshape(width, experts)
        table = vector[at_router + width * experts :].reshape(buckets, head_count)
        own = lax.dynamic_slice_in_dim(table, ((x + 2 * c) ^ t) * heads, heads, 1)
        rel = lax.dot_general(
            own, bucket_onehot, (((0,), (1,)), ((), ())), preferred_element_type=F32
        )
        base = jnp.roll(jnp.pad(rel, ((0, 0), (0, 1))), -(BLOCK - 1), axis=1)
        chosen = route[:, None] == expert_ids[None, :]
        rank = jnp.dot(earlier, chosen.astype(BF16), preferred_element_type=F32)
        rank = jnp.sum(jnp.where(chosen, rank, 0.0), 1).astype(jnp.int32)
        slot = (route ^ (2 * h + (t & 1))) * capacity + rank
        pad = ((0, 0), (0, 128 - experts))
        return (
            gain_one[None],
            base,
            prefix,
            gain_two[None],
            jnp.pad(router, pad),
            jnp.pad(chosen.astype(F32), pad),
            slot[None],
            slot[:, None],
        )

    params = [unpack(vector) for vector in packed]
    got = tuple(rows[:2])
    queries_zero = query_weights(pieces[0][:3], got)
    outs_zero = out_weights(after(pieces[0][3], pieces[0]))
    packs_zero = expert_weights(packs[0])
    slots = experts * capacity
    rows = after(tuple(rows), packs[0])
    later = {}

    def during_zero(arrived):
        arrived = tuple(arrived)
        later["queries"] = query_weights(after(pieces[1][:3], arrived))
        later["outs"] = out_weights(after(pieces[1][3], arrived))
        return tuple(later["queries"][:2]), ()

    zero = layer_forward(
        rows,
        params[0],
        (queries_zero, outs_zero),
        packs_zero,
        experts,
        slots,
        False,
        packs_zero[0],
        packs_zero[1],
        during_zero,
    )
    packs_one = expert_weights(after(packs[1], zero[2][0]))

    def during_one(arrived):
        later["top"] = to_groups(after(cotangent, tuple(arrived)))
        return tuple(later["top"]), ()

    one = layer_forward(
        (zero[0][6], zero[0][8], *zero[2]),
        params[1],
        (later["queries"], later["outs"]),
        packs_one,
        experts,
        slots,
        True,
        packs_one[0],
        packs_one[1],
        during_one,
    )
    top = whole_rows(later["top"])

    def during_back_one(arrived, result):
        outputs = after(jnp.where(x == 0, one[0][0], result), tuple(arrived))
        later["outputs"] = from_groups(outputs)
        return later["outputs"], ()

    grads_one = layer_backward(
        1,
        top,
        one,
        params[1],
        (None, later["outs"]),
        packs_one,
        experts,
        slots,
        during_back_one,
        lambda returned: (),
    )

    def during_back_zero(arrived, _):
        later["heads"] = over_rows(after(grads_one[2], tuple(arrived)))
        return later["heads"], ()

    def at_total_zero(returned):
        later["heads"] = to_quarter(after(later["heads"], returned))
        return later["heads"]

    grads_zero = layer_backward(
        0,
        grads_one[0],
        zero,
        params[0],
        (None, outs_zero),
        packs_zero,
        experts,
        slots,
        during_back_zero,
        at_total_zero,
    )
    outputs = later["outputs"]

    def summed(pair):
        return pair[0].astype(F32) + pair[1].astype(F32)

    expert_zero = summed(after(grads_zero[1], grads_zero[4]))
    own, other = for_own_layer(expert_zero, summed(grads_one[1]))
    expert_own, expert_other = unpack_pair(own), unpack_pair(other.astype(F32))
    heads_zero = over_cores(to_quarter(over_rows(grads_zero[2], grads_zero[4])))
    own, other = for_own_layer(heads_zero, over_cores(later["heads"]))
    heads_grad = own + other.astype(F32)
    grad_rows = from_groups(jnp.where(x == 0, grads_zero[0], grads_one[0]))

    def flat(small):
        gain_one, gain_two, router, diagonal = small
        total = jnp.roll(diagonal, BLOCK - 1, axis=1)[:, : 2 * length - 1]
        table = lax.dot_general(
            bucket_onehot.astype(F32),
            total,
            (((0,), (1,)), ((), ())),
            precision=lax.Precision.HIGHEST,
        )
        whole = lax.dynamic_update_slice_in_dim(
            jnp.zeros((buckets, head_count), F32), table, ((x + 2 * c) ^ t) * heads, 1
        )
        return jnp.concatenate([gain_one, gain_two, router.reshape(-1), whole.reshape(-1)])

    everything = over_groups(jnp.stack([flat(grads_zero[3]), flat(grads_one[3])]))
    core = core_swap(everything)
    size = everything.shape[1] - buckets * head_count
    tables = everything[:, size:] + core[:, size:]
    tables = tables + section_swap(tables)
    shared = at(jnp.where(c == 0, everything, core), x)

    grad_up = ordered(x, expert_own[0], expert_other[0], 1)
    grad_down = ordered(x, expert_own[1], expert_other[1], 0)
    grad_in = heads_grad[:3]
    grad_out = heads_grad[3].T

    return (
        outputs[None],
        grad_rows[None],
        grad_in[None],
        grad_out[None],
        at(tables, x).reshape(1, buckets, head_count),
        shared[:width][None],
        shared[width : 2 * width][None],
        shared[2 * width : size].reshape(1, width, experts),
        grad_up[None, None],
        grad_down[None, None],
    )


def solution(mesh):
    in_specs = (
        P("dp", "tensor", None),
        P("dp", "tensor", None),
        P("section", None, "dp", "tensor"),
        P("section", "tensor", "dp"),
        P("section", None, None),
        P("section", None),
        P("section", None),
        P("section", None, None),
        P("section", "dp", None, "tensor"),
        P("section", "dp", "tensor", None),
        P("section", "dp", None, None),
        P("dp"),
        P(),
    )
    out_specs = (
        P("section", "dp", "tensor", None),
        P("section", "dp", "tensor", None),
        P("section", None, "dp", "tensor"),
        P("section", "tensor", "dp"),
        P("section", None, None),
        P("section", None),
        P("section", None),
        P("section", None, None),
        P("section", "dp", None, "tensor"),
        P("section", "dp", "tensor", None),
    )
    return jax.shard_map(
        per_device, mesh=mesh, in_specs=in_specs, out_specs=out_specs, check_vma=False
    )
```

```python
import functools

import jax
import jax.numpy as jnp
from jax import lax
from jax.experimental import pallas as pl
from jax.experimental.pallas import tpu as pltpu
from jax.sharding import PartitionSpec as P

HEAD_DIM = 64
EPSILON = 1e-06
MASKED = -1000000000.0
AXES = ("section", "dp", "tensor")
BLOCK = 128
DIRECT = 8
LONG = 10**11
BF16 = jnp.bfloat16
F32 = jnp.float32


def send(value, to):
    sections, width, depth = (lax.axis_size(name) for name in AXES)

    def number(x, h, c, t):
        return (x * width + 2 * h + c) * depth + t

    pairs = []
    for x in range(sections):
        for d in range(width):
            for t in range(depth):
                target = to(x, d // 2, d % 2, t)
                if target is not None:
                    pairs.append((number(x, d // 2, d % 2, t), number(*target)))
    return lax.ppermute(value, AXES, pairs)


def core_swap(value):
    return send(value, lambda x, h, c, t: (x, h, 1 - c, t))


def section_swap(value):
    return send(value, lambda x, h, c, t: (1 - x, h, c, t))


def tensor_swap(value, j):
    return send(value, lambda x, h, c, t: (x, h, c, t ^ j))


def host_swap(value, j):
    return send(value, lambda x, h, c, t: (x, h ^ j, c, t))


def expert_swap(value, j):
    def to(x, h, c, t):
        e = (2 * h + (t & 1)) ^ j
        return (x, e >> 1, c, (t & 2) | (e & 1))

    return send(value, to)


def expert_exchange(values):
    count, bit = values.shape[0], 1
    while bit < count:
        parts = values.reshape(count // (2 * bit), 2, bit, *values.shape[1:])
        other = expert_swap(parts[:, 1], bit)
        values = jnp.stack([parts[:, 0], other], 1).reshape(values.shape)
        bit *= 2
    return values


def place():
    d = lax.axis_index("dp")
    return lax.axis_index("section"), d // 2, d % 2, lax.axis_index("tensor")


def ordered(flag, own, other, axis):
    first = jnp.where(flag == 0, own, other)
    second = jnp.where(flag == 0, other, own)
    return jnp.concatenate([first, second], axis)


def at(values, index):
    return lax.dynamic_index_in_dim(values, index, 0, keepdims=False)


def rows_over_hosts(value, axis):
    _, h, _, _ = place()
    bit = 1
    while bit < lax.axis_size("dp") // 2:
        other = host_swap(value, bit)
        value = ordered((h // bit) % 2, value, other, axis)
        bit *= 2
    return value


def to_groups(rows):
    _, _, _, t = place()
    got = []
    for i in range(2):

        def to(x, h, c, t, i=i):
            return (x, h, 1 - (t >> 1), 2 * c + (i ^ (t & 1)))

        got.append(send(at(rows, i ^ (t & 1)), to))
    return got + [core_swap(part) for part in got]


def piece_order():
    c, low = which_core(), lax.axis_index("tensor") & 1
    return [2 * (1 - c) + low, 2 * (1 - c) + (1 - low), 2 * c + low, 2 * c + (1 - low)]


def whole_rows(pieces):
    order = piece_order()
    return jnp.concatenate([at_place(pieces, order, place) for place in range(4)], 0)


def at_place(pieces, order, place):
    value = pieces[3]
    for piece, number in zip(pieces[:3], order[:3]):
        value = jnp.where(number == place, piece, value)
    return value


def from_groups(rows):
    _, _, c, t = place()
    length, width = rows.shape
    pieces = rows.reshape(4, length // 4, width)
    got = []
    for i in range(2):

        def to(x, h, c, t, i=i):
            return (x, h, t >> 1, 2 * (1 - c) + (i ^ (t & 1)))

        got.append(send(at(pieces, 2 * (1 - c) + (i ^ (t & 1))), to))

    def finish():
        low = t & 1
        first, second = jnp.where(low == 0, got[0], got[1]), jnp.where(low == 0, got[1], got[0])
        return jnp.stack([first, second])

    return tuple(got), finish


def head_lanes(width, head):
    lane = lax.broadcasted_iota(jnp.int32, (1, width), 1)
    return (lane // HEAD_DIM) == head


def dot(a, b, contract=(1, 0)):
    dims = (((contract[0],), (contract[1],)), ((), ()))
    return lax.dot_general(a, b, dims, preferred_element_type=F32)


def which_core():
    return lax.rem(lax.axis_index("dp"), 2)


def which_member():
    return lax.axis_index("section") + 2 * which_core()


def half_at(index, half):
    return pl.ds(pl.multiple_of(index * half, half), half)


def row_scale(values):
    return lax.rsqrt(jnp.mean(values * values, -1, keepdims=True) + EPSILON)


def call(kernel, inputs, outputs, grid=(1,), scratch=(), vmem=24, flops=10**9):
    def spec(item):
        value, given = item
        if given is not None:
            return given
        return pl.BlockSpec(value.shape, lambda i, n=len(value.shape): (0,) * n)

    return pl.pallas_call(
        kernel,
        grid=grid,
        in_specs=[spec(item) for item in inputs],
        out_specs=[spec(item) for item in outputs],
        out_shape=[item[0] for item in outputs],
        scratch_shapes=list(scratch),
        cost_estimate=pl.CostEstimate(flops=flops, bytes_accessed=1000, transcendentals=0),
        compiler_params=pltpu.CompilerParams(vmem_limit_bytes=vmem * 2**20),
    )(*[item[0] for item in inputs])


def shape_of(*dims, dtype=BF16):
    return jax.ShapeDtypeStruct(dims, dtype)


SMEM = pl.BlockSpec(memory_space=pltpu.SMEM)


def attend_kernel(heads, mix, orders, *refs):
    if mix:
        middle_ref, gate_ref, own_ref, other_ref, *refs = refs
    else:
        row_refs, refs = refs[:4], refs[4:]
    part_refs, refs = refs[: len(orders)], refs[len(orders) :]
    prefix_ref, gain_ref, base_ref, x_ref, normed_ref, qkv_ref, w_ref, *refs = refs
    o_ref, a_ref, strip, causal, scores_ref = refs
    block = pl.program_id(0)
    length, width = x_ref.shape
    rows = a_ref.shape[1]
    span = base_ref.shape[1]
    lanes_all = o_ref.shape[1] // 2

    @pl.when(block == 0)
    def _():
        step = 256
        for ref, order in zip(part_refs, orders):
            count = ref.shape[0]
            first = 0
            if order is not None:
                first = pl.multiple_of((lax.axis_index("dp") ^ order) * count, 8)
            for v in range(3):
                w_ref[v, pl.ds(first, count), :] = ref[:, v * lanes_all : (v + 1) * lanes_all]
        if not mix:
            for ref, piece in zip(row_refs, piece_order()):
                count = ref.shape[0]
                x_ref[pl.ds(pl.multiple_of(piece * count, count), count), :] = ref[...]
        for at_row in range(0, length, step):
            part = pl.ds(at_row, step)
            if mix:
                half = width // 2
                core = which_core()
                for ref, side in ((own_ref, core), (other_ref, 1 - core)):
                    lanes = half_at(side, half)
                    value = middle_ref[part, lanes] + gate_ref[part, :] * ref[part, :].astype(F32)
                    x_ref[part, lanes] = value.astype(BF16)
            values = x_ref[part, :].astype(F32)
            normed = (values * row_scale(values) * gain_ref[...]).astype(BF16)
            normed_ref[part, :] = normed
            for v in range(3):
                qkv_ref[v, part, :] = dot(normed, w_ref[v]).astype(BF16)
        sub = lax.broadcasted_iota(jnp.int32, (8, span), 0)
        for head in range(heads):
            part = jnp.broadcast_to(base_ref[head : head + 1, :], (8, span))
            for bit in (1, 2, 4):
                part = jnp.where((sub & bit) != 0, pltpu.roll(part, bit, 1), part)
            size = 8
            while size < rows:
                part = jnp.concatenate([part, pltpu.roll(part, size, 1)], 0)
                size *= 2
            strip[head] = part
            ahead = lax.broadcasted_iota(jnp.int32, (rows, span), 1) - lax.broadcasted_iota(
                jnp.int32, (rows, span), 0
            )
            causal[head] = jnp.where(ahead > length - rows, MASKED, part)

    start = pl.multiple_of((length // rows - 1 - block) * rows, rows)
    here = pl.ds(pl.multiple_of(block * rows, rows), rows)
    col = lax.broadcasted_iota(jnp.int32, (1, length), 1)
    inside = col < prefix_ref[0]
    queries, keys, values = qkv_ref[0, here, :], qkv_ref[1], qkv_ref[2]
    queries = queries * jnp.asarray(HEAD_DIM ** (-0.5), BF16)
    step = 32
    for head in range(heads):
        own = jnp.where(head_lanes(lanes_all, head), queries, jnp.zeros_like(queries))
        scores_ref[head] = dot(own, keys, (1, 1))
    out = jnp.zeros((rows, lanes_all), F32)
    for head in range(heads):
        for at_row in range(0, rows, step):
            part = pl.ds(at_row, step)
            across = pl.ds(start, length)
            bias = jnp.where(inside, strip[head, part, across], causal[head, part, across])
            scores = scores_ref[head, part, :] + bias
            weights = jnp.exp(scores - jnp.max(scores, -1, keepdims=True))
            weights = weights * (1.0 / jnp.sum(weights, -1, keepdims=True))
            a_ref[head, part, :] = weights.astype(BF16)
        out = jnp.where(head_lanes(lanes_all, head), dot(a_ref[head], values), out)
    blocks = length // rows
    place = pl.ds(pl.multiple_of(lax.rem(block, blocks // 2) * rows, rows), rows)

    @pl.when(block < blocks // 2)
    def _():
        o_ref[place, :lanes_all] = out.astype(BF16)

    @pl.when(block >= blocks // 2)
    def _():
        o_ref[place, lanes_all:] = out.astype(BF16)


def attend(source, mix, prefix, gain, weights, base):
    weights, orders = weights
    width = gain.shape[1]
    length = source[0].shape[0] * (1 if mix else 4)
    lanes = weights[0].shape[1] // 3
    heads = lanes // HEAD_DIM
    span = base.shape[1]
    inputs = [(part, None) for part in (*source, *weights)]
    inputs += [(prefix, SMEM), (gain, None), (base, None)]
    return call(
        functools.partial(attend_kernel, heads, mix, orders),
        inputs,
        [
            (shape_of(length, width), None),
            (shape_of(length, width), None),
            (shape_of(3, length, lanes), None),
            (shape_of(3, width, lanes), None),
            (shape_of(length // 2, 2 * lanes), None),
            (
                shape_of(heads, length, length),
                pl.BlockSpec((heads, BLOCK, length), lambda i: (0, i, 0)),
            ),
        ],
        grid=(length // BLOCK,),
        scratch=[
            pltpu.VMEM((heads, BLOCK, span), F32),
            pltpu.VMEM((heads, BLOCK, span), F32),
            pltpu.VMEM((heads, BLOCK, length), F32),
        ],
        vmem=58,
        flops=LONG,
    )


def pieces_of(experts):
    return experts if experts <= DIRECT else 1


def selection_block(slot_ref, first, count):
    ids = first + lax.broadcasted_iota(jnp.int32, (count, slot_ref.shape[1]), 0)
    return jnp.where(ids == slot_ref[...], 1.0, 0.0).astype(BF16)


def dispatch_blocks(step, steps, slot_ref, rows_ref, buffer_refs):
    half = rows_ref.shape[1] // 2
    total = sum(ref.shape[0] for ref in buffer_refs) if len(buffer_refs) > 1 else None
    lanes = half_at(which_core(), half)
    if total is None:

        @pl.when(step >= steps)
        def _():
            count = buffer_refs[0].shape[0]
            chosen = selection_block(slot_ref, (step - steps) * count, count)
            buffer_refs[0][...] = dot(chosen, rows_ref[:, lanes]).astype(BF16)

        return
    first = 0
    for index, ref in enumerate(buffer_refs):

        @pl.when(step == steps + index)
        def _(ref=ref, first=first):
            chosen = selection_block(slot_ref, first, ref.shape[0])
            ref[...] = dot(chosen, rows_ref[:, lanes]).astype(BF16)

        first += ref.shape[0]


def buffer_outputs(experts, rows, half, steps):
    count = pieces_of(experts)
    if count > 1:
        return [(shape_of(rows // count, half), None)] * count, steps + count
    blocks = 4
    spec = pl.BlockSpec((rows // blocks, half), lambda i: (jnp.maximum(i - steps, 0), 0))
    return [(shape_of(rows, half), spec)], steps + blocks


def router_probs(normed, router_ref, experts):
    logits = dot(normed, router_ref[...])
    real = lax.broadcasted_iota(jnp.int32, logits.shape, 1) < experts
    logits = jnp.where(real, logits, MASKED)
    weights = jnp.exp(logits - jnp.max(logits, -1, keepdims=True))
    weights = jnp.where(real, weights, 0.0)
    return weights / jnp.sum(weights, -1, keepdims=True)


def middle_kernel(experts, steps, *refs):
    x_ref, *refs = refs
    piece_refs, refs = refs[:4], refs[4:]
    w_ref, gain_ref, router_ref, chosen_ref, slot_ref, middle_ref, normed_ref, gate_ref = refs[:8]
    buffer_refs, kept = refs[8:-1], refs[-1]
    step = pl.program_id(0)
    rows = x_ref.shape[0]

    def mix(side):
        member = which_member()
        half = piece_refs[0].shape[1] // 2
        first = pl.multiple_of(lax.rem(step, steps // 2) * rows, rows)
        lanes = slice(side * half, (side + 1) * half)
        parts = [
            dot(ref[pl.ds(first, rows), lanes], w_ref[member ^ j], (1, 1))
            for j, ref in enumerate(piece_refs)
        ]
        values = x_ref[...].astype(F32) + ((parts[0] + parts[1]) + (parts[2] + parts[3]))
        middle_ref[...] = values
        normed = (values * row_scale(values) * gain_ref[...]).astype(BF16)
        normed_ref[...] = normed
        kept[pl.ds(pl.multiple_of(step * rows, rows), rows), :] = normed
        probs = router_probs(normed, router_ref, experts)
        gate_ref[...] = jnp.sum(probs * chosen_ref[...], -1, keepdims=True)

    @pl.when(step < steps // 2)
    def _():
        mix(0)

    @pl.when((step >= steps // 2) & (step < steps))
    def _():
        mix(1)

    dispatch_blocks(step, steps, slot_ref, kept, buffer_refs)


def middle_and_buffers(rows, pieces, weights, gain, router, chosen, slot, experts, slots):
    length, width = rows.shape
    steps = 4
    block = length // steps

    def by_rows(lanes):
        return pl.BlockSpec((block, lanes), lambda i: (jnp.minimum(i, steps - 1), 0))

    buffers, grid = buffer_outputs(experts, slots, width // 2, steps)
    got = call(
        functools.partial(middle_kernel, experts, steps),
        [(rows, by_rows(width))]
        + [(piece, None) for piece in pieces]
        + [
            (weights, None),
            (gain, None),
            (router, None),
            (chosen, by_rows(chosen.shape[1])),
            (slot, None),
        ],
        [
            (shape_of(length, width, dtype=F32), by_rows(width)),
            (shape_of(length, width), by_rows(width)),
            (shape_of(length, 1, dtype=F32), by_rows(1)),
        ]
        + buffers,
        grid=(grid,),
        scratch=[pltpu.VMEM((length, width), BF16)],
    )
    return got[0], got[1], got[2], got[3:]


def order_of(index, count):
    return (index + count // 2) % count


def parts_of(refs, index, count):
    return refs[:2] if index >= count // 2 or count == 1 else refs[2:]


def part_outputs(rows, half, count):
    if count == 1:
        return [(shape_of(rows, half), None)] * 2
    split = count // 2
    shape = shape_of(rows * split, half)
    upper = pl.BlockSpec((rows, half), lambda i: (jnp.minimum(i, split - 1), 0))
    lower = pl.BlockSpec((rows, half), lambda i: (jnp.maximum(i - split, 0), 0))
    return [(shape, upper)] * 2 + [(shape, lower)] * 2


def ordered_blocks(rows, lanes, count):
    return pl.BlockSpec((rows, lanes), lambda i: ((i + count // 2) % count, 0))


GELU = 0.7978845608028654


def expert_kernel(count, *refs):
    own_refs, other_refs, refs = refs[:count], refs[count : 2 * count], refs[2 * count :]
    *pack_refs, active_ref, slope_ref = refs[:4]
    part_refs = refs[4:]
    half = own_refs[0].shape[1]
    upper, lower = pl.ds(0, half), pl.ds(half, half)
    core = which_core()
    step = pl.program_id(0)
    for index in range(count):
        keep_ref, give_ref = parts_of(part_refs, index, count)

        @pl.when(step == order_of(index, count))
        def _(index=index, keep_ref=keep_ref, give_ref=give_ref):
            mine, others = half_at(core, half), half_at(1 - core, half)
            own, other = own_refs[index][...], other_refs[index][...]
            keep = give = None
            for i, ref in enumerate(pack_refs):
                hidden = dot(own, ref[upper, mine]) + dot(other, ref[upper, others])
                square = hidden * hidden
                inner = jnp.tanh(GELU * hidden * (1.0 + 0.044715 * square))
                active = (0.5 * hidden * (1.0 + inner)).astype(BF16)
                slope = 0.5 * (1.0 + inner) + 0.5 * hidden * (1.0 - inner * inner) * (
                    GELU * (1.0 + 3 * 0.044715 * square)
                )
                active_ref[:, pl.ds(i * half, half)] = active
                slope_ref[:, pl.ds(i * half, half)] = slope.astype(BF16)
                first, second = dot(active, ref[lower, mine]), dot(active, ref[lower, others])
                keep = first if keep is None else keep + first
                give = second if give is None else give + second
            keep_ref[...] = keep.astype(BF16)
            give_ref[...] = give.astype(BF16)


def row_blocks(rows, lanes):
    return pl.BlockSpec((rows, lanes), lambda i: (i, 0))


def expert_rows(own, other, packs):
    count = len(own)
    rows, half = own[0].shape
    hidden = packs[0].shape[1]
    wide = (shape_of(rows * count, hidden), ordered_blocks(rows, hidden, count))
    got = call(
        functools.partial(expert_kernel, count),
        [(part, None) for part in own + other + packs],
        [wide, wide] + part_outputs(rows, half, count),
        grid=(count,),
    )
    return got[0], got[1], got[2:]


def expert_back_kernel(count, *refs):
    own_refs, other_refs, refs = refs[:count], refs[count : 2 * count], refs[2 * count :]
    slope_ref, *pack_refs, hidden_ref = refs[:4]
    part_refs = refs[4:]
    half = own_refs[0].shape[1]
    upper, lower = pl.ds(0, half), pl.ds(half, half)
    core = which_core()
    step = pl.program_id(0)
    for index in range(count):
        keep_ref, give_ref = parts_of(part_refs, index, count)

        @pl.when(step == order_of(index, count))
        def _(index=index, keep_ref=keep_ref, give_ref=give_ref):
            mine, others = half_at(core, half), half_at(1 - core, half)
            own, other = own_refs[index][...], other_refs[index][...]
            keep = give = None
            for i, ref in enumerate(pack_refs):
                lanes = pl.ds(i * half, half)
                grad = dot(own, ref[lower, mine], (1, 1)) + dot(other, ref[lower, others], (1, 1))
                grad = (grad * slope_ref[:, lanes].astype(F32)).astype(BF16)
                hidden_ref[:, lanes] = grad
                first = dot(grad, ref[upper, mine], (1, 1))
                second = dot(grad, ref[upper, others], (1, 1))
                keep = first if keep is None else keep + first
                give = second if give is None else give + second
            keep_ref[...] = keep.astype(BF16)
            give_ref[...] = give.astype(BF16)


def expert_rows_back(own, other, slope, packs):
    count = len(own)
    rows, half = own[0].shape
    hidden = packs[0].shape[1]
    blocks = ordered_blocks(rows, hidden, count)
    got = call(
        functools.partial(expert_back_kernel, count),
        [(part, None) for part in own + other]
        + [(slope, blocks)]
        + [(part, None) for part in packs],
        [(shape_of(rows * count, hidden), blocks)] + part_outputs(rows, half, count),
        grid=(count,),
    )
    return got[0], got[1:]


def expert_grads_kernel(count, *refs):
    own_refs, other_refs, refs = refs[:count], refs[count : 2 * count], refs[2 * count :]
    own_grads, other_grads, refs = refs[:count], refs[count : 2 * count], refs[2 * count :]
    active_ref, hidden_ref, first_ref, second_ref, inputs, grads = refs
    rows, half = own_refs[0].shape
    core = which_core()
    for sources, gradients, side in (
        (own_refs, own_grads, core),
        (other_refs, other_grads, 1 - core),
    ):
        lanes = half_at(side, half)
        for index in range(count):
            part = pl.ds(index * rows, rows)
            inputs[part, :] = sources[index][...]
            grads[part, :] = gradients[index][...]
        for out, ref in enumerate((first_ref, second_ref)):
            own_half = pl.ds(out * half, half)
            up = dot(inputs[...], hidden_ref[:, own_half], (0, 0))
            ref[pl.ds(0, half), lanes] = up.astype(BF16)
            down = dot(active_ref[:, own_half], grads[...], (0, 0))
            ref[pl.ds(half, half), lanes] = down.astype(BF16)


def expert_weight_grads(own, other, own_grads, other_grads, active, hidden):
    count = len(own)
    rows, half = own[0].shape
    return call(
        functools.partial(expert_grads_kernel, count),
        [(part, None) for part in own + other + own_grads + other_grads]
        + [(active, None), (hidden, None)],
        [(shape_of(2 * half, 2 * half), None)] * 2,
        scratch=[pltpu.VMEM((rows * count, half), BF16)] * 2,
        vmem=58,
    )


def combine_kernel(count, *refs):
    refs, slot_ref, out_ref = refs[:-2], refs[-2], refs[-1]
    block = out_ref.shape[0]
    total = jnp.zeros(out_ref.shape, F32)
    first = 0
    for index in range(count):
        if index == 0:
            value = (refs[0][...].astype(F32) + refs[1][...].astype(F32)).astype(BF16)
        else:
            value = refs[index + 1][...]
        ids = first + lax.broadcasted_iota(jnp.int32, (block, value.shape[0]), 1)
        chosen = jnp.where(ids == slot_ref[...], 1.0, 0.0).astype(BF16)
        total += dot(chosen, value)
        first += value.shape[0]
    out_ref[...] = total.astype(BF16)


def combine(first, rest, slot_column):
    length = slot_column.shape[0]
    half = first[0].shape[1]
    block = length // 4
    return call(
        functools.partial(combine_kernel, 1 + len(rest)),
        [(part, None) for part in first]
        + [(part, None) for part in rest]
        + [(slot_column, row_blocks(block, 1))],
        [(shape_of(length, half), row_blocks(block, half))],
        grid=(4,),
    )[0]


def grad_kernel(experts, steps, last, *refs):
    middle_ref, gate_ref, own_ref, other_ref, grad_ref, normed_ref, router_ref = refs[:7]
    chosen_ref, slot_ref, refs = refs[7], refs[8], refs[9:]
    if last:
        result_ref, *refs = refs
    logits_ref, refs = refs[0], refs[1:]
    buffer_refs, kept, joined = refs[:-2], refs[-2], refs[-1]
    step = pl.program_id(0)
    rows, width = middle_ref.shape

    @pl.when(step < steps)
    def _():
        half = width // 2
        core = which_core()
        joined[:, half_at(core, half)] = own_ref[...].astype(F32)
        joined[:, half_at(1 - core, half)] = other_ref[...].astype(F32)
        produced = joined[...]
        gate = gate_ref[...]
        if last:
            result_ref[...] = (middle_ref[...] + gate * produced).astype(BF16)
        grad = grad_ref[...].astype(F32)
        kept[pl.ds(pl.multiple_of(step * rows, rows), rows), :] = (gate * grad).astype(BF16)
        grad_gate = jnp.sum(grad * produced, -1, keepdims=True)
        probs = router_probs(normed_ref[...], router_ref, experts)
        grad_probs = chosen_ref[...] * grad_gate
        inner = jnp.sum(probs * grad_probs, -1, keepdims=True)
        logits_ref[...] = (probs * (grad_probs - inner)).astype(BF16)

    dispatch_blocks(step, steps, slot_ref, kept, buffer_refs)


def grads_and_buffers(
    middle, gate, own, other, grad, normed, router, chosen, slot, experts, slots, last
):
    length, width = middle.shape
    steps = 4
    block = length // steps

    def by_rows(value):
        lanes = value.shape[1]
        return (value, pl.BlockSpec((block, lanes), lambda i: (jnp.minimum(i, steps - 1), 0)))

    buffers, grid = buffer_outputs(experts, slots, width // 2, steps)
    outputs = [by_rows(shape_of(length, width))] if last else []
    outputs += [by_rows(shape_of(length, chosen.shape[1]))]
    got = call(
        functools.partial(grad_kernel, experts, steps, last),
        [by_rows(value) for value in (middle, gate, own, other, grad, normed)]
        + [(router, None), by_rows(chosen), (slot, None)],
        outputs + buffers,
        grid=(grid,),
        scratch=[pltpu.VMEM((length, width), BF16), pltpu.VMEM((block, width), F32)],
    )
    return got[: len(outputs)], got[len(outputs) :]


def attend_back_kernel(heads, *refs):
    own_ref, other_ref, logits_ref, router_ref, middle_ref, grad_ref, gain_ref = refs[:7]
    out_ref, qkv_ref, a_ref, w_ref, refs = refs[7], refs[8], refs[9], refs[10], refs[11:]
    mid_ref, low_ref, gain_grad_ref, dp_ref, diag_ref, keep_ref, give_ref = refs[:7]
    joined, grads_ref, dk, dv, strip, da_ref, ds_ref, query_ref, wide_ref = refs[7:]
    block = pl.program_id(0)
    length, width = middle_ref.shape
    rows = a_ref.shape[1]
    lanes_all = qkv_ref.shape[2]
    span = strip.shape[2]
    half = width // 2
    scaling = HEAD_DIM ** (-0.5)

    @pl.when(block == 0)
    def _():
        core = which_core()
        member = which_member()
        gain = gain_ref[...]
        gain_grad = jnp.zeros((1, width), F32)
        step = joined.shape[0]
        for at_row in range(0, length, step):
            part = pl.ds(at_row, step)
            joined[:, half_at(core, half)] = own_ref[part, :].astype(F32)
            joined[:, half_at(1 - core, half)] = other_ref[part, :].astype(F32)
            grad_normed = joined[...] + dot(logits_ref[part, :], router_ref[...], (1, 1))
            middle = middle_ref[part, :]
            scale = row_scale(middle)
            scaled = grad_normed * gain
            mean = jnp.mean(scaled * middle, -1, keepdims=True)
            grad = grad_ref[part, :].astype(F32) + (
                scale * scaled - middle * (scale * scale * scale) * mean
            )
            gain_grad += jnp.sum(grad_normed * middle * scale, 0, keepdims=True)
            mid_ref[part, :] = grad
            low = grad.astype(BF16)
            low_ref[part, :] = low
            grads_ref[part, :] = dot(low, out_ref[member]).astype(BF16)
        gain_grad_ref[...] = gain_grad
        dk[...] = jnp.zeros_like(dk)
        dv[...] = jnp.zeros_like(dv)
        strip[...] = jnp.zeros_like(strip)

    start = pl.multiple_of((length // rows - 1 - block) * rows, rows)
    here = pl.ds(pl.multiple_of(block * rows, rows), rows)
    queries, keys, values = qkv_ref[0, here, :], qkv_ref[1], qkv_ref[2]
    grads = grads_ref[here, :]
    for head in range(heads):
        lanes = head_lanes(lanes_all, head)
        part = pl.ds(head * rows, rows)
        own_grad = jnp.where(lanes, grads, jnp.zeros_like(grads))
        wide_ref[part, :] = own_grad
        query_ref[part, :] = jnp.where(lanes, queries, jnp.zeros_like(queries))
        da_ref[head] = dot(own_grad, values, (1, 1))
    step = 32
    dq = jnp.zeros((rows, lanes_all), F32)
    for head in range(heads):
        for at_row in range(0, rows, step):
            part = pl.ds(at_row, step)
            weights = a_ref[head, part, :].astype(F32)
            da = da_ref[head, part, :]
            ds = weights * (da - jnp.sum(weights * da, -1, keepdims=True))
            ds = ds.astype(BF16)
            ds_ref[pl.ds(head * rows + at_row, step), :] = ds
            strip[head, part, pl.ds(start, length)] += ds.astype(F32)
        own = dot(ds_ref[pl.ds(head * rows, rows), :], keys)
        dq = jnp.where(head_lanes(lanes_all, head), own, dq)
    dk[...] += dot(ds_ref[...], query_ref[...], (0, 0))
    dv[...] += dot(a_ref[...].reshape(heads * rows, length), wide_ref[...], (0, 0))
    dp_ref[0, here, :] = (dq * scaling).astype(BF16)

    @pl.when(block == length // rows - 1)
    def _():
        dp_ref[1] = (dk[...] * scaling).astype(BF16)
        dp_ref[2] = dv[...].astype(BF16)
        sub = lax.broadcasted_iota(jnp.int32, (8, span), 0)
        for head in range(heads):
            part = strip[head]
            size = rows // 2
            while size >= 8:
                part = part[:size] + pltpu.roll(part[size:], span - size, 1)
                size //= 2
            for bit in (4, 2, 1):
                part = jnp.where((sub & bit) != 0, pltpu.roll(part, span - bit, 1), part)
            diag_ref[head : head + 1, :] = jnp.sum(part, 0, keepdims=True)
        core = which_core()
        for side, ref in ((core, keep_ref), (1 - core, give_ref)):
            for at_row in range(0, length, 256):
                part = pl.ds(at_row, 256)
                total = jnp.zeros((256, half), F32)
                for v in range(3):
                    total += dot(dp_ref[v, part, :], w_ref[v, half_at(side, half), :], (1, 1))
                ref[part, :] = total.astype(BF16)


def attend_back(own, other, logits, router, middle, grad, gain, out, qkv, a, weights):
    length, width = middle.shape
    heads = a.shape[0]
    lanes = qkv.shape[2]
    half = width // 2
    span = 2 * length
    block = pl.BlockSpec((heads, BLOCK, length), lambda i: (0, i, 0))
    return call(
        functools.partial(attend_back_kernel, heads),
        [
            (value, None)
            for value in (own, other, logits, router, middle, grad, gain, out, qkv)
        ]
        + [(a, block), (weights, None)],
        [
            (shape_of(length, width, dtype=F32), None),
            (shape_of(length, width), None),
            (shape_of(1, width, dtype=F32), None),
            (shape_of(3, length, lanes), None),
            (shape_of(heads, span, dtype=F32), None),
            (shape_of(length, half), None),
            (shape_of(length, half), None),
        ],
        grid=(length // BLOCK,),
        scratch=[
            pltpu.VMEM((256, width), F32),
            pltpu.VMEM((length, lanes), BF16),
            pltpu.VMEM((length, lanes), F32),
            pltpu.VMEM((length, lanes), F32),
            pltpu.VMEM((heads, BLOCK, span), F32),
            pltpu.VMEM((heads, BLOCK, length), F32),
            pltpu.VMEM((heads * BLOCK, length), BF16),
            pltpu.VMEM((heads * BLOCK, lanes), BF16),
            pltpu.VMEM((heads * BLOCK, lanes), BF16),
        ],
        vmem=58,
        flops=LONG,
    )


def head_grads_kernel(normed_ref, dp_ref, low_ref, own_ref, out_ref):
    lanes = dp_ref.shape[2]
    for v in range(3):
        part = dot(normed_ref[...], dp_ref[v], (0, 0))
        out_ref[:, v * lanes : (v + 1) * lanes] = part.astype(BF16)
    half = own_ref.shape[0]
    part = dot(low_ref[:half, :], own_ref[:, :lanes], (0, 0))
    part += dot(low_ref[half:, :], own_ref[:, lanes:], (0, 0))
    out_ref[:, 3 * lanes :] = part.astype(BF16)


def head_weight_grads(normed, dp, low, own):
    width = normed.shape[1]
    return call(
        head_grads_kernel,
        [(value, None) for value in (normed, dp, low, own)],
        [(shape_of(width, 4 * dp.shape[2]), None)],
        vmem=58,
    )[0]


def rows_back_kernel(own_ref, other_ref, x_ref, gain_ref, mid_ref, out_ref, gain_grad_ref, joined):
    rows, width = x_ref.shape
    half = width // 2
    core = which_core()

    @pl.when(pl.program_id(0) == 0)
    def _():
        gain_grad_ref[...] = jnp.zeros_like(gain_grad_ref)

    joined[:, half_at(core, half)] = own_ref[...].astype(F32)
    joined[:, half_at(1 - core, half)] = other_ref[...].astype(F32)
    grad = joined[...]
    values = x_ref[...].astype(F32)
    scale = row_scale(values)
    scaled = grad * gain_ref[...]
    mean = jnp.mean(scaled * values, -1, keepdims=True)
    change = scale * scaled - values * (scale * scale * scale) * mean
    out_ref[...] = (mid_ref[...] + change).astype(BF16)
    gain_grad_ref[...] += jnp.sum(grad * values * scale, 0, keepdims=True)


def rows_back(own, other, rows, gain, mid):
    length, width = rows.shape
    block = length // 4
    return call(
        rows_back_kernel,
        [
            (own, row_blocks(block, own.shape[1])),
            (other, row_blocks(block, own.shape[1])),
            (rows, row_blocks(block, width)),
            (gain, None),
            (mid, row_blocks(block, width)),
        ],
        [
            (shape_of(length, width), row_blocks(block, width)),
            (shape_of(1, width, dtype=F32), None),
        ],
        grid=(4,),
        scratch=[pltpu.VMEM((block, width), F32)],
    )


def to_own_quarter(pieces):
    x, _, c, _ = place()

    def to(x, h, c, t):
        return (x, h, c, t ^ (x + 2 * c)) if x + 2 * c else None

    def across(x, h, c, t):
        return (x, h, 1 - c, t ^ (x + 2 * (1 - c)))

    return jnp.where(x + 2 * c == 0, pieces, send(pieces, to)), send(pieces, across)


def query_weights(own, other):
    if lax.axis_size("dp") == 4:
        return [own, other, host_swap(own, 1), host_swap(other, 1)], (0, 1, 2, 3)
    _, _, c, _ = place()
    both = ordered(c, own[None], other[None], 0)
    return [rows_over_hosts(both[None], 0).reshape(-1, own.shape[1])], (None,)


def over_quarters(piece):
    half = piece.shape[0] // 2
    piece = jnp.concatenate([piece[:half], piece[half:]], 1)
    return jnp.stack([piece] + [tensor_swap(piece, j) for j in (1, 2, 3)])


def out_weights(four):
    _, _, c, _ = place()
    hosts = rows_over_hosts(four[:, None], 1)
    whole = ordered(c, hosts[:, :, None], core_swap(hosts)[:, :, None], 2)
    lanes = whole.shape[4] // 2
    halves = jnp.stack([whole[..., :lanes], whole[..., lanes:]], 3)
    return halves.reshape(4, -1, lanes)


def weights_out(i):
    def to(x, h, c, t):
        return (x, h, 1 - (t & 1), c + 2 * (i ^ (t >> 1) ^ c))

    return to


def weights_home(i):
    def to(x, h, c, t):
        return (x, h, t & 1, 2 * (i ^ (t >> 1) ^ (t & 1)) + 1 - c)

    return to


def pack(up, down):
    half = up.shape[0] // 2
    return jnp.concatenate([jnp.concatenate([up[:half], up[half:]], 1), down], 0)


def unpack_pair(packed):
    rows, half = packed.shape[0] // 2, packed.shape[1] // 2
    up = jnp.concatenate([packed[:rows, :half], packed[:rows, half:]], 0)
    return up, packed[rows:]


def expert_weights(packed):
    return [send(packed, weights_out(i)) for i in range(2)]


def for_own_layer(zero, one):
    x, _, _, _ = place()
    other = section_swap(jnp.where(x == 0, one, zero).astype(BF16))
    return jnp.where(x == 0, zero, one), other


def to_expert(buffers, experts):
    if len(buffers) == 1:
        pieces = buffers[0].reshape(experts, -1, buffers[0].shape[1])
        own = [expert_exchange(pieces).reshape(buffers[0].shape)]
    else:
        order = [len(buffers) - 1] + list(range(1, len(buffers) - 1))
        got = {j: expert_swap(buffers[j], j) for j in order}
        own = [buffers[0]] + [got[j] for j in range(1, len(buffers))]
    return own, [core_swap(part) for part in own]


def add(first, second):
    return first + second


def after(values, earlier):
    if not jax.tree.leaves(earlier):
        return values
    return lax.optimization_barrier((values, earlier))[0]


def from_expert(parts, slot_column, experts, at_upper=(), at_lower=(), at_combine=()):
    if len(parts) == 2:
        keep, give = parts
        chip = add(keep, core_swap(give))
        pieces = add(chip, section_swap(chip)).reshape(experts, -1, chip.shape[1])
        whole = expert_exchange(pieces).reshape(chip.shape)
        rows = combine((whole, jnp.zeros_like(whole)), (), slot_column)
        return rows, core_swap(rows)
    split = experts // 2
    chips = [add(keep, core_swap(give)) for keep, give in (parts[:2], parts[2:])]
    back = {}
    for first, chip in ((split, chips[0]), (0, chips[1])):
        other = section_swap(chip)
        other = after(other, at_upper if first else at_lower)
        count = chip.shape[0] // split
        for j in range(first + split - 1, first - 1, -1):
            piece = slice((j - first) * count, (j - first + 1) * count)
            if j == 0:
                local = (chip[piece], other[piece])
            else:
                back[j] = expert_swap(add(chip[piece], other[piece]), j)
    local = after(local, at_combine)
    rows = combine(local, [back[j] for j in range(1, experts)], slot_column)
    return rows, core_swap(rows)


def layer_forward(
    source, params, attention, packs, experts, slots, mix, at_own, at_middle, during
):
    gain_one, base, prefix, gain_two, router, chosen, slot, slot_column = params
    qkv_pieces, out_pieces = attention
    rows, normed, qkv, qkv_weights, own, weights = attend(
        source, mix, prefix, gain_one, qkv_pieces, base
    )
    own = after(own, at_own)
    other = section_swap(own)
    pieces = after((own, other, core_swap(own), core_swap(other)), at_middle)
    middle, normed_two, gate, buffers = middle_and_buffers(
        rows, pieces, out_pieces, gain_two, router, chosen, slot, experts, slots
    )
    arrived = to_expert(buffers, experts)
    gates = during(tuple(arrived[0]))
    active, slope, parts = expert_rows(*arrived, packs)
    produced = from_expert(parts, slot_column, experts, *gates)
    saved = (rows, normed, qkv, qkv_weights, own, weights, middle, normed_two, gate)
    return saved, (arrived, active, slope), produced


def layer_backward(
    layer, grad, forward, params, attention, packs, experts, slots, during, before_total
):
    gain_one, base, prefix, gain_two, router, chosen, slot, slot_column = params
    out_pieces = attention[1]
    saved, (arrived, active, slope), produced = forward
    rows, normed, qkv, qkv_weights, own, weights, middle, normed_two, gate = saved
    last = layer == 1
    got, buffers = grads_and_buffers(
        middle, gate, *produced, grad, normed_two, router, chosen, slot, experts, slots, last
    )
    grad_logits = got[-1]
    grad_arrived = to_expert(buffers, experts)
    at_lower = during(tuple(grad_arrived[0]))
    hidden, parts = expert_rows_back(*grad_arrived, slope, packs)
    expert_grads = expert_weight_grads(*arrived, *grad_arrived, active, hidden)
    first = send(expert_grads[0], weights_home(0))
    grad_normed_two = from_expert(
        parts, slot_column, experts, tuple(expert_grads), at_lower, first
    )
    second = send(after(expert_grads[1], grad_normed_two[0]), weights_home(1))
    grad_router = dot(normed_two, grad_logits, (0, 0))[:, :experts]
    mid, low, grad_gain_two, dp, diagonal, keep, give = after(
        attend_back(
            *grad_normed_two,
            grad_logits,
            router,
            middle,
            grad,
            gain_two,
            out_pieces,
            qkv,
            weights,
            qkv_weights,
        ),
        second,
    )
    chip = add(keep, core_swap(give))
    head_grads = head_weight_grads(normed, dp, low, own)
    heads, at_total = before_total(head_grads, got[0])
    total = add(chip, after(section_swap(chip), (head_grads, at_total)))
    grad_rows, grad_gain_one = rows_back(total, core_swap(total), rows, gain_one, mid)
    small = (grad_gain_one[0], grad_gain_two[0], grad_router, diagonal)
    return grad_rows, (first, second), heads, small, total


def over_rows(grads):
    _, h, _, _ = place()
    hosts = lax.axis_size("dp") // 2
    parts = grads.reshape(hosts, 2, -1, grads.shape[1])
    bit = hosts // 2
    while bit:
        pair = parts.reshape(2, bit, *parts.shape[1:])
        upper = (h & bit) != 0
        keep = jnp.where(upper, pair[1], pair[0])
        arrived = host_swap(jnp.where(upper, pair[0], pair[1]), bit)
        parts = add(keep, arrived)
        bit //= 2
    return arrived, lambda earlier: add(keep, after(arrived, earlier))[0]


def to_quarter(part):
    x, _, c, _ = place()

    def to(x, h, c, t):
        return (x, h, c, t ^ (x + 2 * c)) if x + 2 * c else None

    return jnp.where(x + 2 * c == 0, part, send(part, to))


def over_cores(part):
    _, _, c, _ = place()
    keep = jnp.where(c == 0, part[0], part[1]).astype(F32)
    give = jnp.where(c == 0, part[1], part[0])
    return keep + core_swap(give).astype(F32)


def over_groups(values):
    one, two, three = (tensor_swap(values, j) for j in (1, 2, 3))
    values = (values + one) + (two + three)
    bit = 1
    while bit < lax.axis_size("dp") // 2:
        values = values + host_swap(values, bit)
        bit *= 2
    return values


def pick(flag, first, second):
    return jax.tree.map(lambda a, b: jnp.where(flag == 0, a, b), first, second)


def per_device(
    block_input,
    cotangent,
    query_key_value_weights,
    attention_output_weights,
    bias_table,
    norm_first,
    norm_second,
    router_projection_weights,
    expert_up,
    expert_down,
    routes,
    prefix_lengths,
    relative_buckets,
):
    x, h, c, t = place()
    _, piece, width = block_input.shape
    length = routes.shape[2]
    buckets, head_count = bias_table.shape[1:]
    experts = router_projection_weights.shape[2]
    heads = head_count // 4
    capacity = (5 * length + 4 * experts - 1) // (4 * experts)

    rows = to_groups(block_input)
    pieces = jnp.concatenate(
        [query_key_value_weights[0, v] for v in range(3)] + [attention_output_weights[0].T], 1
    )
    early = section_swap(pieces)
    other = after(early, tuple(rows[:2]))
    pieces = pick(x, (pieces, other), (other, pieces))
    scale = 32
    packed = jnp.concatenate(
        [
            routes[0, :, :, 0].reshape(-1),
            prefix_lengths // scale,
            prefix_lengths % scale,
        ]
    ).astype(BF16)
    both = ordered(c, packed[None], core_swap(packed)[None], 0)
    lower = at(both, t >> 1)
    route = lax.dynamic_slice_in_dim(lower, (t & 1) * length, length, 0)
    numbers = lower[2 * length :].astype(F32).astype(jnp.int32)
    prefix = lax.dynamic_slice_in_dim(numbers[:2] * scale + numbers[2:], t & 1, 1, 0)
    packed = jnp.concatenate(
        [
            route,
            norm_first[0],
            norm_second[0],
            router_projection_weights[0].reshape(-1),
            bias_table[0].reshape(-1),
        ]
    )
    other = section_swap(packed)
    packed = pick(x, (packed, other), (other, packed))

    half = expert_up.shape[3] // 2
    up, down = expert_up[0, 0], expert_down[0, 0]
    lower = pack(up[:, :half], down[:half])
    upper = pack(up[:, half:], down[half:])
    keep = jnp.where(x == 0, lower, upper)
    other = section_swap(after(jnp.where(x == 0, upper, lower), early))
    packs = pick(x, (keep, other), (other, keep))

    bucket_onehot = (
        relative_buckets[:, None] == jnp.arange(buckets, dtype=jnp.int32)[None, :]
    ).astype(BF16)
    earlier = (
        jnp.arange(length, dtype=jnp.int32)[None, :] < jnp.arange(length, dtype=jnp.int32)[:, None]
    ).astype(BF16)
    expert_ids = jnp.arange(experts, dtype=jnp.int32)

    def unpack(vector):
        route = vector[:length].astype(F32).astype(jnp.int32)
        at_one = length
        gain_one = vector[at_one : at_one + width].astype(F32)
        at_two = at_one + width
        gain_two = vector[at_two : at_two + width].astype(F32)
        at_router = at_two + width
        router = vector[at_router : at_router + width * experts].reshape(width, experts)
        table = vector[at_router + width * experts :].reshape(buckets, head_count)
        own = lax.dynamic_slice_in_dim(table, ((x + 2 * c) ^ t) * heads, heads, 1)
        rel = lax.dot_general(
            own, bucket_onehot, (((0,), (1,)), ((), ())), preferred_element_type=F32
        )
        base = jnp.roll(jnp.pad(rel, ((0, 0), (0, 1))), -(BLOCK - 1), axis=1)
        chosen = route[:, None] == expert_ids[None, :]
        rank = jnp.dot(earlier, chosen.astype(BF16), preferred_element_type=F32)
        rank = jnp.sum(jnp.where(chosen, rank, 0.0), 1).astype(jnp.int32)
        slot = (route ^ (2 * h + (t & 1))) * capacity + rank
        pad = ((0, 0), (0, 128 - experts))
        return (
            gain_one[None],
            base,
            prefix,
            gain_two[None],
            jnp.pad(router, pad),
            jnp.pad(chosen.astype(F32), pad),
            slot[None],
            slot[:, None],
        )

    params = [unpack(vector) for vector in packed]
    lanes = 3 * heads * HEAD_DIM
    queries_zero = query_weights(*to_own_quarter(pieces[0][:, :lanes]))
    outs_zero = out_weights(over_quarters(pieces[0][:, lanes:]))
    packs_zero = expert_weights(packs[0])
    slots = experts * capacity
    rows = after(tuple(rows), packs[0])
    later = {}

    def during_zero(arrived):
        piece = after(pieces[1], arrived)
        own, other = to_own_quarter(piece[:, :lanes])
        four = over_quarters(piece[:, lanes:])
        hosts = query_weights(own, other)
        later["queries"] = hosts
        later["outs"] = out_weights(four)
        later["first"] = send(after(packs[1], (arrived, own, other)), weights_out(0))
        return (own, other, four), (tuple(hosts[0]), later["first"]), ()

    zero = layer_forward(
        rows,
        params[0],
        (queries_zero, outs_zero),
        packs_zero,
        experts,
        slots,
        False,
        packs_zero[0],
        (),
        during_zero,
    )
    second = send(after(packs[1], zero[2][0]), weights_out(1))
    packs_one = [later["first"], second]
    outs_one = later["outs"]
    def during_one(arrived):
        later["top"] = to_groups(after(cotangent, arrived))
        return (), (), tuple(later["top"][:2])

    one = layer_forward(
        (zero[0][6], zero[0][8], *zero[2]),
        params[1],
        (later["queries"], outs_one),
        packs_one,
        experts,
        slots,
        True,
        second,
        (),
        during_one,
    )
    top = whole_rows(later["top"])

    def before_total_one(heads, result):
        arrived, heads = over_rows(heads)
        outputs, finish = from_groups(jnp.where(x == 0, one[0][0], result))
        later["outputs"] = finish
        return heads(()), (arrived, outputs)

    grads_one = layer_backward(
        1,
        top,
        one,
        params[1],
        (None, outs_one),
        packs_one,
        experts,
        slots,
        lambda arrived: (),
        before_total_one,
    )

    def during_back_zero(arrived):
        later["heads"] = to_quarter(after(grads_one[2], arrived))
        return later["heads"]

    grads_zero = layer_backward(
        0,
        grads_one[0],
        zero,
        params[0],
        (None, outs_zero),
        packs_zero,
        experts,
        slots,
        during_back_zero,
        lambda heads, _: (over_rows(heads)[1], ()),
    )
    outputs = later["outputs"]()

    def summed(pair):
        return pair[0].astype(F32) + pair[1].astype(F32)

    expert_zero = summed(after(grads_zero[1], grads_zero[4]))
    own, other = for_own_layer(expert_zero, summed(grads_one[1]))
    expert_own, expert_other = unpack_pair(own), unpack_pair(other.astype(F32))
    heads_zero = over_cores(to_quarter(grads_zero[2](grads_zero[4])))
    own, other = for_own_layer(heads_zero, over_cores(later["heads"]))
    heads_grad = own + other.astype(F32)
    grad_rows = from_groups(jnp.where(x == 0, grads_zero[0], grads_one[0]))[1]()

    def flat(small):
        gain_one, gain_two, router, diagonal = small
        total = jnp.roll(diagonal, BLOCK - 1, axis=1)[:, : 2 * length - 1]
        table = lax.dot_general(
            bucket_onehot.astype(F32),
            total,
            (((0,), (1,)), ((), ())),
            precision=lax.Precision.HIGHEST,
        )
        whole = lax.dynamic_update_slice_in_dim(
            jnp.zeros((buckets, head_count), F32), table, ((x + 2 * c) ^ t) * heads, 1
        )
        return jnp.concatenate([gain_one, gain_two, router.reshape(-1), whole.reshape(-1)])

    everything = over_groups(jnp.stack([flat(grads_zero[3]), flat(grads_one[3])]))
    core = core_swap(everything)
    size = everything.shape[1] - buckets * head_count
    tables = everything[:, size:] + core[:, size:]
    tables = tables + section_swap(tables)
    shared = at(jnp.where(c == 0, everything, core), x)

    grad_up = ordered(x, expert_own[0], expert_other[0], 1)
    grad_down = ordered(x, expert_own[1], expert_other[1], 0)
    wide = heads * HEAD_DIM
    grad_in = jnp.stack([heads_grad[:, v * wide : (v + 1) * wide] for v in range(3)])
    grad_out = heads_grad[:, 3 * wide :].T

    return (
        outputs[None],
        grad_rows[None],
        grad_in[None],
        grad_out[None],
        at(tables, x).reshape(1, buckets, head_count),
        shared[:width][None],
        shared[width : 2 * width][None],
        shared[2 * width : size].reshape(1, width, experts),
        grad_up[None, None],
        grad_down[None, None],
    )


def solution(mesh):
    in_specs = (
        P("dp", "tensor", None),
        P("dp", "tensor", None),
        P("section", None, "dp", "tensor"),
        P("section", "tensor", "dp"),
        P("section", None, None),
        P("section", None),
        P("section", None),
        P("section", None, None),
        P("section", "dp", None, "tensor"),
        P("section", "dp", "tensor", None),
        P("section", "dp", None, None),
        P("dp"),
        P(),
    )
    out_specs = (
        P("section", "dp", "tensor", None),
        P("section", "dp", "tensor", None),
        P("section", None, "dp", "tensor"),
        P("section", "tensor", "dp"),
        P("section", None, None),
        P("section", None),
        P("section", None),
        P("section", None, None),
        P("section", "dp", None, "tensor"),
        P("section", "dp", "tensor", None),
    )
    return jax.shard_map(
        per_device, mesh=mesh, in_specs=in_specs, out_specs=out_specs, check_vma=False
    )
```

```python
import functools

import jax
import jax.numpy as jnp
from jax import lax
from jax.experimental import pallas as pl
from jax.experimental.pallas import tpu as pltpu
from jax.sharding import PartitionSpec as P

HEAD_DIM = 64
EPSILON = 1e-06
MASKED = -1000000000.0
AXES = ("section", "dp", "tensor")
BLOCK = 128
DIRECT = 8
LONG = 10**11
BF16 = jnp.bfloat16
F32 = jnp.float32


def send(value, to):
    sections, width, depth = (lax.axis_size(name) for name in AXES)

    def number(x, h, c, t):
        return (x * width + 2 * h + c) * depth + t

    pairs = []
    for x in range(sections):
        for d in range(width):
            for t in range(depth):
                target = to(x, d // 2, d % 2, t)
                if target is not None:
                    pairs.append((number(x, d // 2, d % 2, t), number(*target)))
    return lax.ppermute(value, AXES, pairs)


def core_swap(value):
    return send(value, lambda x, h, c, t: (x, h, 1 - c, t))


def section_swap(value):
    return send(value, lambda x, h, c, t: (1 - x, h, c, t))


def tensor_swap(value, j):
    return send(value, lambda x, h, c, t: (x, h, c, t ^ j))


def host_swap(value, j):
    return send(value, lambda x, h, c, t: (x, h ^ j, c, t))


def expert_swap(value, j):
    def to(x, h, c, t):
        e = (2 * h + (t & 1)) ^ j
        return (x, e >> 1, c, (t & 2) | (e & 1))

    return send(value, to)


def expert_exchange(values):
    count, bit = values.shape[0], 1
    while bit < count:
        parts = values.reshape(count // (2 * bit), 2, bit, *values.shape[1:])
        other = expert_swap(parts[:, 1], bit)
        values = jnp.stack([parts[:, 0], other], 1).reshape(values.shape)
        bit *= 2
    return values


def place():
    d = lax.axis_index("dp")
    return lax.axis_index("section"), d // 2, d % 2, lax.axis_index("tensor")


def ordered(flag, own, other, axis):
    first = jnp.where(flag == 0, own, other)
    second = jnp.where(flag == 0, other, own)
    return jnp.concatenate([first, second], axis)


def at(values, index):
    return lax.dynamic_index_in_dim(values, index, 0, keepdims=False)


def rows_over_hosts(value, axis):
    _, h, _, _ = place()
    bit = 1
    while bit < lax.axis_size("dp") // 2:
        other = host_swap(value, bit)
        value = ordered((h // bit) % 2, value, other, axis)
        bit *= 2
    return value


def to_groups(rows):
    _, _, _, t = place()
    got = []
    for i in range(2):

        def to(x, h, c, t, i=i):
            return (x, h, 1 - (t >> 1), 2 * c + (i ^ (t & 1)))

        got.append(send(at(rows, i ^ (t & 1)), to))
    return got + [core_swap(part) for part in got]


def piece_order():
    c, low = which_core(), lax.axis_index("tensor") & 1
    return [2 * (1 - c) + low, 2 * (1 - c) + (1 - low), 2 * c + low, 2 * c + (1 - low)]


def whole_rows(pieces):
    order = piece_order()
    return jnp.concatenate([at_place(pieces, order, place) for place in range(4)], 0)


def at_place(pieces, order, place):
    value = pieces[3]
    for piece, number in zip(pieces[:3], order[:3]):
        value = jnp.where(number == place, piece, value)
    return value


def from_groups(rows):
    _, _, c, t = place()
    length, width = rows.shape
    pieces = rows.reshape(4, length // 4, width)
    got = []
    for i in range(2):

        def to(x, h, c, t, i=i):
            return (x, h, t >> 1, 2 * (1 - c) + (i ^ (t & 1)))

        got.append(send(at(pieces, 2 * (1 - c) + (i ^ (t & 1))), to))

    def finish():
        low = t & 1
        first, second = jnp.where(low == 0, got[0], got[1]), jnp.where(low == 0, got[1], got[0])
        return jnp.stack([first, second])

    return tuple(got), finish


def head_lanes(width, head):
    lane = lax.broadcasted_iota(jnp.int32, (1, width), 1)
    return (lane // HEAD_DIM) == head


def dot(a, b, contract=(1, 0)):
    dims = (((contract[0],), (contract[1],)), ((), ()))
    return lax.dot_general(a, b, dims, preferred_element_type=F32)


def which_core():
    return lax.rem(lax.axis_index("dp"), 2)


def which_member():
    return lax.axis_index("section") + 2 * which_core()


def half_at(index, half):
    return pl.ds(pl.multiple_of(index * half, half), half)


def row_scale(values):
    return lax.rsqrt(jnp.mean(values * values, -1, keepdims=True) + EPSILON)


def call(kernel, inputs, outputs, grid=(1,), scratch=(), vmem=24, flops=10**9):
    def spec(item):
        value, given = item
        if given is not None:
            return given
        return pl.BlockSpec(value.shape, lambda i, n=len(value.shape): (0,) * n)

    return pl.pallas_call(
        kernel,
        grid=grid,
        in_specs=[spec(item) for item in inputs],
        out_specs=[spec(item) for item in outputs],
        out_shape=[item[0] for item in outputs],
        scratch_shapes=list(scratch),
        cost_estimate=pl.CostEstimate(flops=flops, bytes_accessed=1000, transcendentals=0),
        compiler_params=pltpu.CompilerParams(vmem_limit_bytes=vmem * 2**20),
    )(*[item[0] for item in inputs])


def shape_of(*dims, dtype=BF16):
    return jax.ShapeDtypeStruct(dims, dtype)


SMEM = pl.BlockSpec(memory_space=pltpu.SMEM)


def attend_kernel(heads, mix, orders, *refs):
    if mix:
        middle_ref, gate_ref, own_ref, other_ref, *refs = refs
    else:
        row_refs, refs = refs[:4], refs[4:]
    part_refs, refs = refs[: len(orders)], refs[len(orders) :]
    prefix_ref, gain_ref, base_ref, x_ref, normed_ref, qkv_ref, w_ref, *refs = refs
    o_ref, a_ref, strip, causal, scores_ref = refs
    block = pl.program_id(0)
    length, width = x_ref.shape
    rows = a_ref.shape[1]
    span = base_ref.shape[1]
    lanes_all = o_ref.shape[1] // 2

    @pl.when(block == 0)
    def _():
        step = 256
        for ref, order in zip(part_refs, orders):
            count = ref.shape[0]
            first = 0
            if order is not None:
                first = pl.multiple_of((lax.axis_index("dp") ^ order) * count, 8)
            for v in range(3):
                w_ref[v, pl.ds(first, count), :] = ref[:, v * lanes_all : (v + 1) * lanes_all]
        if not mix:
            for ref, piece in zip(row_refs, piece_order()):
                count = ref.shape[0]
                x_ref[pl.ds(pl.multiple_of(piece * count, count), count), :] = ref[...]
        for at_row in range(0, length, step):
            part = pl.ds(at_row, step)
            if mix:
                half = width // 2
                core = which_core()
                for ref, side in ((own_ref, core), (other_ref, 1 - core)):
                    lanes = half_at(side, half)
                    value = middle_ref[part, lanes] + gate_ref[part, :] * ref[part, :].astype(F32)
                    x_ref[part, lanes] = value.astype(BF16)
            values = x_ref[part, :].astype(F32)
            normed = (values * row_scale(values) * gain_ref[...]).astype(BF16)
            normed_ref[part, :] = normed
            for v in range(3):
                qkv_ref[v, part, :] = dot(normed, w_ref[v]).astype(BF16)
        sub = lax.broadcasted_iota(jnp.int32, (8, span), 0)
        for head in range(heads):
            part = jnp.broadcast_to(base_ref[head : head + 1, :], (8, span))
            for bit in (1, 2, 4):
                part = jnp.where((sub & bit) != 0, pltpu.roll(part, bit, 1), part)
            size = 8
            while size < rows:
                part = jnp.concatenate([part, pltpu.roll(part, size, 1)], 0)
                size *= 2
            strip[head] = part
            ahead = lax.broadcasted_iota(jnp.int32, (rows, span), 1) - lax.broadcasted_iota(
                jnp.int32, (rows, span), 0
            )
            causal[head] = jnp.where(ahead > length - rows, MASKED, part)

    start = pl.multiple_of((length // rows - 1 - block) * rows, rows)
    here = pl.ds(pl.multiple_of(block * rows, rows), rows)
    col = lax.broadcasted_iota(jnp.int32, (1, length), 1)
    inside = col < prefix_ref[0]
    queries, keys, values = qkv_ref[0, here, :], qkv_ref[1], qkv_ref[2]
    queries = queries * jnp.asarray(HEAD_DIM ** (-0.5), BF16)
    step = 32
    for head in range(heads):
        own = jnp.where(head_lanes(lanes_all, head), queries, jnp.zeros_like(queries))
        scores_ref[head] = dot(own, keys, (1, 1))
    out = jnp.zeros((rows, lanes_all), F32)
    for head in range(heads):
        for at_row in range(0, rows, step):
            part = pl.ds(at_row, step)
            across = pl.ds(start, length)
            bias = jnp.where(inside, strip[head, part, across], causal[head, part, across])
            scores = scores_ref[head, part, :] + bias
            weights = jnp.exp(scores - jnp.max(scores, -1, keepdims=True))
            weights = weights * (1.0 / jnp.sum(weights, -1, keepdims=True))
            a_ref[head, part, :] = weights.astype(BF16)
        out = jnp.where(head_lanes(lanes_all, head), dot(a_ref[head], values), out)
    blocks = length // rows
    place = pl.ds(pl.multiple_of(lax.rem(block, blocks // 2) * rows, rows), rows)

    @pl.when(block < blocks // 2)
    def _():
        o_ref[place, :lanes_all] = out.astype(BF16)

    @pl.when(block >= blocks // 2)
    def _():
        o_ref[place, lanes_all:] = out.astype(BF16)


def attend(source, mix, prefix, gain, weights, base):
    weights, orders = weights
    width = gain.shape[1]
    length = source[0].shape[0] * (1 if mix else 4)
    lanes = weights[0].shape[1] // 3
    heads = lanes // HEAD_DIM
    span = base.shape[1]
    inputs = [(part, None) for part in (*source, *weights)]
    inputs += [(prefix, SMEM), (gain, None), (base, None)]
    return call(
        functools.partial(attend_kernel, heads, mix, orders),
        inputs,
        [
            (shape_of(length, width), None),
            (shape_of(length, width), None),
            (shape_of(3, length, lanes), None),
            (shape_of(3, width, lanes), None),
            (shape_of(length // 2, 2 * lanes), None),
            (
                shape_of(heads, length, length),
                pl.BlockSpec((heads, BLOCK, length), lambda i: (0, i, 0)),
            ),
        ],
        grid=(length // BLOCK,),
        scratch=[
            pltpu.VMEM((heads, BLOCK, span), F32),
            pltpu.VMEM((heads, BLOCK, span), F32),
            pltpu.VMEM((heads, BLOCK, length), F32),
        ],
        vmem=58,
        flops=LONG,
    )


def pieces_of(experts):
    return experts if experts <= DIRECT else 1


def selection_block(slot_ref, first, count):
    ids = first + lax.broadcasted_iota(jnp.int32, (count, slot_ref.shape[1]), 0)
    return jnp.where(ids == slot_ref[...], 1.0, 0.0).astype(BF16)


def dispatch_blocks(step, steps, slot_ref, rows_ref, buffer_refs):
    half = rows_ref.shape[1] // 2
    total = sum(ref.shape[0] for ref in buffer_refs) if len(buffer_refs) > 1 else None
    lanes = half_at(which_core(), half)
    if total is None:

        @pl.when(step >= steps)
        def _():
            count = buffer_refs[0].shape[0]
            chosen = selection_block(slot_ref, (step - steps) * count, count)
            buffer_refs[0][...] = dot(chosen, rows_ref[:, lanes]).astype(BF16)

        return
    first = 0
    for index, ref in enumerate(buffer_refs):

        @pl.when(step == steps + index)
        def _(ref=ref, first=first):
            chosen = selection_block(slot_ref, first, ref.shape[0])
            ref[...] = dot(chosen, rows_ref[:, lanes]).astype(BF16)

        first += ref.shape[0]


def buffer_outputs(experts, rows, half, steps):
    count = pieces_of(experts)
    if count > 1:
        return [(shape_of(rows // count, half), None)] * count, steps + count
    blocks = 4
    spec = pl.BlockSpec((rows // blocks, half), lambda i: (jnp.maximum(i - steps, 0), 0))
    return [(shape_of(rows, half), spec)], steps + blocks


def router_probs(normed, router_ref, experts):
    logits = dot(normed, router_ref[...])
    real = lax.broadcasted_iota(jnp.int32, logits.shape, 1) < experts
    logits = jnp.where(real, logits, MASKED)
    weights = jnp.exp(logits - jnp.max(logits, -1, keepdims=True))
    weights = jnp.where(real, weights, 0.0)
    return weights / jnp.sum(weights, -1, keepdims=True)


def middle_kernel(experts, steps, *refs):
    x_ref, *refs = refs
    piece_refs, refs = refs[:4], refs[4:]
    w_ref, gain_ref, router_ref, chosen_ref, slot_ref, middle_ref, normed_ref, gate_ref = refs[:8]
    buffer_refs, kept = refs[8:-1], refs[-1]
    step = pl.program_id(0)
    rows = x_ref.shape[0]

    def mix(side):
        member = which_member()
        half = piece_refs[0].shape[1] // 2
        first = pl.multiple_of(lax.rem(step, steps // 2) * rows, rows)
        lanes = slice(side * half, (side + 1) * half)
        parts = [
            dot(ref[pl.ds(first, rows), lanes], w_ref[member ^ j], (1, 1))
            for j, ref in enumerate(piece_refs)
        ]
        values = x_ref[...].astype(F32) + ((parts[0] + parts[1]) + (parts[2] + parts[3]))
        middle_ref[...] = values
        normed = (values * row_scale(values) * gain_ref[...]).astype(BF16)
        normed_ref[...] = normed
        kept[pl.ds(pl.multiple_of(step * rows, rows), rows), :] = normed
        probs = router_probs(normed, router_ref, experts)
        gate_ref[...] = jnp.sum(probs * chosen_ref[...], -1, keepdims=True)

    @pl.when(step < steps // 2)
    def _():
        mix(0)

    @pl.when((step >= steps // 2) & (step < steps))
    def _():
        mix(1)

    dispatch_blocks(step, steps, slot_ref, kept, buffer_refs)


def middle_and_buffers(rows, pieces, weights, gain, router, chosen, slot, experts, slots):
    length, width = rows.shape
    steps = 4
    block = length // steps

    def by_rows(lanes):
        return pl.BlockSpec((block, lanes), lambda i: (jnp.minimum(i, steps - 1), 0))

    buffers, grid = buffer_outputs(experts, slots, width // 2, steps)
    got = call(
        functools.partial(middle_kernel, experts, steps),
        [(rows, by_rows(width))]
        + [(piece, None) for piece in pieces]
        + [
            (weights, None),
            (gain, None),
            (router, None),
            (chosen, by_rows(chosen.shape[1])),
            (slot, None),
        ],
        [
            (shape_of(length, width, dtype=F32), by_rows(width)),
            (shape_of(length, width), by_rows(width)),
            (shape_of(length, 1, dtype=F32), by_rows(1)),
        ]
        + buffers,
        grid=(grid,),
        scratch=[pltpu.VMEM((length, width), BF16)],
    )
    return got[0], got[1], got[2], got[3:]


def order_of(index, count):
    return (index + count // 2) % count


def parts_of(refs, index, count):
    return refs[:2] if index >= count // 2 or count == 1 else refs[2:]


def part_outputs(rows, half, count):
    if count == 1:
        return [(shape_of(rows, half), None)] * 2
    split = count // 2
    shape = shape_of(rows * split, half)
    upper = pl.BlockSpec((rows, half), lambda i: (jnp.minimum(i, split - 1), 0))
    lower = pl.BlockSpec((rows, half), lambda i: (jnp.maximum(i - split, 0), 0))
    return [(shape, upper)] * 2 + [(shape, lower)] * 2


def ordered_blocks(rows, lanes, count):
    return pl.BlockSpec((rows, lanes), lambda i: ((i + count // 2) % count, 0))


GELU = 0.7978845608028654


def expert_kernel(count, *refs):
    own_refs, other_refs, refs = refs[:count], refs[count : 2 * count], refs[2 * count :]
    *pack_refs, active_ref, slope_ref = refs[:4]
    part_refs = refs[4:]
    half = own_refs[0].shape[1]
    upper, lower = pl.ds(0, half), pl.ds(half, half)
    core = which_core()
    step = pl.program_id(0)
    for index in range(count):
        keep_ref, give_ref = parts_of(part_refs, index, count)

        @pl.when(step == order_of(index, count))
        def _(index=index, keep_ref=keep_ref, give_ref=give_ref):
            mine, others = half_at(core, half), half_at(1 - core, half)
            own, other = own_refs[index][...], other_refs[index][...]
            keep = give = None
            for i, ref in enumerate(pack_refs):
                hidden = dot(own, ref[upper, mine]) + dot(other, ref[upper, others])
                square = hidden * hidden
                inner = jnp.tanh(GELU * hidden * (1.0 + 0.044715 * square))
                active = (0.5 * hidden * (1.0 + inner)).astype(BF16)
                slope = 0.5 * (1.0 + inner) + 0.5 * hidden * (1.0 - inner * inner) * (
                    GELU * (1.0 + 3 * 0.044715 * square)
                )
                active_ref[:, pl.ds(i * half, half)] = active
                slope_ref[:, pl.ds(i * half, half)] = slope.astype(BF16)
                first, second = dot(active, ref[lower, mine]), dot(active, ref[lower, others])
                keep = first if keep is None else keep + first
                give = second if give is None else give + second
            keep_ref[...] = keep.astype(BF16)
            give_ref[...] = give.astype(BF16)


def row_blocks(rows, lanes):
    return pl.BlockSpec((rows, lanes), lambda i: (i, 0))


def expert_rows(own, other, packs):
    count = len(own)
    rows, half = own[0].shape
    hidden = packs[0].shape[1]
    wide = (shape_of(rows * count, hidden), ordered_blocks(rows, hidden, count))
    got = call(
        functools.partial(expert_kernel, count),
        [(part, None) for part in own + other + packs],
        [wide, wide] + part_outputs(rows, half, count),
        grid=(count,),
    )
    return got[0], got[1], got[2:]


def expert_back_kernel(count, *refs):
    own_refs, other_refs, refs = refs[:count], refs[count : 2 * count], refs[2 * count :]
    slope_ref, *pack_refs, hidden_ref = refs[:4]
    part_refs = refs[4:]
    half = own_refs[0].shape[1]
    upper, lower = pl.ds(0, half), pl.ds(half, half)
    core = which_core()
    step = pl.program_id(0)
    for index in range(count):
        keep_ref, give_ref = parts_of(part_refs, index, count)

        @pl.when(step == order_of(index, count))
        def _(index=index, keep_ref=keep_ref, give_ref=give_ref):
            mine, others = half_at(core, half), half_at(1 - core, half)
            own, other = own_refs[index][...], other_refs[index][...]
            keep = give = None
            for i, ref in enumerate(pack_refs):
                lanes = pl.ds(i * half, half)
                grad = dot(own, ref[lower, mine], (1, 1)) + dot(other, ref[lower, others], (1, 1))
                grad = (grad * slope_ref[:, lanes].astype(F32)).astype(BF16)
                hidden_ref[:, lanes] = grad
                first = dot(grad, ref[upper, mine], (1, 1))
                second = dot(grad, ref[upper, others], (1, 1))
                keep = first if keep is None else keep + first
                give = second if give is None else give + second
            keep_ref[...] = keep.astype(BF16)
            give_ref[...] = give.astype(BF16)


def expert_rows_back(own, other, slope, packs):
    count = len(own)
    rows, half = own[0].shape
    hidden = packs[0].shape[1]
    blocks = ordered_blocks(rows, hidden, count)
    got = call(
        functools.partial(expert_back_kernel, count),
        [(part, None) for part in own + other]
        + [(slope, blocks)]
        + [(part, None) for part in packs],
        [(shape_of(rows * count, hidden), blocks)] + part_outputs(rows, half, count),
        grid=(count,),
    )
    return got[0], got[1:]


def expert_grads_kernel(count, *refs):
    own_refs, other_refs, refs = refs[:count], refs[count : 2 * count], refs[2 * count :]
    own_grads, other_grads, refs = refs[:count], refs[count : 2 * count], refs[2 * count :]
    active_ref, hidden_ref, first_ref, second_ref, inputs, grads = refs
    rows, half = own_refs[0].shape
    core = which_core()
    for sources, gradients, side in (
        (own_refs, own_grads, core),
        (other_refs, other_grads, 1 - core),
    ):
        lanes = half_at(side, half)
        for index in range(count):
            part = pl.ds(index * rows, rows)
            inputs[part, :] = sources[index][...]
            grads[part, :] = gradients[index][...]
        for out, ref in enumerate((first_ref, second_ref)):
            own_half = pl.ds(out * half, half)
            up = dot(inputs[...], hidden_ref[:, own_half], (0, 0))
            ref[pl.ds(0, half), lanes] = up.astype(BF16)
            down = dot(active_ref[:, own_half], grads[...], (0, 0))
            ref[pl.ds(half, half), lanes] = down.astype(BF16)


def expert_weight_grads(own, other, own_grads, other_grads, active, hidden):
    count = len(own)
    rows, half = own[0].shape
    return call(
        functools.partial(expert_grads_kernel, count),
        [(part, None) for part in own + other + own_grads + other_grads]
        + [(active, None), (hidden, None)],
        [(shape_of(2 * half, 2 * half), None)] * 2,
        scratch=[pltpu.VMEM((rows * count, half), BF16)] * 2,
        vmem=58,
    )


def combine_kernel(count, *refs):
    refs, slot_ref, out_ref = refs[:-2], refs[-2], refs[-1]
    block = out_ref.shape[0]
    total = jnp.zeros(out_ref.shape, F32)
    first = 0
    for index in range(count):
        if index == 0:
            value = (refs[0][...].astype(F32) + refs[1][...].astype(F32)).astype(BF16)
        else:
            value = refs[index + 1][...]
        ids = first + lax.broadcasted_iota(jnp.int32, (block, value.shape[0]), 1)
        chosen = jnp.where(ids == slot_ref[...], 1.0, 0.0).astype(BF16)
        total += dot(chosen, value)
        first += value.shape[0]
    out_ref[...] = total.astype(BF16)


def combine(first, rest, slot_column):
    length = slot_column.shape[0]
    half = first[0].shape[1]
    block = length // 4
    return call(
        functools.partial(combine_kernel, 1 + len(rest)),
        [(part, None) for part in first]
        + [(part, None) for part in rest]
        + [(slot_column, row_blocks(block, 1))],
        [(shape_of(length, half), row_blocks(block, half))],
        grid=(4,),
    )[0]


def grad_kernel(experts, steps, last, *refs):
    middle_ref, gate_ref, own_ref, other_ref, grad_ref, normed_ref, router_ref = refs[:7]
    chosen_ref, slot_ref, refs = refs[7], refs[8], refs[9:]
    if last:
        result_ref, *refs = refs
    logits_ref, refs = refs[0], refs[1:]
    buffer_refs, kept, joined = refs[:-2], refs[-2], refs[-1]
    step = pl.program_id(0)
    rows, width = middle_ref.shape

    @pl.when(step < steps)
    def _():
        half = width // 2
        core = which_core()
        joined[:, half_at(core, half)] = own_ref[...].astype(F32)
        joined[:, half_at(1 - core, half)] = other_ref[...].astype(F32)
        produced = joined[...]
        gate = gate_ref[...]
        if last:
            result_ref[...] = (middle_ref[...] + gate * produced).astype(BF16)
        grad = grad_ref[...].astype(F32)
        kept[pl.ds(pl.multiple_of(step * rows, rows), rows), :] = (gate * grad).astype(BF16)
        grad_gate = jnp.sum(grad * produced, -1, keepdims=True)
        probs = router_probs(normed_ref[...], router_ref, experts)
        grad_probs = chosen_ref[...] * grad_gate
        inner = jnp.sum(probs * grad_probs, -1, keepdims=True)
        logits_ref[...] = (probs * (grad_probs - inner)).astype(BF16)

    dispatch_blocks(step, steps, slot_ref, kept, buffer_refs)


def grads_and_buffers(
    middle, gate, own, other, grad, normed, router, chosen, slot, experts, slots, last
):
    length, width = middle.shape
    steps = 4
    block = length // steps

    def by_rows(value):
        lanes = value.shape[1]
        return (value, pl.BlockSpec((block, lanes), lambda i: (jnp.minimum(i, steps - 1), 0)))

    buffers, grid = buffer_outputs(experts, slots, width // 2, steps)
    outputs = [by_rows(shape_of(length, width))] if last else []
    outputs += [by_rows(shape_of(length, chosen.shape[1]))]
    got = call(
        functools.partial(grad_kernel, experts, steps, last),
        [by_rows(value) for value in (middle, gate, own, other, grad, normed)]
        + [(router, None), by_rows(chosen), (slot, None)],
        outputs + buffers,
        grid=(grid,),
        scratch=[pltpu.VMEM((length, width), BF16), pltpu.VMEM((block, width), F32)],
    )
    return got[: len(outputs)], got[len(outputs) :]


def attend_back_kernel(heads, *refs):
    own_ref, other_ref, logits_ref, router_ref, middle_ref, grad_ref, gain_ref = refs[:7]
    out_ref, qkv_ref, a_ref, w_ref, refs = refs[7], refs[8], refs[9], refs[10], refs[11:]
    mid_ref, low_ref, gain_grad_ref, dp_ref, diag_ref, keep_ref, give_ref = refs[:7]
    joined, grads_ref, dk, dv, strip, da_ref, ds_ref, query_ref, wide_ref = refs[7:]
    block = pl.program_id(0)
    length, width = middle_ref.shape
    rows = a_ref.shape[1]
    lanes_all = qkv_ref.shape[2]
    span = strip.shape[2]
    half = width // 2
    scaling = HEAD_DIM ** (-0.5)

    @pl.when(block == 0)
    def _():
        core = which_core()
        member = which_member()
        gain = gain_ref[...]
        gain_grad = jnp.zeros((1, width), F32)
        step = joined.shape[0]
        for at_row in range(0, length, step):
            part = pl.ds(at_row, step)
            joined[:, half_at(core, half)] = own_ref[part, :].astype(F32)
            joined[:, half_at(1 - core, half)] = other_ref[part, :].astype(F32)
            grad_normed = joined[...] + dot(logits_ref[part, :], router_ref[...], (1, 1))
            middle = middle_ref[part, :]
            scale = row_scale(middle)
            scaled = grad_normed * gain
            mean = jnp.mean(scaled * middle, -1, keepdims=True)
            grad = grad_ref[part, :].astype(F32) + (
                scale * scaled - middle * (scale * scale * scale) * mean
            )
            gain_grad += jnp.sum(grad_normed * middle * scale, 0, keepdims=True)
            mid_ref[part, :] = grad
            low = grad.astype(BF16)
            low_ref[part, :] = low
            grads_ref[part, :] = dot(low, out_ref[member]).astype(BF16)
        gain_grad_ref[...] = gain_grad
        dk[...] = jnp.zeros_like(dk)
        dv[...] = jnp.zeros_like(dv)
        strip[...] = jnp.zeros_like(strip)

    start = pl.multiple_of((length // rows - 1 - block) * rows, rows)
    here = pl.ds(pl.multiple_of(block * rows, rows), rows)
    queries, keys, values = qkv_ref[0, here, :], qkv_ref[1], qkv_ref[2]
    grads = grads_ref[here, :]
    for head in range(heads):
        lanes = head_lanes(lanes_all, head)
        part = pl.ds(head * rows, rows)
        own_grad = jnp.where(lanes, grads, jnp.zeros_like(grads))
        wide_ref[part, :] = own_grad
        query_ref[part, :] = jnp.where(lanes, queries, jnp.zeros_like(queries))
        da_ref[head] = dot(own_grad, values, (1, 1))
    step = 32
    dq = jnp.zeros((rows, lanes_all), F32)
    for head in range(heads):
        for at_row in range(0, rows, step):
            part = pl.ds(at_row, step)
            weights = a_ref[head, part, :].astype(F32)
            da = da_ref[head, part, :]
            ds = weights * (da - jnp.sum(weights * da, -1, keepdims=True))
            ds = ds.astype(BF16)
            ds_ref[pl.ds(head * rows + at_row, step), :] = ds
            strip[head, part, pl.ds(start, length)] += ds.astype(F32)
        own = dot(ds_ref[pl.ds(head * rows, rows), :], keys)
        dq = jnp.where(head_lanes(lanes_all, head), own, dq)
    dk[...] += dot(query_ref[...], ds_ref[...], (0, 0))
    dv[...] += dot(wide_ref[...], a_ref[...].reshape(heads * rows, length), (0, 0))
    dp_ref[0, here, :] = (dq * scaling).astype(BF16)

    @pl.when(block == length // rows - 1)
    def _():
        dp_ref[1] = (dk[...].T * scaling).astype(BF16)
        dp_ref[2] = dv[...].T.astype(BF16)
        sub = lax.broadcasted_iota(jnp.int32, (8, span), 0)
        for head in range(heads):
            part = strip[head]
            size = rows // 2
            while size >= 8:
                part = part[:size] + pltpu.roll(part[size:], span - size, 1)
                size //= 2
            for bit in (4, 2, 1):
                part = jnp.where((sub & bit) != 0, pltpu.roll(part, span - bit, 1), part)
            diag_ref[head : head + 1, :] = jnp.sum(part, 0, keepdims=True)
        core = which_core()
        for side, ref in ((core, keep_ref), (1 - core, give_ref)):
            for at_row in range(0, length, 256):
                part = pl.ds(at_row, 256)
                total = jnp.zeros((256, half), F32)
                for v in range(3):
                    total += dot(dp_ref[v, part, :], w_ref[v, half_at(side, half), :], (1, 1))
                ref[part, :] = total.astype(BF16)


def attend_back(own, other, logits, router, middle, grad, gain, out, qkv, a, weights):
    length, width = middle.shape
    heads = a.shape[0]
    lanes = qkv.shape[2]
    half = width // 2
    span = 2 * length
    block = pl.BlockSpec((heads, BLOCK, length), lambda i: (0, i, 0))
    return call(
        functools.partial(attend_back_kernel, heads),
        [
            (value, None)
            for value in (own, other, logits, router, middle, grad, gain, out, qkv)
        ]
        + [(a, block), (weights, None)],
        [
            (shape_of(length, width, dtype=F32), None),
            (shape_of(length, width), None),
            (shape_of(1, width, dtype=F32), None),
            (shape_of(3, length, lanes), None),
            (shape_of(heads, span, dtype=F32), None),
            (shape_of(length, half), None),
            (shape_of(length, half), None),
        ],
        grid=(length // BLOCK,),
        scratch=[
            pltpu.VMEM((256, width), F32),
            pltpu.VMEM((length, lanes), BF16),
            pltpu.VMEM((lanes, length), F32),
            pltpu.VMEM((lanes, length), F32),
            pltpu.VMEM((heads, BLOCK, span), F32),
            pltpu.VMEM((heads, BLOCK, length), F32),
            pltpu.VMEM((heads * BLOCK, length), BF16),
            pltpu.VMEM((heads * BLOCK, lanes), BF16),
            pltpu.VMEM((heads * BLOCK, lanes), BF16),
        ],
        vmem=58,
        flops=LONG,
    )


def head_grads_kernel(normed_ref, dp_ref, low_ref, own_ref, out_ref):
    lanes = dp_ref.shape[2]
    for v in range(3):
        part = dot(normed_ref[...], dp_ref[v], (0, 0))
        out_ref[:, v * lanes : (v + 1) * lanes] = part.astype(BF16)
    half = own_ref.shape[0]
    part = dot(low_ref[:half, :], own_ref[:, :lanes], (0, 0))
    part += dot(low_ref[half:, :], own_ref[:, lanes:], (0, 0))
    out_ref[:, 3 * lanes :] = part.astype(BF16)


def head_weight_grads(normed, dp, low, own):
    width = normed.shape[1]
    return call(
        head_grads_kernel,
        [(value, None) for value in (normed, dp, low, own)],
        [(shape_of(width, 4 * dp.shape[2]), None)],
        vmem=58,
    )[0]


def rows_back_kernel(own_ref, other_ref, x_ref, gain_ref, mid_ref, out_ref, gain_grad_ref, joined):
    rows, width = x_ref.shape
    half = width // 2
    core = which_core()

    @pl.when(pl.program_id(0) == 0)
    def _():
        gain_grad_ref[...] = jnp.zeros_like(gain_grad_ref)

    joined[:, half_at(core, half)] = own_ref[...].astype(F32)
    joined[:, half_at(1 - core, half)] = other_ref[...].astype(F32)
    grad = joined[...]
    values = x_ref[...].astype(F32)
    scale = row_scale(values)
    scaled = grad * gain_ref[...]
    mean = jnp.mean(scaled * values, -1, keepdims=True)
    change = scale * scaled - values * (scale * scale * scale) * mean
    out_ref[...] = (mid_ref[...] + change).astype(BF16)
    gain_grad_ref[...] += jnp.sum(grad * values * scale, 0, keepdims=True)


def rows_back(own, other, rows, gain, mid):
    length, width = rows.shape
    block = length // 4
    return call(
        rows_back_kernel,
        [
            (own, row_blocks(block, own.shape[1])),
            (other, row_blocks(block, own.shape[1])),
            (rows, row_blocks(block, width)),
            (gain, None),
            (mid, row_blocks(block, width)),
        ],
        [
            (shape_of(length, width), row_blocks(block, width)),
            (shape_of(1, width, dtype=F32), None),
        ],
        grid=(4,),
        scratch=[pltpu.VMEM((block, width), F32)],
    )


def to_own_quarter(pieces):
    x, _, c, _ = place()

    def to(x, h, c, t):
        return (x, h, c, t ^ (x + 2 * c)) if x + 2 * c else None

    def across(x, h, c, t):
        return (x, h, 1 - c, t ^ (x + 2 * (1 - c)))

    return jnp.where(x + 2 * c == 0, pieces, send(pieces, to)), send(pieces, across)


def query_weights(own, other):
    if lax.axis_size("dp") == 4:
        return [own, other, host_swap(own, 1), host_swap(other, 1)], (0, 1, 2, 3)
    _, _, c, _ = place()
    both = ordered(c, own[None], other[None], 0)
    return [rows_over_hosts(both[None], 0).reshape(-1, own.shape[1])], (None,)


def over_quarters(piece):
    half = piece.shape[0] // 2
    piece = jnp.concatenate([piece[:half], piece[half:]], 1)
    return jnp.stack([piece] + [tensor_swap(piece, j) for j in (1, 2, 3)])


def out_weights(four):
    _, _, c, _ = place()
    hosts = rows_over_hosts(four[:, None], 1)
    whole = ordered(c, hosts[:, :, None], core_swap(hosts)[:, :, None], 2)
    lanes = whole.shape[4] // 2
    halves = jnp.stack([whole[..., :lanes], whole[..., lanes:]], 3)
    return halves.reshape(4, -1, lanes)


def weights_out(i):
    def to(x, h, c, t):
        return (x, h, 1 - (t & 1), c + 2 * (i ^ (t >> 1) ^ c))

    return to


def weights_home(i):
    def to(x, h, c, t):
        return (x, h, t & 1, 2 * (i ^ (t >> 1) ^ (t & 1)) + 1 - c)

    return to


def pack(up, down):
    half = up.shape[0] // 2
    return jnp.concatenate([jnp.concatenate([up[:half], up[half:]], 1), down], 0)


def unpack_pair(packed):
    rows, half = packed.shape[0] // 2, packed.shape[1] // 2
    up = jnp.concatenate([packed[:rows, :half], packed[:rows, half:]], 0)
    return up, packed[rows:]


def expert_weights(packed):
    return [send(packed, weights_out(i)) for i in range(2)]


def for_own_layer(zero, one):
    x, _, _, _ = place()
    other = section_swap(jnp.where(x == 0, one, zero).astype(BF16))
    return jnp.where(x == 0, zero, one), other


def to_expert(buffers, experts):
    if len(buffers) == 1:
        pieces = buffers[0].reshape(experts, -1, buffers[0].shape[1])
        own = [expert_exchange(pieces).reshape(buffers[0].shape)]
    else:
        order = [len(buffers) - 1] + list(range(1, len(buffers) - 1))
        got = {j: expert_swap(buffers[j], j) for j in order}
        own = [buffers[0]] + [got[j] for j in range(1, len(buffers))]
    return own, [core_swap(part) for part in own]


def add(first, second):
    return first + second


def after(values, earlier):
    if not jax.tree.leaves(earlier):
        return values
    return lax.optimization_barrier((values, earlier))[0]


def from_expert(parts, slot_column, experts, at_upper=(), at_lower=(), at_combine=()):
    if len(parts) == 2:
        keep, give = parts
        chip = add(keep, core_swap(give))
        pieces = add(chip, section_swap(chip)).reshape(experts, -1, chip.shape[1])
        whole = expert_exchange(pieces).reshape(chip.shape)
        rows = combine((whole, jnp.zeros_like(whole)), (), slot_column)
        return rows, core_swap(rows)
    split = experts // 2
    chips = [add(keep, core_swap(give)) for keep, give in (parts[:2], parts[2:])]
    back = {}
    for first, chip in ((split, chips[0]), (0, chips[1])):
        other = section_swap(chip)
        other = after(other, at_upper if first else at_lower)
        count = chip.shape[0] // split
        for j in range(first + split - 1, first - 1, -1):
            piece = slice((j - first) * count, (j - first + 1) * count)
            if j == 0:
                local = (chip[piece], other[piece])
            else:
                back[j] = expert_swap(add(chip[piece], other[piece]), j)
    local = after(local, at_combine)
    rows = combine(local, [back[j] for j in range(1, experts)], slot_column)
    return rows, core_swap(rows)


def layer_forward(
    source, params, attention, packs, experts, slots, mix, at_own, at_middle, during
):
    gain_one, base, prefix, gain_two, router, chosen, slot, slot_column = params
    qkv_pieces, out_pieces = attention
    rows, normed, qkv, qkv_weights, own, weights = attend(
        source, mix, prefix, gain_one, qkv_pieces, base
    )
    own = after(own, at_own)
    other = section_swap(own)
    pieces = after((own, other, core_swap(own), core_swap(other)), at_middle)
    middle, normed_two, gate, buffers = middle_and_buffers(
        rows, pieces, out_pieces, gain_two, router, chosen, slot, experts, slots
    )
    arrived = to_expert(buffers, experts)
    gates = during(tuple(arrived[0]))
    active, slope, parts = expert_rows(*arrived, packs)
    produced = from_expert(parts, slot_column, experts, *gates)
    saved = (rows, normed, qkv, qkv_weights, own, weights, middle, normed_two, gate)
    return saved, (arrived, active, slope), produced


def layer_backward(
    layer, grad, forward, params, attention, packs, experts, slots, during, before_total
):
    gain_one, base, prefix, gain_two, router, chosen, slot, slot_column = params
    out_pieces = attention[1]
    saved, (arrived, active, slope), produced = forward
    rows, normed, qkv, qkv_weights, own, weights, middle, normed_two, gate = saved
    last = layer == 1
    got, buffers = grads_and_buffers(
        middle, gate, *produced, grad, normed_two, router, chosen, slot, experts, slots, last
    )
    grad_logits = got[-1]
    grad_arrived = to_expert(buffers, experts)
    at_lower = during(tuple(grad_arrived[0]))
    hidden, parts = expert_rows_back(*grad_arrived, slope, packs)
    expert_grads = expert_weight_grads(*arrived, *grad_arrived, active, hidden)
    first = send(expert_grads[0], weights_home(0))
    grad_normed_two = from_expert(
        parts, slot_column, experts, tuple(expert_grads), at_lower
    )
    second = send(after(expert_grads[1], grad_normed_two[0]), weights_home(1))
    grad_router = dot(normed_two, grad_logits, (0, 0))[:, :experts]
    mid, low, grad_gain_two, dp, diagonal, keep, give = after(
        attend_back(
            *grad_normed_two,
            grad_logits,
            router,
            middle,
            grad,
            gain_two,
            out_pieces,
            qkv,
            weights,
            qkv_weights,
        ),
        second,
    )
    chip = add(keep, core_swap(give))
    head_grads = head_weight_grads(normed, dp, low, own)
    heads, at_total = before_total(head_grads, got[0])
    total = add(chip, after(section_swap(chip), (head_grads, at_total)))
    grad_rows, grad_gain_one = rows_back(total, core_swap(total), rows, gain_one, mid)
    small = (grad_gain_one[0], grad_gain_two[0], grad_router, diagonal)
    return grad_rows, (first, second), heads, small, total


def over_rows(grads):
    _, h, _, _ = place()
    hosts = lax.axis_size("dp") // 2
    parts = grads.reshape(hosts, 2, -1, grads.shape[1])
    bit = hosts // 2
    while bit:
        pair = parts.reshape(2, bit, *parts.shape[1:])
        upper = (h & bit) != 0
        keep = jnp.where(upper, pair[1], pair[0])
        arrived = host_swap(jnp.where(upper, pair[0], pair[1]), bit)
        parts = add(keep, arrived)
        bit //= 2
    return arrived, lambda earlier: add(keep, after(arrived, earlier))[0]


def to_quarter(part):
    x, _, c, _ = place()

    def to(x, h, c, t):
        return (x, h, c, t ^ (x + 2 * c)) if x + 2 * c else None

    return jnp.where(x + 2 * c == 0, part, send(part, to))


def over_cores(part):
    _, _, c, _ = place()
    keep = jnp.where(c == 0, part[0], part[1]).astype(F32)
    give = jnp.where(c == 0, part[1], part[0])
    return keep + core_swap(give).astype(F32)


def over_groups(values):
    one, two, three = (tensor_swap(values, j) for j in (1, 2, 3))
    values = (values + one) + (two + three)
    bit = 1
    while bit < lax.axis_size("dp") // 2:
        values = values + host_swap(values, bit)
        bit *= 2
    return values


def pick(flag, first, second):
    return jax.tree.map(lambda a, b: jnp.where(flag == 0, a, b), first, second)


def per_device(
    block_input,
    cotangent,
    query_key_value_weights,
    attention_output_weights,
    bias_table,
    norm_first,
    norm_second,
    router_projection_weights,
    expert_up,
    expert_down,
    routes,
    prefix_lengths,
    relative_buckets,
):
    x, h, c, t = place()
    _, piece, width = block_input.shape
    length = routes.shape[2]
    buckets, head_count = bias_table.shape[1:]
    experts = router_projection_weights.shape[2]
    heads = head_count // 4
    capacity = (5 * length + 4 * experts - 1) // (4 * experts)

    rows = to_groups(block_input)
    pieces = jnp.concatenate(
        [query_key_value_weights[0, v] for v in range(3)] + [attention_output_weights[0].T], 1
    )
    early = section_swap(pieces)
    other = after(early, tuple(rows[:2]))
    pieces = pick(x, (pieces, other), (other, pieces))
    scale = 32
    packed = jnp.concatenate(
        [
            routes[0, :, :, 0].reshape(-1),
            prefix_lengths // scale,
            prefix_lengths % scale,
        ]
    ).astype(BF16)
    both = ordered(c, packed[None], core_swap(packed)[None], 0)
    lower = at(both, t >> 1)
    route = lax.dynamic_slice_in_dim(lower, (t & 1) * length, length, 0)
    numbers = lower[2 * length :].astype(F32).astype(jnp.int32)
    prefix = lax.dynamic_slice_in_dim(numbers[:2] * scale + numbers[2:], t & 1, 1, 0)
    packed = jnp.concatenate(
        [
            route,
            norm_first[0],
            norm_second[0],
            router_projection_weights[0].reshape(-1),
            bias_table[0].reshape(-1),
        ]
    )
    other = section_swap(packed)
    packed = pick(x, (packed, other), (other, packed))

    half = expert_up.shape[3] // 2
    up, down = expert_up[0, 0], expert_down[0, 0]
    lower = pack(up[:, :half], down[:half])
    upper = pack(up[:, half:], down[half:])
    keep = jnp.where(x == 0, lower, upper)
    other = section_swap(after(jnp.where(x == 0, upper, lower), early))
    packs = pick(x, (keep, other), (other, keep))

    bucket_onehot = (
        relative_buckets[:, None] == jnp.arange(buckets, dtype=jnp.int32)[None, :]
    ).astype(BF16)
    earlier = (
        jnp.arange(length, dtype=jnp.int32)[None, :] < jnp.arange(length, dtype=jnp.int32)[:, None]
    ).astype(BF16)
    expert_ids = jnp.arange(experts, dtype=jnp.int32)

    def unpack(vector):
        route = vector[:length].astype(F32).astype(jnp.int32)
        at_one = length
        gain_one = vector[at_one : at_one + width].astype(F32)
        at_two = at_one + width
        gain_two = vector[at_two : at_two + width].astype(F32)
        at_router = at_two + width
        router = vector[at_router : at_router + width * experts].reshape(width, experts)
        table = vector[at_router + width * experts :].reshape(buckets, head_count)
        own = lax.dynamic_slice_in_dim(table, ((x + 2 * c) ^ t) * heads, heads, 1)
        rel = lax.dot_general(
            own, bucket_onehot, (((0,), (1,)), ((), ())), preferred_element_type=F32
        )
        base = jnp.roll(jnp.pad(rel, ((0, 0), (0, 1))), -(BLOCK - 1), axis=1)
        chosen = route[:, None] == expert_ids[None, :]
        rank = jnp.dot(earlier, chosen.astype(BF16), preferred_element_type=F32)
        rank = jnp.sum(jnp.where(chosen, rank, 0.0), 1).astype(jnp.int32)
        slot = (route ^ (2 * h + (t & 1))) * capacity + rank
        pad = ((0, 0), (0, 128 - experts))
        return (
            gain_one[None],
            base,
            prefix,
            gain_two[None],
            jnp.pad(router, pad),
            jnp.pad(chosen.astype(F32), pad),
            slot[None],
            slot[:, None],
        )

    params = [unpack(vector) for vector in packed]
    lanes = 3 * heads * HEAD_DIM
    queries_zero = query_weights(*to_own_quarter(pieces[0][:, :lanes]))
    outs_zero = out_weights(over_quarters(pieces[0][:, lanes:]))
    packs_zero = expert_weights(packs[0])
    slots = experts * capacity
    rows = after(tuple(rows), packs[0])
    later = {}

    def during_zero(arrived):
        piece = after(pieces[1], arrived)
        own, other = to_own_quarter(piece[:, :lanes])
        four = over_quarters(piece[:, lanes:])
        hosts = query_weights(own, other)
        later["queries"] = hosts
        later["outs"] = out_weights(four)
        later["first"] = send(after(packs[1], (arrived, own, other)), weights_out(0))
        return (own, other, four), (tuple(hosts[0]), later["first"]), ()

    zero = layer_forward(
        rows,
        params[0],
        (queries_zero, outs_zero),
        packs_zero,
        experts,
        slots,
        False,
        packs_zero[0],
        (),
        during_zero,
    )
    second = send(after(packs[1], zero[2][0]), weights_out(1))
    packs_one = [later["first"], second]
    outs_one = later["outs"]
    def during_one(arrived):
        later["top"] = to_groups(after(cotangent, arrived))
        return (), (), tuple(later["top"][:2])

    one = layer_forward(
        (zero[0][6], zero[0][8], *zero[2]),
        params[1],
        (later["queries"], outs_one),
        packs_one,
        experts,
        slots,
        True,
        second,
        (),
        during_one,
    )
    top = whole_rows(later["top"])

    def before_total_one(heads, result):
        arrived, heads = over_rows(heads)
        outputs, finish = from_groups(jnp.where(x == 0, one[0][0], result))
        later["outputs"] = finish
        return heads(()), (arrived, outputs)

    grads_one = layer_backward(
        1,
        top,
        one,
        params[1],
        (None, outs_one),
        packs_one,
        experts,
        slots,
        lambda arrived: (),
        before_total_one,
    )

    def during_back_zero(arrived):
        later["heads"] = to_quarter(after(grads_one[2], arrived))
        return later["heads"]

    grads_zero = layer_backward(
        0,
        grads_one[0],
        zero,
        params[0],
        (None, outs_zero),
        packs_zero,
        experts,
        slots,
        during_back_zero,
        lambda heads, _: (over_rows(heads)[1], ()),
    )
    outputs = later["outputs"]()

    def summed(pair):
        return pair[0].astype(F32) + pair[1].astype(F32)

    expert_zero = summed(after(grads_zero[1], grads_zero[4]))
    own, other = for_own_layer(expert_zero, summed(grads_one[1]))
    expert_own, expert_other = unpack_pair(own), unpack_pair(other.astype(F32))
    heads_zero = over_cores(to_quarter(grads_zero[2](grads_zero[4])))
    own, other = for_own_layer(heads_zero, over_cores(later["heads"]))
    heads_grad = own + other.astype(F32)
    grad_rows = from_groups(jnp.where(x == 0, grads_zero[0], grads_one[0]))[1]()

    def flat(small):
        gain_one, gain_two, router, diagonal = small
        total = jnp.roll(diagonal, BLOCK - 1, axis=1)[:, : 2 * length - 1]
        table = lax.dot_general(
            bucket_onehot.astype(F32),
            total,
            (((0,), (1,)), ((), ())),
            precision=lax.Precision.HIGHEST,
        )
        whole = lax.dynamic_update_slice_in_dim(
            jnp.zeros((buckets, head_count), F32), table, ((x + 2 * c) ^ t) * heads, 1
        )
        return jnp.concatenate([gain_one, gain_two, router.reshape(-1), whole.reshape(-1)])

    everything = over_groups(jnp.stack([flat(grads_zero[3]), flat(grads_one[3])]))
    core = core_swap(everything)
    size = everything.shape[1] - buckets * head_count
    tables = everything[:, size:] + core[:, size:]
    tables = tables + section_swap(tables)
    shared = at(jnp.where(c == 0, everything, core), x)

    grad_up = ordered(x, expert_own[0], expert_other[0], 1)
    grad_down = ordered(x, expert_own[1], expert_other[1], 0)
    wide = heads * HEAD_DIM
    grad_in = jnp.stack([heads_grad[:, v * wide : (v + 1) * wide] for v in range(3)])
    grad_out = heads_grad[:, 3 * wide :].T

    return (
        outputs[None],
        grad_rows[None],
        grad_in[None],
        grad_out[None],
        at(tables, x).reshape(1, buckets, head_count),
        shared[:width][None],
        shared[width : 2 * width][None],
        shared[2 * width : size].reshape(1, width, experts),
        grad_up[None, None],
        grad_down[None, None],
    )


def solution(mesh):
    in_specs = (
        P("dp", "tensor", None),
        P("dp", "tensor", None),
        P("section", None, "dp", "tensor"),
        P("section", "tensor", "dp"),
        P("section", None, None),
        P("section", None),
        P("section", None),
        P("section", None, None),
        P("section", "dp", None, "tensor"),
        P("section", "dp", "tensor", None),
        P("section", "dp", None, None),
        P("dp"),
        P(),
    )
    out_specs = (
        P("section", "dp", "tensor", None),
        P("section", "dp", "tensor", None),
        P("section", None, "dp", "tensor"),
        P("section", "tensor", "dp"),
        P("section", None, None),
        P("section", None),
        P("section", None),
        P("section", None, None),
        P("section", "dp", None, "tensor"),
        P("section", "dp", "tensor", None),
    )
    return jax.shard_map(
        per_device, mesh=mesh, in_specs=in_specs, out_specs=out_specs, check_vma=False
    )
```

```python
import functools

import jax
import jax.numpy as jnp
from jax import lax
from jax.experimental import pallas as pl
from jax.experimental.pallas import tpu as pltpu
from jax.sharding import PartitionSpec as P

HEAD_DIM = 64
EPSILON = 1e-06
MASKED = -1000000000.0
AXES = ("section", "dp", "tensor")
BLOCK = 256
DIRECT = 8
LONG = 10**11
BF16 = jnp.bfloat16
F32 = jnp.float32


def send(value, to):
    sections, width, depth = (lax.axis_size(name) for name in AXES)

    def number(x, h, c, t):
        return (x * width + 2 * h + c) * depth + t

    pairs = []
    for x in range(sections):
        for d in range(width):
            for t in range(depth):
                target = to(x, d // 2, d % 2, t)
                if target is not None:
                    pairs.append((number(x, d // 2, d % 2, t), number(*target)))
    return lax.ppermute(value, AXES, pairs)


def core_swap(value):
    return send(value, lambda x, h, c, t: (x, h, 1 - c, t))


def section_swap(value):
    return send(value, lambda x, h, c, t: (1 - x, h, c, t))


def tensor_swap(value, j):
    return send(value, lambda x, h, c, t: (x, h, c, t ^ j))


def host_swap(value, j):
    return send(value, lambda x, h, c, t: (x, h ^ j, c, t))


def expert_swap(value, j):
    def to(x, h, c, t):
        e = (2 * h + (t & 1)) ^ j
        return (x, e >> 1, c, (t & 2) | (e & 1))

    return send(value, to)


def expert_exchange(values):
    count, bit = values.shape[0], 1
    while bit < count:
        parts = values.reshape(count // (2 * bit), 2, bit, *values.shape[1:])
        other = expert_swap(parts[:, 1], bit)
        values = jnp.stack([parts[:, 0], other], 1).reshape(values.shape)
        bit *= 2
    return values


def place():
    d = lax.axis_index("dp")
    return lax.axis_index("section"), d // 2, d % 2, lax.axis_index("tensor")


def ordered(flag, own, other, axis):
    first = jnp.where(flag == 0, own, other)
    second = jnp.where(flag == 0, other, own)
    return jnp.concatenate([first, second], axis)


def at(values, index):
    return lax.dynamic_index_in_dim(values, index, 0, keepdims=False)


def rows_over_hosts(value, axis):
    _, h, _, _ = place()
    bit = 1
    while bit < lax.axis_size("dp") // 2:
        other = host_swap(value, bit)
        value = ordered((h // bit) % 2, value, other, axis)
        bit *= 2
    return value


def to_groups(rows):
    _, _, _, t = place()
    got = []
    for i in range(2):

        def to(x, h, c, t, i=i):
            return (x, h, 1 - (t >> 1), 2 * c + (i ^ (t & 1)))

        got.append(send(at(rows, i ^ (t & 1)), to))
    return got + [core_swap(part) for part in got]


def piece_order():
    c, low = which_core(), lax.axis_index("tensor") & 1
    return [2 * (1 - c) + low, 2 * (1 - c) + (1 - low), 2 * c + low, 2 * c + (1 - low)]


def whole_rows(pieces):
    order = piece_order()
    return jnp.concatenate([at_place(pieces, order, place) for place in range(4)], 0)


def at_place(pieces, order, place):
    value = pieces[3]
    for piece, number in zip(pieces[:3], order[:3]):
        value = jnp.where(number == place, piece, value)
    return value


def from_groups(rows):
    _, _, c, t = place()
    length, width = rows.shape
    pieces = rows.reshape(4, length // 4, width)
    got = []
    for i in range(2):

        def to(x, h, c, t, i=i):
            return (x, h, t >> 1, 2 * (1 - c) + (i ^ (t & 1)))

        got.append(send(at(pieces, 2 * (1 - c) + (i ^ (t & 1))), to))

    def finish():
        low = t & 1
        first, second = jnp.where(low == 0, got[0], got[1]), jnp.where(low == 0, got[1], got[0])
        return jnp.stack([first, second])

    return tuple(got), finish


def head_lanes(width, head):
    lane = lax.broadcasted_iota(jnp.int32, (1, width), 1)
    return (lane // HEAD_DIM) == head


def dot(a, b, contract=(1, 0)):
    dims = (((contract[0],), (contract[1],)), ((), ()))
    return lax.dot_general(a, b, dims, preferred_element_type=F32)


def which_core():
    return lax.rem(lax.axis_index("dp"), 2)


def which_member():
    return lax.axis_index("section") + 2 * which_core()


def half_at(index, half):
    return pl.ds(pl.multiple_of(index * half, half), half)


def row_scale(values):
    return lax.rsqrt(jnp.mean(values * values, -1, keepdims=True) + EPSILON)


def call(kernel, inputs, outputs, grid=(1,), scratch=(), vmem=24, flops=10**9):
    def spec(item):
        value, given = item
        if given is not None:
            return given
        return pl.BlockSpec(value.shape, lambda i, n=len(value.shape): (0,) * n)

    return pl.pallas_call(
        kernel,
        grid=grid,
        in_specs=[spec(item) for item in inputs],
        out_specs=[spec(item) for item in outputs],
        out_shape=[item[0] for item in outputs],
        scratch_shapes=list(scratch),
        cost_estimate=pl.CostEstimate(flops=flops, bytes_accessed=1000, transcendentals=0),
        compiler_params=pltpu.CompilerParams(vmem_limit_bytes=vmem * 2**20),
    )(*[item[0] for item in inputs])


def shape_of(*dims, dtype=BF16):
    return jax.ShapeDtypeStruct(dims, dtype)


SMEM = pl.BlockSpec(memory_space=pltpu.SMEM)


def attend_kernel(heads, mix, orders, *refs):
    if mix:
        middle_ref, gate_ref, own_ref, other_ref, *refs = refs
    else:
        row_refs, refs = refs[:4], refs[4:]
    part_refs, refs = refs[: len(orders)], refs[len(orders) :]
    prefix_ref, gain_ref, base_ref, x_ref, normed_ref, qkv_ref, w_ref, *refs = refs
    o_ref, a_ref, strip, causal, scores_ref = refs
    block = pl.program_id(0)
    length, width = x_ref.shape
    rows = a_ref.shape[1]
    span = base_ref.shape[1]
    lanes_all = o_ref.shape[1] // 2

    @pl.when(block == 0)
    def _():
        step = 256
        for ref, order in zip(part_refs, orders):
            count = ref.shape[0]
            first = 0
            if order is not None:
                first = pl.multiple_of((lax.axis_index("dp") ^ order) * count, 8)
            for v in range(3):
                w_ref[v, pl.ds(first, count), :] = ref[:, v * lanes_all : (v + 1) * lanes_all]
        if not mix:
            for ref, piece in zip(row_refs, piece_order()):
                count = ref.shape[0]
                x_ref[pl.ds(pl.multiple_of(piece * count, count), count), :] = ref[...]
        for at_row in range(0, length, step):
            part = pl.ds(at_row, step)
            if mix:
                half = width // 2
                core = which_core()
                for ref, side in ((own_ref, core), (other_ref, 1 - core)):
                    lanes = half_at(side, half)
                    value = middle_ref[part, lanes] + gate_ref[part, :] * ref[part, :].astype(F32)
                    x_ref[part, lanes] = value.astype(BF16)
            values = x_ref[part, :].astype(F32)
            normed = (values * row_scale(values) * gain_ref[...]).astype(BF16)
            normed_ref[part, :] = normed
            for v in range(3):
                qkv_ref[v, part, :] = dot(normed, w_ref[v]).astype(BF16)
        sub = lax.broadcasted_iota(jnp.int32, (8, span), 0)
        for head in range(heads):
            part = jnp.broadcast_to(base_ref[head : head + 1, :], (8, span))
            for bit in (1, 2, 4):
                part = jnp.where((sub & bit) != 0, pltpu.roll(part, bit, 1), part)
            size = 8
            while size < rows:
                part = jnp.concatenate([part, pltpu.roll(part, size, 1)], 0)
                size *= 2
            strip[head] = part
            ahead = lax.broadcasted_iota(jnp.int32, (rows, span), 1) - lax.broadcasted_iota(
                jnp.int32, (rows, span), 0
            )
            causal[head] = jnp.where(ahead > length - rows, MASKED, part)

    start = pl.multiple_of((length // rows - 1 - block) * rows, rows)
    here = pl.ds(pl.multiple_of(block * rows, rows), rows)
    col = lax.broadcasted_iota(jnp.int32, (1, length), 1)
    inside = col < prefix_ref[0]
    queries, keys, values = qkv_ref[0, here, :], qkv_ref[1], qkv_ref[2]
    queries = queries * jnp.asarray(HEAD_DIM ** (-0.5), BF16)
    step = 32
    for head in range(heads):
        own = jnp.where(head_lanes(lanes_all, head), queries, jnp.zeros_like(queries))
        scores_ref[head] = dot(own, keys, (1, 1))
    out = jnp.zeros((rows, lanes_all), F32)
    for head in range(heads):
        for at_row in range(0, rows, step):
            part = pl.ds(at_row, step)
            across = pl.ds(start, length)
            bias = jnp.where(inside, strip[head, part, across], causal[head, part, across])
            scores = scores_ref[head, part, :] + bias
            weights = jnp.exp(scores - jnp.max(scores, -1, keepdims=True))
            weights = weights * (1.0 / jnp.sum(weights, -1, keepdims=True))
            a_ref[head, part, :] = weights.astype(BF16)
        out = jnp.where(head_lanes(lanes_all, head), dot(a_ref[head], values), out)
    blocks = length // rows
    place = pl.ds(pl.multiple_of(lax.rem(block, blocks // 2) * rows, rows), rows)

    @pl.when(block < blocks // 2)
    def _():
        o_ref[place, :lanes_all] = out.astype(BF16)

    @pl.when(block >= blocks // 2)
    def _():
        o_ref[place, lanes_all:] = out.astype(BF16)


def attend(source, mix, prefix, gain, weights, base):
    weights, orders = weights
    width = gain.shape[1]
    length = source[0].shape[0] * (1 if mix else 4)
    lanes = weights[0].shape[1] // 3
    heads = lanes // HEAD_DIM
    span = base.shape[1]
    inputs = [(part, None) for part in (*source, *weights)]
    inputs += [(prefix, SMEM), (gain, None), (base, None)]
    return call(
        functools.partial(attend_kernel, heads, mix, orders),
        inputs,
        [
            (shape_of(length, width), None),
            (shape_of(length, width), None),
            (shape_of(3, length, lanes), None),
            (shape_of(3, width, lanes), None),
            (shape_of(length // 2, 2 * lanes), None),
            (
                shape_of(heads, length, length),
                pl.BlockSpec((heads, BLOCK, length), lambda i: (0, i, 0)),
            ),
        ],
        grid=(length // BLOCK,),
        scratch=[
            pltpu.VMEM((heads, BLOCK, span), F32),
            pltpu.VMEM((heads, BLOCK, span), F32),
            pltpu.VMEM((heads, BLOCK, length), F32),
        ],
        vmem=58,
        flops=LONG,
    )


def pieces_of(experts):
    return experts if experts <= DIRECT else 1


def selection_block(slot_ref, first, count):
    ids = first + lax.broadcasted_iota(jnp.int32, (count, slot_ref.shape[1]), 0)
    return jnp.where(ids == slot_ref[...], 1.0, 0.0).astype(BF16)


def dispatch_blocks(step, steps, slot_ref, rows_ref, buffer_refs):
    half = rows_ref.shape[1] // 2
    total = sum(ref.shape[0] for ref in buffer_refs) if len(buffer_refs) > 1 else None
    lanes = half_at(which_core(), half)
    if total is None:

        @pl.when(step >= steps)
        def _():
            count = buffer_refs[0].shape[0]
            chosen = selection_block(slot_ref, (step - steps) * count, count)
            buffer_refs[0][...] = dot(chosen, rows_ref[:, lanes]).astype(BF16)

        return
    first = 0
    for index, ref in enumerate(buffer_refs):

        @pl.when(step == steps + index)
        def _(ref=ref, first=first):
            chosen = selection_block(slot_ref, first, ref.shape[0])
            ref[...] = dot(chosen, rows_ref[:, lanes]).astype(BF16)

        first += ref.shape[0]


def buffer_outputs(experts, rows, half, steps):
    count = pieces_of(experts)
    if count > 1:
        return [(shape_of(rows // count, half), None)] * count, steps + count
    blocks = 4
    spec = pl.BlockSpec((rows // blocks, half), lambda i: (jnp.maximum(i - steps, 0), 0))
    return [(shape_of(rows, half), spec)], steps + blocks


def router_probs(normed, router_ref, experts):
    logits = dot(normed, router_ref[...])
    real = lax.broadcasted_iota(jnp.int32, logits.shape, 1) < experts
    logits = jnp.where(real, logits, MASKED)
    weights = jnp.exp(logits - jnp.max(logits, -1, keepdims=True))
    weights = jnp.where(real, weights, 0.0)
    return weights / jnp.sum(weights, -1, keepdims=True)


def middle_kernel(experts, steps, *refs):
    x_ref, *refs = refs
    piece_refs, refs = refs[:4], refs[4:]
    w_ref, gain_ref, router_ref, chosen_ref, slot_ref, middle_ref, normed_ref, gate_ref = refs[:8]
    buffer_refs, kept = refs[8:-1], refs[-1]
    step = pl.program_id(0)
    rows = x_ref.shape[0]

    def mix(side):
        member = which_member()
        half = piece_refs[0].shape[1] // 2
        first = pl.multiple_of(lax.rem(step, steps // 2) * rows, rows)
        lanes = slice(side * half, (side + 1) * half)
        parts = [
            dot(ref[pl.ds(first, rows), lanes], w_ref[member ^ j], (1, 1))
            for j, ref in enumerate(piece_refs)
        ]
        values = x_ref[...].astype(F32) + ((parts[0] + parts[1]) + (parts[2] + parts[3]))
        middle_ref[...] = values
        normed = (values * row_scale(values) * gain_ref[...]).astype(BF16)
        normed_ref[...] = normed
        kept[pl.ds(pl.multiple_of(step * rows, rows), rows), :] = normed
        probs = router_probs(normed, router_ref, experts)
        gate_ref[...] = jnp.sum(probs * chosen_ref[...], -1, keepdims=True)

    @pl.when(step < steps // 2)
    def _():
        mix(0)

    @pl.when((step >= steps // 2) & (step < steps))
    def _():
        mix(1)

    dispatch_blocks(step, steps, slot_ref, kept, buffer_refs)


def middle_and_buffers(rows, pieces, weights, gain, router, chosen, slot, experts, slots):
    length, width = rows.shape
    steps = 4
    block = length // steps

    def by_rows(lanes):
        return pl.BlockSpec((block, lanes), lambda i: (jnp.minimum(i, steps - 1), 0))

    buffers, grid = buffer_outputs(experts, slots, width // 2, steps)
    got = call(
        functools.partial(middle_kernel, experts, steps),
        [(rows, by_rows(width))]
        + [(piece, None) for piece in pieces]
        + [
            (weights, None),
            (gain, None),
            (router, None),
            (chosen, by_rows(chosen.shape[1])),
            (slot, None),
        ],
        [
            (shape_of(length, width, dtype=F32), by_rows(width)),
            (shape_of(length, width), by_rows(width)),
            (shape_of(length, 1, dtype=F32), by_rows(1)),
        ]
        + buffers,
        grid=(grid,),
        scratch=[pltpu.VMEM((length, width), BF16)],
    )
    return got[0], got[1], got[2], got[3:]


def order_of(index, count):
    return (index + count // 2) % count


def parts_of(refs, index, count):
    return refs[:2] if index >= count // 2 or count == 1 else refs[2:]


def part_outputs(rows, half, count):
    if count == 1:
        return [(shape_of(rows, half), None)] * 2
    split = count // 2
    shape = shape_of(rows * split, half)
    upper = pl.BlockSpec((rows, half), lambda i: (jnp.minimum(i, split - 1), 0))
    lower = pl.BlockSpec((rows, half), lambda i: (jnp.maximum(i - split, 0), 0))
    return [(shape, upper)] * 2 + [(shape, lower)] * 2


def ordered_blocks(rows, lanes, count):
    return pl.BlockSpec((rows, lanes), lambda i: ((i + count // 2) % count, 0))


GELU = 0.7978845608028654


def expert_kernel(count, *refs):
    own_refs, other_refs, refs = refs[:count], refs[count : 2 * count], refs[2 * count :]
    *pack_refs, active_ref, slope_ref = refs[:4]
    part_refs = refs[4:]
    half = own_refs[0].shape[1]
    upper, lower = pl.ds(0, half), pl.ds(half, half)
    core = which_core()
    step = pl.program_id(0)
    for index in range(count):
        keep_ref, give_ref = parts_of(part_refs, index, count)

        @pl.when(step == order_of(index, count))
        def _(index=index, keep_ref=keep_ref, give_ref=give_ref):
            mine, others = half_at(core, half), half_at(1 - core, half)
            own, other = own_refs[index][...], other_refs[index][...]
            keep = give = None
            for i, ref in enumerate(pack_refs):
                hidden = dot(own, ref[upper, mine]) + dot(other, ref[upper, others])
                square = hidden * hidden
                inner = jnp.tanh(GELU * hidden * (1.0 + 0.044715 * square))
                active = (0.5 * hidden * (1.0 + inner)).astype(BF16)
                slope = 0.5 * (1.0 + inner) + 0.5 * hidden * (1.0 - inner * inner) * (
                    GELU * (1.0 + 3 * 0.044715 * square)
                )
                active_ref[:, pl.ds(i * half, half)] = active
                slope_ref[:, pl.ds(i * half, half)] = slope.astype(BF16)
                first, second = dot(active, ref[lower, mine]), dot(active, ref[lower, others])
                keep = first if keep is None else keep + first
                give = second if give is None else give + second
            keep_ref[...] = keep.astype(BF16)
            give_ref[...] = give.astype(BF16)


def row_blocks(rows, lanes):
    return pl.BlockSpec((rows, lanes), lambda i: (i, 0))


def expert_rows(own, other, packs):
    count = len(own)
    rows, half = own[0].shape
    hidden = packs[0].shape[1]
    wide = (shape_of(rows * count, hidden), ordered_blocks(rows, hidden, count))
    got = call(
        functools.partial(expert_kernel, count),
        [(part, None) for part in own + other + packs],
        [wide, wide] + part_outputs(rows, half, count),
        grid=(count,),
    )
    return got[0], got[1], got[2:]


def expert_back_kernel(count, *refs):
    own_refs, other_refs, refs = refs[:count], refs[count : 2 * count], refs[2 * count :]
    slope_ref, *pack_refs, hidden_ref = refs[:4]
    part_refs = refs[4:]
    half = own_refs[0].shape[1]
    upper, lower = pl.ds(0, half), pl.ds(half, half)
    core = which_core()
    step = pl.program_id(0)
    for index in range(count):
        keep_ref, give_ref = parts_of(part_refs, index, count)

        @pl.when(step == order_of(index, count))
        def _(index=index, keep_ref=keep_ref, give_ref=give_ref):
            mine, others = half_at(core, half), half_at(1 - core, half)
            own, other = own_refs[index][...], other_refs[index][...]
            keep = give = None
            for i, ref in enumerate(pack_refs):
                lanes = pl.ds(i * half, half)
                grad = dot(own, ref[lower, mine], (1, 1)) + dot(other, ref[lower, others], (1, 1))
                grad = (grad * slope_ref[:, lanes].astype(F32)).astype(BF16)
                hidden_ref[:, lanes] = grad
                first = dot(grad, ref[upper, mine], (1, 1))
                second = dot(grad, ref[upper, others], (1, 1))
                keep = first if keep is None else keep + first
                give = second if give is None else give + second
            keep_ref[...] = keep.astype(BF16)
            give_ref[...] = give.astype(BF16)


def expert_rows_back(own, other, slope, packs):
    count = len(own)
    rows, half = own[0].shape
    hidden = packs[0].shape[1]
    blocks = ordered_blocks(rows, hidden, count)
    got = call(
        functools.partial(expert_back_kernel, count),
        [(part, None) for part in own + other]
        + [(slope, blocks)]
        + [(part, None) for part in packs],
        [(shape_of(rows * count, hidden), blocks)] + part_outputs(rows, half, count),
        grid=(count,),
    )
    return got[0], got[1:]


def expert_grads_kernel(count, *refs):
    own_refs, other_refs, refs = refs[:count], refs[count : 2 * count], refs[2 * count :]
    own_grads, other_grads, refs = refs[:count], refs[count : 2 * count], refs[2 * count :]
    active_ref, hidden_ref, first_ref, second_ref, inputs, grads = refs
    rows, half = own_refs[0].shape
    core = which_core()
    for sources, gradients, side in (
        (own_refs, own_grads, core),
        (other_refs, other_grads, 1 - core),
    ):
        lanes = half_at(side, half)
        for index in range(count):
            part = pl.ds(index * rows, rows)
            inputs[part, :] = sources[index][...]
            grads[part, :] = gradients[index][...]
        for out, ref in enumerate((first_ref, second_ref)):
            own_half = pl.ds(out * half, half)
            up = dot(inputs[...], hidden_ref[:, own_half], (0, 0))
            ref[pl.ds(0, half), lanes] = up.astype(BF16)
            down = dot(active_ref[:, own_half], grads[...], (0, 0))
            ref[pl.ds(half, half), lanes] = down.astype(BF16)


def expert_weight_grads(own, other, own_grads, other_grads, active, hidden):
    count = len(own)
    rows, half = own[0].shape
    return call(
        functools.partial(expert_grads_kernel, count),
        [(part, None) for part in own + other + own_grads + other_grads]
        + [(active, None), (hidden, None)],
        [(shape_of(2 * half, 2 * half), None)] * 2,
        scratch=[pltpu.VMEM((rows * count, half), BF16)] * 2,
        vmem=58,
    )


def expert_sums_kernel(zero_a, zero_b, one_a, one_b, other_ref, up_ref, down_ref):
    section = lax.axis_index("section")
    half = other_ref.shape[1]

    def lay(value, side):
        lanes = half_at(side, half)
        up_ref[:, lanes] = value[:half]
        down_ref[lanes, :] = value[half:]

    @pl.when(section == 0)
    def _():
        lay(zero_a[...].astype(F32) + zero_b[...].astype(F32), 0)

    @pl.when(section != 0)
    def _():
        lay(one_a[...].astype(F32) + one_b[...].astype(F32), 1)

    lay(other_ref[...].astype(F32), 1 - section)


def expert_sums(zero, one, other):
    rows, width = other.shape
    half = width // 2
    block = pl.BlockSpec((rows, half), lambda i: (0, i))
    return call(
        expert_sums_kernel,
        [(value, block) for value in (*zero, *one, other)],
        [
            (shape_of(rows, width, dtype=F32), pl.BlockSpec((half, width), lambda i: (i, 0))),
            (shape_of(rows, width, dtype=F32), block),
        ],
        grid=(2,),
    )


def combine_kernel(count, *refs):
    refs, slot_ref, out_ref = refs[:-2], refs[-2], refs[-1]
    block = out_ref.shape[0]
    total = jnp.zeros(out_ref.shape, F32)
    first = 0
    for index in range(count):
        if index == 0:
            value = (refs[0][...].astype(F32) + refs[1][...].astype(F32)).astype(BF16)
        else:
            value = refs[index + 1][...]
        ids = first + lax.broadcasted_iota(jnp.int32, (block, value.shape[0]), 1)
        chosen = jnp.where(ids == slot_ref[...], 1.0, 0.0).astype(BF16)
        total += dot(chosen, value)
        first += value.shape[0]
    out_ref[...] = total.astype(BF16)


def combine(first, rest, slot_column):
    length = slot_column.shape[0]
    half = first[0].shape[1]
    block = length // 4
    return call(
        functools.partial(combine_kernel, 1 + len(rest)),
        [(part, None) for part in first]
        + [(part, None) for part in rest]
        + [(slot_column, row_blocks(block, 1))],
        [(shape_of(length, half), row_blocks(block, half))],
        grid=(4,),
    )[0]


def grad_kernel(experts, steps, last, *refs):
    middle_ref, gate_ref, own_ref, other_ref, grad_ref, normed_ref, router_ref = refs[:7]
    chosen_ref, slot_ref, refs = refs[7], refs[8], refs[9:]
    if last:
        result_ref, *refs = refs
    logits_ref, refs = refs[0], refs[1:]
    buffer_refs, kept, joined = refs[:-2], refs[-2], refs[-1]
    step = pl.program_id(0)
    rows, width = middle_ref.shape

    @pl.when(step < steps)
    def _():
        half = width // 2
        core = which_core()
        joined[:, half_at(core, half)] = own_ref[...].astype(F32)
        joined[:, half_at(1 - core, half)] = other_ref[...].astype(F32)
        produced = joined[...]
        gate = gate_ref[...]
        if last:
            result_ref[...] = (middle_ref[...] + gate * produced).astype(BF16)
        grad = grad_ref[...].astype(F32)
        kept[pl.ds(pl.multiple_of(step * rows, rows), rows), :] = (gate * grad).astype(BF16)
        grad_gate = jnp.sum(grad * produced, -1, keepdims=True)
        probs = router_probs(normed_ref[...], router_ref, experts)
        grad_probs = chosen_ref[...] * grad_gate
        inner = jnp.sum(probs * grad_probs, -1, keepdims=True)
        logits_ref[...] = (probs * (grad_probs - inner)).astype(BF16)

    dispatch_blocks(step, steps, slot_ref, kept, buffer_refs)


def grads_and_buffers(
    middle, gate, own, other, grad, normed, router, chosen, slot, experts, slots, last
):
    length, width = middle.shape
    steps = 4
    block = length // steps

    def by_rows(value):
        lanes = value.shape[1]
        return (value, pl.BlockSpec((block, lanes), lambda i: (jnp.minimum(i, steps - 1), 0)))

    buffers, grid = buffer_outputs(experts, slots, width // 2, steps)
    outputs = [by_rows(shape_of(length, width))] if last else []
    outputs += [by_rows(shape_of(length, chosen.shape[1]))]
    got = call(
        functools.partial(grad_kernel, experts, steps, last),
        [by_rows(value) for value in (middle, gate, own, other, grad, normed)]
        + [(router, None), by_rows(chosen), (slot, None)],
        outputs + buffers,
        grid=(grid,),
        scratch=[pltpu.VMEM((length, width), BF16), pltpu.VMEM((block, width), F32)],
    )
    return got[: len(outputs)], got[len(outputs) :]


def attend_back_kernel(heads, *refs):
    own_ref, other_ref, logits_ref, router_ref, middle_ref, grad_ref, gain_ref = refs[:7]
    out_ref, qkv_ref, a_ref, w_ref, refs = refs[7], refs[8], refs[9], refs[10], refs[11:]
    mid_ref, low_ref, gain_grad_ref, dp_ref, diag_ref, keep_ref, give_ref = refs[:7]
    joined, grads_ref, dk, dv, strip, da_ref, ds_ref, query_ref, wide_ref = refs[7:]
    block = pl.program_id(0)
    length, width = middle_ref.shape
    rows = a_ref.shape[1]
    lanes_all = qkv_ref.shape[2]
    span = strip.shape[2]
    half = width // 2
    scaling = HEAD_DIM ** (-0.5)

    @pl.when(block == 0)
    def _():
        core = which_core()
        member = which_member()
        gain = gain_ref[...]
        gain_grad = jnp.zeros((1, width), F32)
        step = joined.shape[0]
        for at_row in range(0, length, step):
            part = pl.ds(at_row, step)
            joined[:, half_at(core, half)] = own_ref[part, :].astype(F32)
            joined[:, half_at(1 - core, half)] = other_ref[part, :].astype(F32)
            grad_normed = joined[...] + dot(logits_ref[part, :], router_ref[...], (1, 1))
            middle = middle_ref[part, :]
            scale = row_scale(middle)
            scaled = grad_normed * gain
            mean = jnp.mean(scaled * middle, -1, keepdims=True)
            grad = grad_ref[part, :].astype(F32) + (
                scale * scaled - middle * (scale * scale * scale) * mean
            )
            gain_grad += jnp.sum(grad_normed * middle * scale, 0, keepdims=True)
            mid_ref[part, :] = grad
            low = grad.astype(BF16)
            low_ref[part, :] = low
            grads_ref[part, :] = dot(low, out_ref[member]).astype(BF16)
        gain_grad_ref[...] = gain_grad
        dk[...] = jnp.zeros_like(dk)
        dv[...] = jnp.zeros_like(dv)
        strip[...] = jnp.zeros_like(strip)

    start = pl.multiple_of((length // rows - 1 - block) * rows, rows)
    here = pl.ds(pl.multiple_of(block * rows, rows), rows)
    queries, keys, values = qkv_ref[0, here, :], qkv_ref[1], qkv_ref[2]
    grads = grads_ref[here, :]
    for head in range(heads):
        lanes = head_lanes(lanes_all, head)
        part = pl.ds(head * rows, rows)
        own_grad = jnp.where(lanes, grads, jnp.zeros_like(grads))
        wide_ref[part, :] = own_grad
        query_ref[part, :] = jnp.where(lanes, queries, jnp.zeros_like(queries))
        da_ref[head] = dot(own_grad, values, (1, 1))
    step = 32
    dq = jnp.zeros((rows, lanes_all), F32)
    for head in range(heads):
        for at_row in range(0, rows, step):
            part = pl.ds(at_row, step)
            weights = a_ref[head, part, :].astype(F32)
            da = da_ref[head, part, :]
            ds = weights * (da - jnp.sum(weights * da, -1, keepdims=True))
            ds = ds.astype(BF16)
            ds_ref[pl.ds(head * rows + at_row, step), :] = ds
            strip[head, part, pl.ds(start, length)] += ds.astype(F32)
        own = dot(ds_ref[pl.ds(head * rows, rows), :], keys)
        dq = jnp.where(head_lanes(lanes_all, head), own, dq)
    dk[...] += dot(query_ref[...], ds_ref[...], (0, 0))
    dv[...] += dot(wide_ref[...], a_ref[...].reshape(heads * rows, length), (0, 0))
    dp_ref[0, here, :] = (dq * scaling).astype(BF16)

    @pl.when(block == length // rows - 1)
    def _():
        dp_ref[1] = (dk[...].T * scaling).astype(BF16)
        dp_ref[2] = dv[...].T.astype(BF16)
        sub = lax.broadcasted_iota(jnp.int32, (8, span), 0)
        for head in range(heads):
            part = strip[head]
            size = rows // 2
            while size >= 8:
                part = part[:size] + pltpu.roll(part[size:], span - size, 1)
                size //= 2
            for bit in (4, 2, 1):
                part = jnp.where((sub & bit) != 0, pltpu.roll(part, span - bit, 1), part)
            diag_ref[head : head + 1, :] = jnp.sum(part, 0, keepdims=True)
        core = which_core()
        for side, ref in ((core, keep_ref), (1 - core, give_ref)):
            for at_row in range(0, length, 256):
                part = pl.ds(at_row, 256)
                total = jnp.zeros((256, half), F32)
                for v in range(3):
                    total += dot(dp_ref[v, part, :], w_ref[v, half_at(side, half), :], (1, 1))
                ref[part, :] = total.astype(BF16)


def attend_back(own, other, logits, router, middle, grad, gain, out, qkv, a, weights):
    length, width = middle.shape
    heads = a.shape[0]
    lanes = qkv.shape[2]
    half = width // 2
    span = 2 * length
    block = pl.BlockSpec((heads, BLOCK, length), lambda i: (0, i, 0))
    return call(
        functools.partial(attend_back_kernel, heads),
        [
            (value, None)
            for value in (own, other, logits, router, middle, grad, gain, out, qkv)
        ]
        + [(a, block), (weights, None)],
        [
            (shape_of(length, width, dtype=F32), None),
            (shape_of(length, width), None),
            (shape_of(1, width, dtype=F32), None),
            (shape_of(3, length, lanes), None),
            (shape_of(heads, span, dtype=F32), None),
            (shape_of(length, half), None),
            (shape_of(length, half), None),
        ],
        grid=(length // BLOCK,),
        scratch=[
            pltpu.VMEM((256, width), F32),
            pltpu.VMEM((length, lanes), BF16),
            pltpu.VMEM((lanes, length), F32),
            pltpu.VMEM((lanes, length), F32),
            pltpu.VMEM((heads, BLOCK, span), F32),
            pltpu.VMEM((heads, BLOCK, length), F32),
            pltpu.VMEM((heads * BLOCK, length), BF16),
            pltpu.VMEM((heads * BLOCK, lanes), BF16),
            pltpu.VMEM((heads * BLOCK, lanes), BF16),
        ],
        vmem=58,
        flops=LONG,
    )


def head_grads_kernel(normed_ref, dp_ref, low_ref, own_ref, out_ref):
    lanes = dp_ref.shape[2]
    for v in range(3):
        part = dot(normed_ref[...], dp_ref[v], (0, 0))
        out_ref[:, v * lanes : (v + 1) * lanes] = part.astype(BF16)
    half = own_ref.shape[0]
    part = dot(low_ref[:half, :], own_ref[:, :lanes], (0, 0))
    part += dot(low_ref[half:, :], own_ref[:, lanes:], (0, 0))
    out_ref[:, 3 * lanes :] = part.astype(BF16)


def head_weight_grads(normed, dp, low, own):
    width = normed.shape[1]
    return call(
        head_grads_kernel,
        [(value, None) for value in (normed, dp, low, own)],
        [(shape_of(width, 4 * dp.shape[2]), None)],
        vmem=58,
    )[0]


def rows_back_kernel(own_ref, other_ref, x_ref, gain_ref, mid_ref, out_ref, gain_grad_ref, joined):
    rows, width = x_ref.shape
    half = width // 2
    core = which_core()

    @pl.when(pl.program_id(0) == 0)
    def _():
        gain_grad_ref[...] = jnp.zeros_like(gain_grad_ref)

    joined[:, half_at(core, half)] = own_ref[...].astype(F32)
    joined[:, half_at(1 - core, half)] = other_ref[...].astype(F32)
    grad = joined[...]
    values = x_ref[...].astype(F32)
    scale = row_scale(values)
    scaled = grad * gain_ref[...]
    mean = jnp.mean(scaled * values, -1, keepdims=True)
    change = scale * scaled - values * (scale * scale * scale) * mean
    out_ref[...] = (mid_ref[...] + change).astype(BF16)
    gain_grad_ref[...] += jnp.sum(grad * values * scale, 0, keepdims=True)


def rows_back(own, other, rows, gain, mid):
    length, width = rows.shape
    block = length // 4
    return call(
        rows_back_kernel,
        [
            (own, row_blocks(block, own.shape[1])),
            (other, row_blocks(block, own.shape[1])),
            (rows, row_blocks(block, width)),
            (gain, None),
            (mid, row_blocks(block, width)),
        ],
        [
            (shape_of(length, width), row_blocks(block, width)),
            (shape_of(1, width, dtype=F32), None),
        ],
        grid=(4,),
        scratch=[pltpu.VMEM((block, width), F32)],
    )


def to_own_quarter(pieces):
    x, _, c, _ = place()

    def to(x, h, c, t):
        return (x, h, c, t ^ (x + 2 * c)) if x + 2 * c else None

    def across(x, h, c, t):
        return (x, h, 1 - c, t ^ (x + 2 * (1 - c)))

    return jnp.where(x + 2 * c == 0, pieces, send(pieces, to)), send(pieces, across)


def query_weights(own, other):
    if lax.axis_size("dp") == 4:
        return [own, other, host_swap(own, 1), host_swap(other, 1)], (0, 1, 2, 3)
    _, _, c, _ = place()
    both = ordered(c, own[None], other[None], 0)
    return [rows_over_hosts(both[None], 0).reshape(-1, own.shape[1])], (None,)


def over_quarters(piece):
    half = piece.shape[0] // 2
    piece = jnp.concatenate([piece[:half], piece[half:]], 1)
    return jnp.stack([piece] + [tensor_swap(piece, j) for j in (1, 2, 3)])


def out_weights(four):
    _, _, c, _ = place()
    hosts = rows_over_hosts(four[:, None], 1)
    whole = ordered(c, hosts[:, :, None], core_swap(hosts)[:, :, None], 2)
    lanes = whole.shape[4] // 2
    halves = jnp.stack([whole[..., :lanes], whole[..., lanes:]], 3)
    return halves.reshape(4, -1, lanes)


def weights_out(i):
    def to(x, h, c, t):
        return (x, h, 1 - (t & 1), c + 2 * (i ^ (t >> 1) ^ c))

    return to


def weights_home(i):
    def to(x, h, c, t):
        return (x, h, t & 1, 2 * (i ^ (t >> 1) ^ (t & 1)) + 1 - c)

    return to


def pack(up, down):
    half = up.shape[0] // 2
    return jnp.concatenate([jnp.concatenate([up[:half], up[half:]], 1), down], 0)


def unpack_pair(packed):
    rows, half = packed.shape[0] // 2, packed.shape[1] // 2
    up = jnp.concatenate([packed[:rows, :half], packed[:rows, half:]], 0)
    return up, packed[rows:]


def expert_weights(packed):
    return [send(packed, weights_out(i)) for i in range(2)]


def for_own_layer(zero, one):
    x, _, _, _ = place()
    other = section_swap(jnp.where(x == 0, one, zero).astype(BF16))
    return jnp.where(x == 0, zero, one), other


def to_expert(buffers, experts):
    if len(buffers) == 1:
        pieces = buffers[0].reshape(experts, -1, buffers[0].shape[1])
        own = [expert_exchange(pieces).reshape(buffers[0].shape)]
    else:
        order = [len(buffers) - 1] + list(range(1, len(buffers) - 1))
        got = {j: expert_swap(buffers[j], j) for j in order}
        own = [buffers[0]] + [got[j] for j in range(1, len(buffers))]
    return own, [core_swap(part) for part in own]


def add(first, second):
    return first + second


def after(values, earlier):
    if not jax.tree.leaves(earlier):
        return values
    return lax.optimization_barrier((values, earlier))[0]


def from_expert(parts, slot_column, experts, at_upper=(), at_lower=(), at_combine=()):
    if len(parts) == 2:
        keep, give = parts
        chip = add(keep, core_swap(give))
        pieces = add(chip, section_swap(chip)).reshape(experts, -1, chip.shape[1])
        whole = expert_exchange(pieces).reshape(chip.shape)
        rows = combine((whole, jnp.zeros_like(whole)), (), slot_column)
        return rows, core_swap(rows)
    split = experts // 2
    chips = [add(keep, core_swap(give)) for keep, give in (parts[:2], parts[2:])]
    back = {}
    for first, chip in ((split, chips[0]), (0, chips[1])):
        other = section_swap(chip)
        other = after(other, at_upper if first else at_lower)
        count = chip.shape[0] // split
        for j in range(first + split - 1, first - 1, -1):
            piece = slice((j - first) * count, (j - first + 1) * count)
            if j == 0:
                local = (chip[piece], other[piece])
            else:
                back[j] = expert_swap(add(chip[piece], other[piece]), j)
    local = after(local, at_combine)
    rows = combine(local, [back[j] for j in range(1, experts)], slot_column)
    return rows, core_swap(rows)


def layer_forward(
    source, params, attention, packs, experts, slots, mix, at_own, at_middle, during
):
    gain_one, base, prefix, gain_two, router, chosen, slot, slot_column = params
    qkv_pieces, out_pieces = attention
    rows, normed, qkv, qkv_weights, own, weights = attend(
        source, mix, prefix, gain_one, qkv_pieces, base
    )
    own = after(own, at_own)
    other = section_swap(own)
    pieces = after((own, other, core_swap(own), core_swap(other)), at_middle)
    middle, normed_two, gate, buffers = middle_and_buffers(
        rows, pieces, out_pieces, gain_two, router, chosen, slot, experts, slots
    )
    arrived = to_expert(buffers, experts)
    gates = during(tuple(arrived[0]))
    active, slope, parts = expert_rows(*arrived, packs)
    produced = from_expert(parts, slot_column, experts, *gates)
    saved = (rows, normed, qkv, qkv_weights, own, weights, middle, normed_two, gate)
    return saved, (arrived, active, slope), produced


def layer_backward(
    layer, grad, forward, params, attention, packs, experts, slots, during, before_total
):
    gain_one, base, prefix, gain_two, router, chosen, slot, slot_column = params
    out_pieces = attention[1]
    saved, (arrived, active, slope), produced = forward
    rows, normed, qkv, qkv_weights, own, weights, middle, normed_two, gate = saved
    last = layer == 1
    got, buffers = grads_and_buffers(
        middle, gate, *produced, grad, normed_two, router, chosen, slot, experts, slots, last
    )
    grad_logits = got[-1]
    grad_arrived = to_expert(buffers, experts)
    at_lower = during(tuple(grad_arrived[0]))
    hidden, parts = expert_rows_back(*grad_arrived, slope, packs)
    expert_grads = expert_weight_grads(*arrived, *grad_arrived, active, hidden)
    first = send(expert_grads[0], weights_home(0))
    grad_normed_two = from_expert(
        parts, slot_column, experts, tuple(expert_grads), at_lower
    )
    second = send(after(expert_grads[1], grad_normed_two[0]), weights_home(1))
    grad_router = dot(normed_two, grad_logits, (0, 0))[:, :experts]
    mid, low, grad_gain_two, dp, diagonal, keep, give = after(
        attend_back(
            *grad_normed_two,
            grad_logits,
            router,
            middle,
            grad,
            gain_two,
            out_pieces,
            qkv,
            weights,
            qkv_weights,
        ),
        second,
    )
    chip = add(keep, core_swap(give))
    head_grads = head_weight_grads(normed, dp, low, own)
    heads, at_total = before_total(head_grads, got[0])
    total = add(chip, after(section_swap(chip), (head_grads, at_total)))
    grad_rows, grad_gain_one = rows_back(total, core_swap(total), rows, gain_one, mid)
    small = (grad_gain_one[0], grad_gain_two[0], grad_router, diagonal)
    return grad_rows, (first, second), heads, small, total


def over_rows(grads):
    _, h, _, _ = place()
    hosts = lax.axis_size("dp") // 2
    parts = grads.reshape(hosts, 2, -1, grads.shape[1])
    bit = hosts // 2
    while bit:
        pair = parts.reshape(2, bit, *parts.shape[1:])
        upper = (h & bit) != 0
        keep = jnp.where(upper, pair[1], pair[0])
        arrived = host_swap(jnp.where(upper, pair[0], pair[1]), bit)
        parts = add(keep, arrived)
        bit //= 2
    return arrived, lambda earlier: add(keep, after(arrived, earlier))[0]


def to_quarter(part):
    x, _, c, _ = place()

    def to(x, h, c, t):
        return (x, h, c, t ^ (x + 2 * c)) if x + 2 * c else None

    return jnp.where(x + 2 * c == 0, part, send(part, to))


def over_cores(part):
    _, _, c, _ = place()
    keep = jnp.where(c == 0, part[0], part[1]).astype(F32)
    give = jnp.where(c == 0, part[1], part[0])
    return keep + core_swap(give).astype(F32)


def over_groups(values):
    one, two, three = (tensor_swap(values, j) for j in (1, 2, 3))
    values = (values + one) + (two + three)
    bit = 1
    while bit < lax.axis_size("dp") // 2:
        values = values + host_swap(values, bit)
        bit *= 2
    return values


def pick(flag, first, second):
    return jax.tree.map(lambda a, b: jnp.where(flag == 0, a, b), first, second)


def per_device(
    block_input,
    cotangent,
    query_key_value_weights,
    attention_output_weights,
    bias_table,
    norm_first,
    norm_second,
    router_projection_weights,
    expert_up,
    expert_down,
    routes,
    prefix_lengths,
    relative_buckets,
):
    x, h, c, t = place()
    _, piece, width = block_input.shape
    length = routes.shape[2]
    buckets, head_count = bias_table.shape[1:]
    experts = router_projection_weights.shape[2]
    heads = head_count // 4
    capacity = (5 * length + 4 * experts - 1) // (4 * experts)

    rows = to_groups(block_input)
    pieces = jnp.concatenate(
        [query_key_value_weights[0, v] for v in range(3)] + [attention_output_weights[0].T], 1
    )
    early = section_swap(pieces)
    other = after(early, tuple(rows[:2]))
    pieces = pick(x, (pieces, other), (other, pieces))
    scale = 32
    packed = jnp.concatenate(
        [
            routes[0, :, :, 0].reshape(-1),
            prefix_lengths // scale,
            prefix_lengths % scale,
        ]
    ).astype(BF16)
    both = ordered(c, packed[None], core_swap(packed)[None], 0)
    lower = at(both, t >> 1)
    route = lax.dynamic_slice_in_dim(lower, (t & 1) * length, length, 0)
    numbers = lower[2 * length :].astype(F32).astype(jnp.int32)
    prefix = lax.dynamic_slice_in_dim(numbers[:2] * scale + numbers[2:], t & 1, 1, 0)
    packed = jnp.concatenate(
        [
            route,
            norm_first[0],
            norm_second[0],
            router_projection_weights[0].reshape(-1),
            bias_table[0].reshape(-1),
        ]
    )
    other = section_swap(packed)
    packed = pick(x, (packed, other), (other, packed))

    half = expert_up.shape[3] // 2
    up, down = expert_up[0, 0], expert_down[0, 0]
    lower = pack(up[:, :half], down[:half])
    upper = pack(up[:, half:], down[half:])
    keep = jnp.where(x == 0, lower, upper)
    other = section_swap(after(jnp.where(x == 0, upper, lower), early))
    packs = pick(x, (keep, other), (other, keep))

    bucket_onehot = (
        relative_buckets[:, None] == jnp.arange(buckets, dtype=jnp.int32)[None, :]
    ).astype(BF16)
    earlier = (
        jnp.arange(length, dtype=jnp.int32)[None, :] < jnp.arange(length, dtype=jnp.int32)[:, None]
    ).astype(BF16)
    expert_ids = jnp.arange(experts, dtype=jnp.int32)

    def unpack(vector):
        route = vector[:length].astype(F32).astype(jnp.int32)
        at_one = length
        gain_one = vector[at_one : at_one + width].astype(F32)
        at_two = at_one + width
        gain_two = vector[at_two : at_two + width].astype(F32)
        at_router = at_two + width
        router = vector[at_router : at_router + width * experts].reshape(width, experts)
        table = vector[at_router + width * experts :].reshape(buckets, head_count)
        own = lax.dynamic_slice_in_dim(table, ((x + 2 * c) ^ t) * heads, heads, 1)
        rel = lax.dot_general(
            own, bucket_onehot, (((0,), (1,)), ((), ())), preferred_element_type=F32
        )
        base = jnp.roll(jnp.pad(rel, ((0, 0), (0, 1))), -(BLOCK - 1), axis=1)
        chosen = route[:, None] == expert_ids[None, :]
        rank = jnp.dot(earlier, chosen.astype(BF16), preferred_element_type=F32)
        rank = jnp.sum(jnp.where(chosen, rank, 0.0), 1).astype(jnp.int32)
        slot = (route ^ (2 * h + (t & 1))) * capacity + rank
        pad = ((0, 0), (0, 128 - experts))
        return (
            gain_one[None],
            base,
            prefix,
            gain_two[None],
            jnp.pad(router, pad),
            jnp.pad(chosen.astype(F32), pad),
            slot[None],
            slot[:, None],
        )

    params = [unpack(vector) for vector in packed]
    lanes = 3 * heads * HEAD_DIM
    queries_zero = query_weights(*to_own_quarter(pieces[0][:, :lanes]))
    outs_zero = out_weights(over_quarters(pieces[0][:, lanes:]))
    packs_zero = expert_weights(packs[0])
    slots = experts * capacity
    rows = after(tuple(rows), packs[0])
    later = {}

    def during_zero(arrived):
        piece = after(pieces[1], arrived)
        own, other = to_own_quarter(piece[:, :lanes])
        four = over_quarters(piece[:, lanes:])
        hosts = query_weights(own, other)
        later["queries"] = hosts
        later["outs"] = out_weights(four)
        later["first"] = send(after(packs[1], (arrived, own, other)), weights_out(0))
        return (own, other, four), (tuple(hosts[0]), later["first"]), ()

    zero = layer_forward(
        rows,
        params[0],
        (queries_zero, outs_zero),
        packs_zero,
        experts,
        slots,
        False,
        packs_zero[0],
        (),
        during_zero,
    )
    second = send(after(packs[1], zero[2][0]), weights_out(1))
    packs_one = [later["first"], second]
    outs_one = later["outs"]
    def during_one(arrived):
        later["top"] = to_groups(after(cotangent, arrived))
        return (), (), tuple(later["top"][:2])

    one = layer_forward(
        (zero[0][6], zero[0][8], *zero[2]),
        params[1],
        (later["queries"], outs_one),
        packs_one,
        experts,
        slots,
        True,
        second,
        (),
        during_one,
    )
    top = whole_rows(later["top"])

    def before_total_one(heads, result):
        arrived, heads = over_rows(heads)
        outputs, finish = from_groups(jnp.where(x == 0, one[0][0], result))
        later["outputs"] = finish
        return heads(()), (arrived, outputs)

    grads_one = layer_backward(
        1,
        top,
        one,
        params[1],
        (None, outs_one),
        packs_one,
        experts,
        slots,
        lambda arrived: (),
        before_total_one,
    )

    def during_back_zero(arrived):
        later["heads"] = to_quarter(after(grads_one[2], arrived))
        return later["heads"]

    grads_zero = layer_backward(
        0,
        grads_one[0],
        zero,
        params[0],
        (None, outs_zero),
        packs_zero,
        experts,
        slots,
        during_back_zero,
        lambda heads, _: (over_rows(heads)[1], ()),
    )
    outputs = later["outputs"]()

    expert_zero = after(grads_zero[1], grads_zero[4])
    give = jnp.where(x == 0, add(*grads_one[1]), add(*expert_zero))
    grad_up, grad_down = expert_sums(expert_zero, grads_one[1], section_swap(give))
    heads_zero = over_cores(to_quarter(grads_zero[2](grads_zero[4])))
    own, other = for_own_layer(heads_zero, over_cores(later["heads"]))
    heads_grad = own + other.astype(F32)
    grad_rows = from_groups(jnp.where(x == 0, grads_zero[0], grads_one[0]))[1]()

    def flat(small):
        gain_one, gain_two, router, diagonal = small
        total = jnp.roll(diagonal, BLOCK - 1, axis=1)[:, : 2 * length - 1]
        table = lax.dot_general(
            bucket_onehot.astype(F32),
            total,
            (((0,), (1,)), ((), ())),
            precision=lax.Precision.HIGHEST,
        )
        whole = lax.dynamic_update_slice_in_dim(
            jnp.zeros((buckets, head_count), F32), table, ((x + 2 * c) ^ t) * heads, 1
        )
        return jnp.concatenate([gain_one, gain_two, router.reshape(-1), whole.reshape(-1)])

    everything = over_groups(jnp.stack([flat(grads_zero[3]), flat(grads_one[3])]))
    core = core_swap(everything)
    size = everything.shape[1] - buckets * head_count
    tables = everything[:, size:] + core[:, size:]
    tables = tables + section_swap(tables)
    shared = at(jnp.where(c == 0, everything, core), x)

    wide = heads * HEAD_DIM
    grad_in = jnp.stack([heads_grad[:, v * wide : (v + 1) * wide] for v in range(3)])
    grad_out = heads_grad[:, 3 * wide :].T

    return (
        outputs[None],
        grad_rows[None],
        grad_in[None],
        grad_out[None],
        at(tables, x).reshape(1, buckets, head_count),
        shared[:width][None],
        shared[width : 2 * width][None],
        shared[2 * width : size].reshape(1, width, experts),
        grad_up[None, None],
        grad_down[None, None],
    )


def solution(mesh):
    in_specs = (
        P("dp", "tensor", None),
        P("dp", "tensor", None),
        P("section", None, "dp", "tensor"),
        P("section", "tensor", "dp"),
        P("section", None, None),
        P("section", None),
        P("section", None),
        P("section", None, None),
        P("section", "dp", None, "tensor"),
        P("section", "dp", "tensor", None),
        P("section", "dp", None, None),
        P("dp"),
        P(),
    )
    out_specs = (
        P("section", "dp", "tensor", None),
        P("section", "dp", "tensor", None),
        P("section", None, "dp", "tensor"),
        P("section", "tensor", "dp"),
        P("section", None, None),
        P("section", None),
        P("section", None),
        P("section", None, None),
        P("section", "dp", None, "tensor"),
        P("section", "dp", "tensor", None),
    )
    return jax.shard_map(
        per_device, mesh=mesh, in_specs=in_specs, out_specs=out_specs, check_vma=False
    )
```
